512 devices in a mesh: dp: 64 (over x, z), seq: 8 (over y, core).
Axes of the slice: x: 4, y: 4, z: 16, core: 2. Of those that a mesh axis runs over, the one named last changes fastest.
Arguments:
- tokens: bfloat16 [131072, 1024], P(('dp', 'seq')), may hold values from -6 to 6
- teacher: float32 [131072], P(('dp', 'seq')), may hold values from -21 to 21
- cand_items: int32 [131072, 2], P(('dp', 'seq')), may hold values from 0 to 511, as said below
- owner_map: int32 [32768], P(('dp', 'seq')), may hold values from 0 to 63, as said below
- lengths: int32 [64], replicated, may hold values from 1 to 2048, 65536 in all
- w_proj: bfloat16 [1024, 2048], P('dp'), may hold values from -0.1875 to 0.1875
- w_out: bfloat16 [512, 1024], P('dp'), may hold values from -0.25 to 0.25
- gain_in: float32 [1024], replicated, may hold values from 0.5 to 1.5
- gain_mid: float32 [512], replicated, may hold values from 0.5 to 1.5
- item_table: bfloat16 [32768, 1024], P('dp'), may hold values from -0.1875 to 0.1875
Outputs:
- grad_tokens: bfloat16 [131072, 1024], P(('dp', 'seq'))
- loss: float32 [], replicated
The draws below stay inside these ranges and needn't reach their ends.
Inputs may be any that keep to these rules, and one draw needn't show every extreme that they name: `owner_map`: the 64 entries held by each device name every index of dp once. `cand_items`: A row's two candidates are different items.
All inputs are finite; a program needn't handle non-finite values.
Results may differ from the reference program's by a relative error of at most 0.023.
Values may be sent and summed in bfloat16 or wider, within the bound.
A program may use at most 128 MiB of HBM per device.

```python
import math
import jax
import jax.numpy as jnp
import numpy as np
from jax import lax

D = 1024
HEADS = 4
HD = 128
ITEMS_DEV = 512
HW = 512
LEN = 2048
TOKENS = 131072
CAP = 4
ITEMS = 32768
N_DP = 64
N_SEQ = 8


def draw_owner_map(key, part):
    key = jax.random.fold_in(key, 3)
    device_keys = jax.random.split(key, N_DP * N_SEQ)
    orders = jax.vmap(lambda single: jax.random.permutation(single, N_DP))(device_keys)
    return orders.reshape(-1).astype(jnp.int32)


def draw_cand_items(key, part):
    key = jax.random.fold_in(key, 5)
    first_key, second_key = jax.random.split(key)
    first = jax.random.randint(first_key, (TOKENS,), 0, ITEMS_DEV)
    offset = jax.random.randint(second_key, (TOKENS,), 1, ITEMS_DEV)
    second = (first + offset) % ITEMS_DEV
    return jnp.stack([first, second], axis=1).astype(jnp.int32)


def draw_teacher(key, part):
    key = jax.random.fold_in(key, 7)
    place = (jnp.arange(TOKENS) // LEN).astype(jnp.float32) / (N_DP - 1)
    base = jnp.clip(jax.random.normal(key, (TOKENS,), jnp.float32), -3.0, 3.0)
    factor = 1.0 + 3.0 * place
    return (1.5 * base * factor).astype(jnp.float32)


def shard_levels(rng, dims, cuts, smallest, high):
    def one(position, shards_of):
        draws = jax.random.uniform(jax.random.fold_in(jax.random.fold_in(rng, 6), position), (shards_of,), jnp.float32, smallest / len(cuts), high / len(cuts))
        return jnp.repeat(jnp.exp(draws), dims[position] // shards_of).reshape((-1,) + (1,) * (len(dims) - position - 1))

    factor_of = one(*cuts[0])
    for cut in cuts[1:]:
        factor_of = factor_of * one(*cut)
    return factor_of


def profile(count, total, most, lean):
    portions = [(1 << 20) // math.isqrt(standing ** lean) + 1 for standing in range(2, count + 1)]
    spare, given = total - most - (count - 1), [1] * (count - 1)
    while spare > 0:
        candidates = [i for i in range(count - 1) if given[i] < most]
        pool, left = sum([portions[i] for i in candidates]), spare
        for i in candidates:
            more = min(most - given[i], max(1, left * portions[i] // pool), spare)
            given[i] = given[i] + more
            spare = spare - more
    return np.array([most] + given)


def ragged_sizes(stream_key, number_of, total, most, lean):
    if number_of == 2:
        one = jax.random.randint(stream_key, (), max(1, total - most), min(most, total - 1) + 1)
        return jnp.stack([one, total - one])
    sizes = jnp.asarray(profile(number_of, total, most, lean), jnp.int32)
    couples = (number_of - 1) // 2
    giver, receiver = sizes[1:1 + 2 * couples:2], sizes[2:2 + 2 * couples:2]
    room = jnp.minimum(giver - 1, most - receiver)
    passed = jax.random.randint(jax.random.fold_in(stream_key, 1), (couples,), 0, 1 << 20) % (room + 1)
    sizes = sizes.at[1:1 + 2 * couples:2].set(giver - passed).at[2:2 + 2 * couples:2].set(receiver + passed)
    return sizes[jax.random.permutation(jax.random.fold_in(stream_key, 2), number_of)]


def noise(key, dims, deviation, reach, shards=(), dtype=jnp.bfloat16):
    array = deviation * jax.random.normal(key, dims, jnp.float32)
    if shards:
        array = array * shard_levels(key, dims, shards, -0.22, 0.18)
    return jnp.clip(array, -reach, reach).astype(dtype)


def setup_inputs(seed: int = 0) -> dict:
    arg_keys = jax.random.split(jax.random.key(seed), 11)
    tokens = noise(arg_keys[0], (TOKENS, D), 1.0, 6.0, ((0, 512),))
    teacher = draw_teacher(jax.random.fold_in(arg_keys[10], 71), 0)
    cand_items = draw_cand_items(jax.random.fold_in(arg_keys[10], 71), 0)
    owner_map = draw_owner_map(jax.random.fold_in(arg_keys[10], 71), 0)
    lengths = ragged_sizes(arg_keys[4], N_DP, N_DP * LEN // 2, LEN, 2).astype(jnp.int32)
    w_proj = noise(arg_keys[5], (D, 4 * HW), D ** -0.5, 0.1875, ((0, 64),))
    w_out = noise(arg_keys[6], (HW, D), HW ** -0.5, 0.25, ((0, 64),))
    gain_in = jnp.clip(1.0 + 0.1 * jax.random.normal(arg_keys[7], (D,), jnp.float32), 0.5, 1.5)
    gain_mid = jnp.clip(1.0 + 0.1 * jax.random.normal(arg_keys[8], (HW,), jnp.float32), 0.5, 1.5)
    item_table = noise(arg_keys[9], (ITEMS, D), D ** -0.5, 0.1875, ((0, 64),))
    return dict(tokens=tokens, teacher=teacher, cand_items=cand_items, owner_map=owner_map, lengths=lengths, w_proj=w_proj, w_out=w_out, gain_in=gain_in, gain_mid=gain_mid, item_table=item_table)


epsilon = 1e-05

def silu_slope(inputs):
    sigma = jax.nn.sigmoid(inputs)
    return sigma * (1.0 + inputs * (1.0 - sigma))

def normalize(inputs):
    centered = inputs - lax.optimization_barrier(jnp.mean(inputs, axis=-1, keepdims=True))
    factor = lax.rsqrt(lax.optimization_barrier(jnp.mean(centered * centered, axis=-1, keepdims=True)) + epsilon)
    return (centered * factor, factor)

def normalize_back(upstream, normed, factor):
    inner = lax.optimization_barrier(jnp.mean(upstream * normed, axis=-1, keepdims=True))
    return (upstream - lax.optimization_barrier(jnp.mean(upstream, axis=-1, keepdims=True)) - normed * inner) * factor

def reference(tokens, teacher, cand_items, owner_map, lengths, w_proj, w_out, gain_in, gain_mid, item_table):
    live_total = jnp.sum(lengths).astype(jnp.float32)
    scale_factor = HD ** (-0.5)
    owner_rows = jnp.repeat(owner_map, CAP).astype(jnp.int32)
    global_items = (owner_rows[:, None] * ITEMS_DEV + cand_items).astype(jnp.int32)
    positions = jnp.arange(LEN)

    def one_group(inputs):
        group_tokens, target, items, live_length = inputs
        normed_raw, factor_in = normalize(group_tokens.astype(jnp.float32))
        normed_in = (normed_raw * gain_in).astype(jnp.bfloat16)
        projected = jnp.dot(normed_in, w_proj, preferred_element_type=jnp.float32)
        activated = jax.nn.silu(projected).astype(jnp.bfloat16)
        gate_rows, value_rows, query_rows, key_rows = jnp.split(activated, 4, axis=1)
        query_heads = query_rows.astype(jnp.float32).reshape(LEN, HEADS, HD)
        key_heads = key_rows.astype(jnp.float32).reshape(LEN, HEADS, HD)
        value_heads = value_rows.astype(jnp.float32).reshape(LEN, HEADS, HD)
        mask = ((positions[None, :] <= positions[:, None]) & (positions[None, :] < live_length)).astype(jnp.float32)
        scores = jnp.einsum('qhd,khd->hqk', query_heads, key_heads) * scale_factor
        weights = (jax.nn.silu(scores) * (mask / LEN)).astype(jnp.bfloat16)
        weight_values = lax.optimization_barrier(weights).astype(jnp.float32)
        attended = jnp.einsum('hqk,khd->qhd', weight_values, value_heads).reshape(LEN, HW)
        normed_mid, factor_mid = normalize(attended)
        gated = (normed_mid * gain_mid * gate_rows.astype(jnp.float32)).astype(jnp.bfloat16)
        layer_out = (group_tokens.astype(jnp.float32) + jnp.dot(gated, w_out, preferred_element_type=jnp.float32)).astype(jnp.bfloat16)
        item_diff = item_table[items[:, 0]].astype(jnp.float32) - item_table[items[:, 1]].astype(jnp.float32)
        alive_rows = (positions < live_length).astype(jnp.float32)
        errors = (lax.optimization_barrier(jnp.sum(layer_out.astype(jnp.float32) * item_diff, axis=1)) - target) * alive_rows
        grad_out = (2.0 / live_total * errors[:, None] * item_diff).astype(jnp.bfloat16)
        grad_gated = jnp.dot(grad_out, w_out.T, preferred_element_type=jnp.float32)
        grad_gate = grad_gated * normed_mid * gain_mid
        grad_normed = grad_gated * gain_mid * gate_rows.astype(jnp.float32)
        grad_attended = normalize_back(grad_normed, normed_mid, factor_mid).astype(jnp.bfloat16)
        grad_heads = lax.optimization_barrier(grad_attended).astype(jnp.float32).reshape(LEN, HEADS, HD)
        grad_weights = jnp.einsum('qhd,khd->hqk', grad_heads, value_heads)
        grad_scores = (grad_weights * silu_slope(scores) * (mask * (scale_factor / LEN))).astype(jnp.bfloat16)
        score_values = lax.optimization_barrier(grad_scores).astype(jnp.float32)
        grad_query = jnp.einsum('hqk,khd->qhd', score_values, key_heads).reshape(LEN, HW)
        grad_key = jnp.einsum('hqk,qhd->khd', score_values, query_heads).reshape(LEN, HW)
        grad_value = jnp.einsum('hqk,qhd->khd', weight_values, grad_heads).reshape(LEN, HW)
        grad_proj = jnp.concatenate([grad_gate, grad_value, grad_query, grad_key], axis=1)
        grad_pre = (grad_proj * silu_slope(projected)).astype(jnp.bfloat16)
        grad_in = jnp.dot(grad_pre, w_proj.T, preferred_element_type=jnp.float32)
        grad_tokens = grad_out.astype(jnp.float32) + normalize_back(grad_in * gain_in, normed_raw, factor_in)
        return (grad_tokens.astype(jnp.bfloat16), jnp.sum(errors * errors))
    grads, terms = lax.map(one_group, (tokens.reshape(N_DP, LEN, D), teacher.reshape(N_DP, LEN), global_items.reshape(N_DP, LEN, 2), lengths))
    return (grads.reshape(TOKENS, D), jnp.sum(terms) / live_total)
```

```python
import functools

import jax
import jax.numpy as jnp
from jax import lax
from jax.experimental import pallas as pl
from jax.experimental.pallas import tpu as pltpu
from jax.sharding import PartitionSpec as P

MESH = pl.DeviceIdType.MESH
F32 = jnp.float32
BF16 = jnp.bfloat16
HEADS = 4
NZ = 16
CORES = 2
TILE = 16
EPSILON = 1e-05


def dot(a, b):
    return jnp.dot(a, b, preferred_element_type=F32)


def dot_nt(a, b):
    return lax.dot_general(a, b, (((1,), (1,)), ((), ())), preferred_element_type=F32)


def iota(shape, axis):
    return lax.broadcasted_iota(jnp.int32, shape, axis)


def one_hot(condition):
    return jnp.where(condition, 1.0, 0.0).astype(BF16)


def silu_slope(inputs):
    sigma = jax.nn.sigmoid(inputs)
    return sigma * (1.0 + inputs * (1.0 - sigma))


def normalize(inputs):
    centered = inputs - jnp.mean(inputs, axis=-1, keepdims=True)
    factor = lax.rsqrt(jnp.mean(centered * centered, axis=-1, keepdims=True) + EPSILON)
    return (centered * factor, factor)


def normalize_back(upstream, normed, factor):
    inner = jnp.mean(upstream * normed, axis=-1, keepdims=True)
    return (upstream - jnp.mean(upstream, axis=-1, keepdims=True) - normed * inner) * factor


def small_parts(values):
    whole = values.astype(jnp.int32)
    return (whole >> 4).astype(F32).astype(BF16), (whole & 15).astype(F32).astype(BF16)


def pair(t, u, parity):
    return t * (t + 1) + 2 * u + parity


def kernel(
    tok_ref, teach_ref, cand_ref, own_ref, len_ref, wp_ref, wo_ref, gin_ref, gmid_ref, table_hbm,
    out_ref, loss_ref,
    wall, xn, table, req_send, req_recv, rq, dsend, drecv, idiff, proj, kv, kt, vt, qs, qt, wst, slope,
    att_send, att_recv, gproj, wout, gout, gpg, da_send, da_recv, dat, dvk_send, dvk_recv, dqt,
    gps, gpr, lb0, lb1, lb2,
    lsem, xs, xr, zs, zr, rs, rr, ts, tr, req_s, req_r, dif_s, dif_r,
    ws, wr, wrs, wrr, vs, vr, vrs, vrr, ks, kr, as_, ar, gs, gr, ps, pr, fs, fr, l0s, l0r, l1s, l1r, l2s, l2r,
):
    rows, width = tok_ref.shape
    hd = kv.shape[2] // 2
    ndp = req_send.shape[0]
    nx = ndp // NZ
    nseq = HEADS * CORES
    half = NZ // 2
    cap = rows // ndp
    quarter = width // 4
    history = rows * nseq
    scale = float(hd) ** -0.5

    dp = lax.axis_index("dp")
    sq = lax.axis_index("seq")
    x, z = lax.div(dp, NZ), lax.rem(dp, NZ)
    y, c = lax.div(sq, CORES), lax.rem(sq, CORES)
    other = 1 - c
    way = 1 - 2 * c
    yp, ym = lax.rem(y + 1, HEADS), lax.rem(y + HEADS - 1, HEADS)
    yo = lax.rem(y + 2, HEADS)
    up, down = (dp, yp * CORES + c), (dp, ym * CORES + c)
    sibling = (dp, y * CORES + other)

    def rcopy(src, dst, send, recv, device):
        return pltpu.make_async_remote_copy(
            src_ref=src, dst_ref=dst, send_sem=send, recv_sem=recv, device_id=device, device_id_type=MESH
        )

    barrier = pltpu.get_barrier_semaphore()

    def greet(i, carry):
        pl.semaphore_signal(barrier, inc=1, device_id=(lax.rem(dp + i, ndp), sq), device_id_type=MESH)
        return carry

    lax.fori_loop(1, ndp, greet, 0)
    for d in range(1, nseq):
        pl.semaphore_signal(barrier, inc=1, device_id=(dp, lax.rem(sq + d, nseq)), device_id_type=MESH)

    hw = HEADS * hd
    pieces = [
        (wo_ref, 0, 0),
        (wp_ref, 0, hd),
        (wp_ref, hw, 2 * hd),
        (wp_ref, 3 * hw, 3 * hd),
        (wp_ref, 2 * hw, 4 * hd),
    ]
    local = []
    for i, (src, start, to) in enumerate(pieces):
        begin = pl.multiple_of(start + y * hd, hd)
        local.append(
            pltpu.make_async_copy(src.at[:, pl.ds(begin, hd)], wall.at[y, x, z, :, pl.ds(to, hd)], lsem.at[i])
        )
    table_copy = pltpu.make_async_copy(table_hbm, table, lsem.at[5])
    for copy in local:
        copy.start()
    table_copy.start()

    tokens = tok_ref[...].astype(F32)
    normed_raw, factor_in = normalize(tokens)
    xn[y] = (normed_raw * gin_ref[...]).astype(BF16)

    own_row = own_ref[...]
    expand = one_hot(lax.div(iota((ndp, rows), 1), cap) == iota((ndp, rows), 0))
    own_rep = dot(jnp.broadcast_to(own_row.astype(F32).astype(BF16), (8, ndp)), expand)[0:1, :]
    to_owner = one_hot(iota((ndp, rows), 0).astype(F32) == own_rep)
    lane = iota((128, rows), 0)
    inside = (lax.div(lane, 2) == lax.rem(iota((128, rows), 1), cap)) & (lane < 2 * cap)
    both = jnp.where(lax.rem(lane, 2) == 0, cand_ref[0:1, :], cand_ref[1:2, :])
    high, low = small_parts(jnp.where(inside, both, 0))
    requests = dot_nt(to_owner, high) * 16.0 + dot_nt(to_owner, low)
    for p in range(ndp):
        req_send[p] = requests[p : p + 1, :]

    for copy in local:
        copy.wait()
    pl.semaphore_wait(barrier, ndp - 1 + nseq - 1)

    x_copies = []
    for d in range(1, nx):
        device = (lax.rem(x + d, nx) * NZ + z, sq)
        copy = rcopy(wall.at[y, x, z], wall.at[y, x, z], xs.at[d - 1], xr.at[d - 1], device)
        copy.start()
        x_copies.append(copy)

    def y_copies(part, send, recv):
        return [
            rcopy(part(y, 0), part(y, 0), send.at[0], recv.at[0], up),
            rcopy(part(y, 1), part(y, 1), send.at[1], recv.at[1], down),
            rcopy(part(y, 1), part(y, 1), send.at[2], recv.at[2], up),
            rcopy(part(y, 0), part(y, 0), send.at[3], recv.at[3], down),
            rcopy(part(ym, 0), part(ym, 0), send.at[4], recv.at[4], up),
            rcopy(part(yp, 1), part(yp, 1), send.at[5], recv.at[5], down),
        ]

    def y_start(copies):
        for copy in copies[:4]:
            copy.start()

    def y_forward(copies):
        copies[0].wait_recv()
        copies[4].start()
        copies[1].wait_recv()
        copies[5].start()

    tok_copies = y_copies(lambda at, h: xn.at[at, pl.ds(h * (rows // 2), rows // 2), :], ts, tr)
    y_start(tok_copies)

    def send_request(i, carry):
        p = lax.rem(dp + i, ndp)
        rcopy(req_send.at[p], req_recv.at[dp], req_s, req_r, (p, sq)).start()
        return carry

    lax.fori_loop(1, ndp, send_request, 0)
    req_recv[dp] = req_send[dp]

    def at_z(distance):
        return lax.rem(z - way * distance + NZ, NZ)

    ahead = (x * NZ + lax.rem(z + way + NZ, NZ), sq)
    z_copies, relays = [], []
    for k in range(half):
        src = wall.at[y, :, at_z(k)]
        z_copies.append(rcopy(src, src, zs.at[k], zr.at[k], ahead))
        if k < half - 1:
            got = wall.at[y, :, at_z(k + 1)]
            relays.append(rcopy(got, got, rs.at[k], rr.at[k], sibling))

    def ring_step(k):
        z_copies[k].wait_recv()
        if k + 1 < half:
            z_copies[k + 1].start()
            relays[k].start()

    for copy in x_copies:
        copy.wait_recv()
    z_copies[0].start()
    first = min(2, half)
    for k in range(first):
        ring_step(k)

    bulk = pl.ds(0, ndp - 1)
    neighbour = (lax.rem(dp + 1, ndp), sq)
    request_bulk = rcopy(req_send.at[bulk], req_recv.at[bulk], req_s, req_r, neighbour)
    request_bulk.wait_recv()
    for p in range(ndp):
        rq[p : p + 1, :] = req_recv[p]
    table_copy.wait()
    high, low = small_parts(rq[...])
    chunk = ndp * TILE // 4
    per = chunk // TILE
    for part in range(4):
        row = iota((chunk, 128), 0)
        spread = one_hot(lax.div(iota((chunk, ndp), 0), TILE) + part * per == iota((chunk, ndp), 1))
        wanted = dot(spread, high) * 16.0 + dot(spread, low)
        place = 2 * lax.rem(row, cap)
        lanes = iota((chunk, 128), 1)
        first_item = jnp.sum(jnp.where(lanes == place, wanted, 0.0), axis=1, keepdims=True)
        second_item = jnp.sum(jnp.where(lanes == place + 1, wanted, 0.0), axis=1, keepdims=True)
        items = iota((chunk, table.shape[0]), 1).astype(F32)
        signs = jnp.where(items == first_item, 1.0, 0.0) - jnp.where(items == second_item, 1.0, 0.0)
        signs = signs.astype(BF16)
        group = lax.div(lax.rem(iota((chunk, quarter), 0), TILE), cap)
        total = jnp.zeros((chunk, quarter), F32)
        for g in range(4):
            term = dot(signs, table[:, g * quarter : (g + 1) * quarter])
            total = jnp.where(group == g, term, total)
        dsend[part * per : (part + 1) * per] = total.astype(BF16).reshape(per, TILE, quarter)

    def send_difference(i, carry):
        p = lax.rem(dp + i, ndp)
        rcopy(dsend.at[p], drecv.at[dp], dif_s, dif_r, (p, sq)).start()
        return carry

    lax.fori_loop(1, ndp, send_difference, 0)
    drecv[dp] = dsend[dp]
    for k in range(first, half):
        ring_step(k)
    y_forward(tok_copies)
    for copy in relays:
        copy.wait_recv()

    near = pl.ds(0, 2 * hd)
    far = pl.ds(2 * hd, 3 * hd)
    per_core = nx // CORES

    def weight_part(columns):
        def part(at, h):
            return wall.at[at, pl.ds(c * per_core, per_core), pl.ds(h * half, half), :, columns]

        return part

    def weight_relay(at, index, columns, send, recv):
        block = wall.at[at, pl.ds(c * per_core, per_core), :, :, columns]
        return rcopy(block, block, send.at[index], recv.at[index], sibling)

    near_copies = y_copies(weight_part(near), ws, wr)
    near_relays = [weight_relay(at, i, near, wrs, wrr) for i, at in enumerate((ym, yp, yo))]
    far_copies = y_copies(weight_part(far), vs, vr)
    far_relays = [weight_relay(at, i, far, vrs, vrr) for i, at in enumerate((ym, yp, yo))]

    def relay_start(copies, relayed):
        copies[2].wait_recv()
        relayed[0].start()
        copies[3].wait_recv()
        relayed[1].start()
        copies[4].wait_recv()
        copies[5].wait_recv()
        relayed[2].start()

    y_start(near_copies)

    length = jnp.sum(jnp.where(iota((1, ndp), 1) == dp, len_ref[...], 0), axis=1, keepdims=True)
    live_total = jnp.sum(len_ref[...], axis=1, keepdims=True).astype(F32)
    index = iota((rows, 1), 0)
    w_head = wall[y, :, :, :, 2 * hd : 5 * hd].reshape(width, 3 * hd)
    kv_copies = []

    def alive_of(block):
        return jnp.where(index + block * rows < length, 1.0, 0.0)

    def project(at, order):
        projected = dot(xn[at], w_head)
        proj[at] = projected
        activated = projected * jax.nn.sigmoid(projected)
        value, key = activated[:, :hd], activated[:, hd : 2 * hd] * alive_of(CORES * at + c)
        query = activated[:, 2 * hd :]
        kv[CORES * at + c, :, :hd] = value.astype(BF16)
        kv[CORES * at + c, :, hd:] = key.astype(BF16)
        copy = rcopy(kv.at[CORES * at + c], kv.at[CORES * at + c], ks.at[order], kr.at[order], sibling)
        copy.start()
        kv_copies.append(copy)
        vt[CORES * at + c] = value.T.astype(BF16)
        kt[CORES * at + c] = key.T.astype(BF16)
        qs[at] = query.astype(BF16)
        qt[at] = query.T.astype(BF16)

    project(y, 0)
    tok_copies[2].wait_recv()
    project(ym, 1)
    tok_copies[3].wait_recv()
    project(yp, 2)
    tok_copies[4].wait_recv()
    tok_copies[5].wait_recv()
    project(yo, 3)
    y_forward(near_copies)
    for copy in kv_copies:
        copy.wait_recv()
    for u in range(HEADS):
        block = CORES * u + other
        both = kv[block].astype(F32)
        vt[block] = both[:, :hd].T.astype(BF16)
        kt[block] = both[:, hd:].T.astype(BF16)

    def send_when(t, src, dst, send, recv):
        @pl.when(y != t)
        def _():
            rcopy(src, dst, send.at[t], recv.at[y], (dp, t * CORES + c)).start()

        @pl.when(y == t)
        def _():
            dst[...] = src[...]

    def wait_when(t, ref, send, recv):
        @pl.when(y != t)
        def _():
            rcopy(ref, ref, send.at[t], recv.at[t], (dp, t * CORES + c)).wait_recv()

    def done_when(t, ref, send, recv):
        @pl.when(y != t)
        def _():
            rcopy(ref, ref, send.at[t], recv.at[t], (dp, t * CORES + c)).wait_send()

    causal = jnp.where(iota((rows, rows), 0) <= iota((rows, rows), 1), 1.0, 0.0)
    before = c.astype(F32)
    for t in reversed(range(HEADS)):
        total = jnp.zeros((hd, rows), F32)
        for parity in range(2):
            for u in range(t + 1):
                block = CORES * u + (c if parity == 0 else other)
                scores = dot(kv[block, :, hd:], qt[t]) * scale
                sigma = jax.nn.sigmoid(scores)
                weights = scores * sigma
                change = (sigma + weights * (1.0 - sigma)) * (scale / history)
                weights = weights * (1.0 / history)
                if u == t:
                    mask = causal if parity == 0 else before
                    weights, change = weights * mask, change * mask
                weights = weights.astype(BF16)
                wst[pair(t, u, parity)] = weights
                slope[pair(t, u, parity)] = change
                total = total + dot(vt[block], weights)
        att_send[t] = total.T.astype(BF16)
        send_when(t, att_send.at[t], att_recv.at[y], as_, ar)

    relay_start(near_copies, near_relays)
    drop = rcopy(dsend.at[bulk], drecv.at[bulk], dif_s, dif_r, neighbour)
    drop.wait_recv()
    own_col = jnp.sum(
        jnp.where(iota((rows, ndp), 1) == lax.div(iota((rows, ndp), 0), cap), own_row, 0), axis=1, keepdims=True
    )
    received = drecv[...].reshape(ndp * TILE, quarter)
    source = own_col * TILE + lax.rem(index, cap)
    for g in range(4):
        pick = one_hot(iota((rows, ndp * TILE), 1) == source + g * cap)
        idiff[:, g * quarter : (g + 1) * quarter] = dot(pick, received).astype(BF16)
    for copy in near_relays:
        copy.wait_recv()
    for t in range(HEADS):
        gproj[:, t * hd : (t + 1) * hd] = dot(xn[y], wall[t, :, :, :, hd : 2 * hd].reshape(width, hd))
    shard = TILE // 2
    line, spot = iota((hw, width), 0), iota((hw, width), 1)
    origin = lax.div(line, shard) * TILE + lax.rem(line, shard)
    for side in range(2):
        select = one_hot(spot == origin + side * shard)
        for t in range(HEADS):
            begin = side * (width // 2) + t * hd
            wout[:, begin : begin + hd] = dot(select, wall[t, :, :, :, :hd].reshape(width, hd)).astype(BF16)

    eye = iota((rows, rows), 0) == iota((rows, rows), 1)
    teacher = jnp.sum(jnp.where(eye, teach_ref[...], 0.0), axis=1, keepdims=True)
    alive = alive_of(sq)
    projected = gproj[...]
    gate = (projected * jax.nn.sigmoid(projected)).astype(BF16).astype(F32)
    gain_mid = gmid_ref[...]
    for t in range(HEADS):
        wait_when(t, att_recv.at[t], as_, ar)
    y_start(far_copies)
    attended = jnp.concatenate([att_recv[t].astype(F32) for t in range(HEADS)], axis=1)
    normed_mid, factor_mid = normalize(attended)
    gated = (normed_mid * gain_mid * gate).astype(BF16)
    layer_out = (tok_ref[...].astype(F32) + dot(gated, wout[...])).astype(BF16).astype(F32)
    difference = idiff[...].astype(F32)
    errors = (jnp.sum(layer_out * difference, axis=1, keepdims=True) - teacher) * alive
    grad_out = (2.0 / live_total * errors * difference).astype(BF16)
    gout[...] = grad_out
    grad_gated = dot_nt(grad_out, wout[...])
    grad_normed = grad_gated * gain_mid * gate
    grad_attended = normalize_back(grad_normed, normed_mid, factor_mid).astype(BF16)
    for t in range(HEADS):
        da_send[t] = grad_attended[:, t * hd : (t + 1) * hd]
        send_when(t, da_send.at[t], da_recv.at[y], gs, gr)
    gpg[...] = (grad_gated * normed_mid * gain_mid * silu_slope(projected)).astype(BF16)

    lb0[sq] = jnp.broadcast_to(jnp.sum(errors * errors, axis=0, keepdims=True), (8, 128))
    loss_copies = []
    for d in range(1, nseq):
        device = (dp, lax.rem(sq + d, nseq))
        loss_copies.append(rcopy(lb0.at[sq], lb0.at[sq], l0s.at[d - 1], l0r.at[d - 1], device))
    for copy in loss_copies:
        copy.start()
    y_forward(far_copies)
    for t in range(HEADS):
        wait_when(t, da_recv.at[t], gs, gr)
    for t in range(HEADS):
        dat[t] = da_recv[t].astype(F32).T.astype(BF16)

    def backward(u, parity):
        block = CORES * u + (c if parity == 0 else other)
        grad_value = jnp.zeros((rows, hd), F32)
        grad_key = jnp.zeros((rows, hd), F32)
        for t in range(u, HEADS):
            n = pair(t, u, parity)
            grad_weights = dot(kv[block, :, :hd], dat[t])
            grad_scores = (grad_weights * slope[n]).astype(BF16)
            grad_value = grad_value + dot(wst[n], da_recv[t])
            grad_key = grad_key + dot(grad_scores, qs[t])
            term = dot(kt[block], grad_scores)
            if parity == 1 and u == 0:
                dqt[t] = term
            else:
                dqt[t] = dqt[t] + term
        return grad_value, grad_key

    part_copies = []
    for u in range(HEADS):
        grad_value, grad_key = backward(u, 1)
        dvk_send[u, :, :hd] = grad_value
        dvk_send[u, :, hd:] = grad_key
        copy = rcopy(dvk_send.at[u], dvk_recv.at[u], ps.at[u], pr.at[u], sibling)
        copy.start()
        part_copies.append(copy)
    relay_start(far_copies, far_relays)
    for copy in loss_copies:
        copy.wait_recv()
    lb1[x] = jnp.sum(lb0[...], axis=0)
    loss_x = []
    for d in range(1, nx):
        device = (lax.rem(x + d, nx) * NZ + z, sq)
        loss_x.append(rcopy(lb1.at[x], lb1.at[x], l1s.at[d - 1], l1r.at[d - 1], device))
    for copy in loss_x:
        copy.start()
    for u in range(HEADS):
        grad_value, grad_key = backward(u, 0)
        part_copies[u].wait_recv()
        keep = alive_of(CORES * u + c)
        grad_value = (grad_value + dvk_recv[u, :, :hd]) * keep
        grad_key = (grad_key + dvk_recv[u, :, hd:]) * keep
        grad_query = dqt[u].T
        gps[u, :, :hd] = (grad_value * silu_slope(proj[u, :, :hd])).astype(BF16)
        gps[u, :, hd : 2 * hd] = (grad_key * silu_slope(proj[u, :, hd : 2 * hd])).astype(BF16)
        gps[u, :, 2 * hd :] = (grad_query * silu_slope(proj[u, :, 2 * hd :])).astype(BF16)
        send_when(u, gps.at[u], gpr.at[y], fs, fr)

    for copy in loss_x:
        copy.wait_recv()
    lb2[z] = jnp.sum(lb1[...], axis=0)
    loss_z = []
    for d in range(1, NZ):
        device = (x * NZ + lax.rem(z + d, NZ), sq)
        loss_z.append(rcopy(lb2.at[z], lb2.at[z], l2s.at[d - 1], l2r.at[d - 1], device))
    for copy in loss_z:
        copy.start()

    for copy in far_relays:
        copy.wait_recv()
    grad_in = jnp.zeros((rows, width), F32)
    for t in range(HEADS):
        grad_in = grad_in + dot_nt(
            gpg[:, t * hd : (t + 1) * hd], wall[t, :, :, :, hd : 2 * hd].reshape(width, hd)
        )
    for t in range(HEADS):
        wait_when(t, gpr.at[t], fs, fr)
        grad_in = grad_in + dot_nt(gpr[t], wall[t, :, :, :, 2 * hd :].reshape(width, 3 * hd))
    normed_raw, factor_in = normalize(tok_ref[...].astype(F32))
    grad_norm = normalize_back(grad_in * gin_ref[...], normed_raw, factor_in)
    out_ref[...] = (gout[...].astype(F32) + grad_norm).astype(BF16)

    for copy in loss_z:
        copy.wait_recv()
    loss_ref[...] = jnp.sum(lb2[...], axis=0) / live_total

    for copy in x_copies + z_copies + relays + tok_copies + near_copies + near_relays + far_copies + far_relays:
        copy.wait_send()
    for copy in kv_copies + part_copies + loss_copies + loss_x + loss_z:
        copy.wait_send()
    request_bulk.wait_send()
    drop.wait_send()
    for t in range(HEADS):
        done_when(t, att_send.at[t], as_, ar)
        done_when(t, da_send.at[t], gs, gr)
        done_when(t, gps.at[t], fs, fr)


def on_device(
    tokens, teacher, cand_items, owner_map, lengths, w_proj, w_out, gain_in, gain_mid, item_table
):
    rows, width = tokens.shape
    ndp = lax.axis_size("dp")
    nx = ndp // NZ
    hw = gain_mid.shape[0]
    hd = hw // HEADS
    blocks = HEADS * CORES
    pairs = HEADS * (HEADS + 1)
    half = NZ // 2
    quarter = width // 4
    w_out_tile = jnp.concatenate([w_out[:, : width // 2], w_out[:, width // 2 :]], axis=0)

    vmem = pltpu.VMEM
    dma = pltpu.SemaphoreType.DMA
    scratch = [
        vmem((HEADS, nx, NZ, TILE, 5 * hd), BF16),
        vmem((HEADS, rows, width), BF16),
        vmem(item_table.shape, BF16),
        vmem((ndp, 1, 128), F32),
        vmem((ndp, 1, 128), F32),
        vmem((ndp, 128), F32),
        vmem((ndp, TILE, quarter), BF16),
        vmem((ndp, TILE, quarter), BF16),
        vmem((rows, width), BF16),
        vmem((HEADS, rows, 3 * hd), F32),
        vmem((blocks, rows, 2 * hd), BF16),
        vmem((blocks, hd, rows), BF16),
        vmem((blocks, hd, rows), BF16),
        vmem((HEADS, rows, hd), BF16),
        vmem((HEADS, hd, rows), BF16),
        vmem((pairs, rows, rows), BF16),
        vmem((pairs, rows, rows), F32),
        vmem((HEADS, rows, hd), BF16),
        vmem((HEADS, rows, hd), BF16),
        vmem((rows, hw), F32),
        vmem((hw, width), BF16),
        vmem((rows, width), BF16),
        vmem((rows, hw), BF16),
        vmem((HEADS, rows, hd), BF16),
        vmem((HEADS, rows, hd), BF16),
        vmem((HEADS, hd, rows), BF16),
        vmem((HEADS, rows, 2 * hd), F32),
        vmem((HEADS, rows, 2 * hd), F32),
        vmem((HEADS, hd, rows), F32),
        vmem((HEADS, rows, 3 * hd), BF16),
        vmem((HEADS, rows, 3 * hd), BF16),
        vmem((blocks, 8, 128), F32),
        vmem((nx, 8, 128), F32),
        vmem((NZ, 8, 128), F32),
        dma((6,)),
        dma((nx,)), dma((nx,)),
        dma((half,)), dma((half,)),
        dma((half,)), dma((half,)),
        dma((6,)), dma((6,)),
        dma, dma,
        dma, dma,
        dma((6,)), dma((6,)), dma((3,)), dma((3,)),
        dma((6,)), dma((6,)), dma((3,)), dma((3,)),
        dma((HEADS,)), dma((HEADS,)),
        dma((HEADS,)), dma((HEADS,)),
        dma((HEADS,)), dma((HEADS,)),
        dma((HEADS,)), dma((HEADS,)),
        dma((HEADS,)), dma((HEADS,)),
        dma((blocks,)), dma((blocks,)), dma((nx,)), dma((nx,)), dma((NZ,)), dma((NZ,)),
    ]
    whole = pl.BlockSpec(memory_space=pltpu.VMEM)
    anywhere = pl.BlockSpec(memory_space=pl.ANY)
    grads, loss = pl.pallas_call(
        kernel,
        out_shape=(jax.ShapeDtypeStruct(tokens.shape, BF16), jax.ShapeDtypeStruct((8, 128), F32)),
        in_specs=[whole] * 5 + [anywhere, anywhere, whole, whole, anywhere],
        out_specs=(whole, whole),
        scratch_shapes=scratch,
        compiler_params=pltpu.CompilerParams(
            collective_id=0, has_side_effects=True, vmem_limit_bytes=56 * 1024 * 1024
        ),
    )(
        tokens,
        teacher.reshape(1, rows),
        cand_items.T,
        owner_map.reshape(1, ndp),
        lengths.reshape(1, ndp),
        w_proj,
        w_out_tile,
        gain_in.reshape(1, width),
        gain_mid.reshape(1, hw),
        item_table,
    )
    return (grads, loss[0, 0])


def solution(mesh):
    in_specs = (
        P(("dp", "seq"), None),
        P(("dp", "seq")),
        P(("dp", "seq"), None),
        P(("dp", "seq")),
        P(),
        P("dp", None),
        P("dp", None),
        P(),
        P(),
        P("dp", None),
    )
    out_specs = (P(("dp", "seq"), None), P())
    return jax.shard_map(
        on_device, mesh=mesh, in_specs=in_specs, out_specs=out_specs, check_vma=False
    )
```

```python
import functools

import jax
import jax.numpy as jnp
from jax import lax
from jax.experimental import pallas as pl
from jax.experimental.pallas import tpu as pltpu
from jax.sharding import PartitionSpec as P

MESH = pl.DeviceIdType.MESH
F32 = jnp.float32
BF16 = jnp.bfloat16
HEADS = 4
NZ = 16
CORES = 2
TILE = 16
EPSILON = 1e-05


def dot(a, b):
    return jnp.dot(a, b, preferred_element_type=F32)


def dot_nt(a, b):
    return lax.dot_general(a, b, (((1,), (1,)), ((), ())), preferred_element_type=F32)


def iota(shape, axis):
    return lax.broadcasted_iota(jnp.int32, shape, axis)


def one_hot(condition):
    return jnp.where(condition, 1.0, 0.0).astype(BF16)


def silu_slope(inputs):
    sigma = jax.nn.sigmoid(inputs)
    return sigma * (1.0 + inputs * (1.0 - sigma))


def normalize(inputs):
    centered = inputs - jnp.mean(inputs, axis=-1, keepdims=True)
    factor = lax.rsqrt(jnp.mean(centered * centered, axis=-1, keepdims=True) + EPSILON)
    return (centered * factor, factor)


def normalize_back(upstream, normed, factor):
    inner = jnp.mean(upstream * normed, axis=-1, keepdims=True)
    return (upstream - jnp.mean(upstream, axis=-1, keepdims=True) - normed * inner) * factor


def small_parts(values):
    whole = values.astype(jnp.int32)
    return (whole >> 4).astype(F32).astype(BF16), (whole & 15).astype(F32).astype(BF16)


def pair(t, u, parity):
    return t * (t + 1) + 2 * u + parity


def kernel(
    tok_hbm, teach_hbm, cand_hbm, own_hbm, len_hbm, wp_ref, wo_hbm, gin_hbm, gmid_hbm, table_hbm,
    out_ref, loss_ref,
    tok_ref, teach_ref, cand_ref, own_ref, len_ref, wo_ref, gin_ref, gmid_ref,
    wall, xn, table, req_send, req_mid, req_recv, rq, dsend, dmid, drecv, idiff, proj, kv, kt, vt, qs, qt, wst, slope,
    att_send, att_recv, gproj, wout, gout, gpg, da_send, da_recv, dat, dvk_send, dvk_recv, dqt,
    gps, gpr, lby, lbc, lbx, lbz,
    lsem, isem, xs, xr, zs, zr, rs, rr, ts, tr, qxs, qxr, qzs, qzr, dxs, dxr, dzs, dzr,
    ws, wr, wrs, wrr, vs, vr, vrs, vrr, ks, kr, as_, ar, gs, gr, ps, pr, fs, fr, lys, lyr, lcs, lcr, lxs, lxr, lzs, lzr,
):
    rows, width = tok_ref.shape
    hd = kv.shape[2] // 2
    nx = req_send.shape[0]
    ndp = nx * NZ
    nseq = HEADS * CORES
    half = NZ // 2
    cap = rows // ndp
    quarter = width // 4
    history = rows * nseq
    scale = float(hd) ** -0.5

    dp = lax.axis_index("dp")
    sq = lax.axis_index("seq")
    x, z = lax.div(dp, NZ), lax.rem(dp, NZ)
    y, c = lax.div(sq, CORES), lax.rem(sq, CORES)
    other = 1 - c
    way = 1 - 2 * c
    yp, ym = lax.rem(y + 1, HEADS), lax.rem(y + HEADS - 1, HEADS)
    yo = lax.rem(y + 2, HEADS)
    up, down = (dp, yp * CORES + c), (dp, ym * CORES + c)
    sibling = (dp, y * CORES + other)

    def rcopy(src, dst, send, recv, device):
        return pltpu.make_async_remote_copy(
            src_ref=src, dst_ref=dst, send_sem=send, recv_sem=recv, device_id=device, device_id_type=MESH
        )

    def beside_x(d):
        return (lax.rem(x + d, nx) * NZ + z, sq)

    def beside_z(d):
        return (x * NZ + lax.rem(z + d, NZ), sq)

    def beside_y(d):
        return (dp, lax.rem(y + d, HEADS) * CORES + c)

    barrier = pltpu.get_barrier_semaphore()
    partners = [sibling] + [beside_y(d) for d in range(1, HEADS)]
    partners += [beside_x(d) for d in range(1, nx)] + [beside_z(d) for d in range(1, NZ)]
    for device in partners:
        pl.semaphore_signal(barrier, inc=1, device_id=device, device_id_type=MESH)

    hw = HEADS * hd
    arguments = [
        (tok_hbm, tok_ref), (gin_hbm, gin_ref), (own_hbm, own_ref), (cand_hbm, cand_ref),
        (wo_hbm, wo_ref), (len_hbm, len_ref), (teach_hbm, teach_ref), (gmid_hbm, gmid_ref),
    ]
    inputs = [pltpu.make_async_copy(src, dst, isem.at[i]) for i, (src, dst) in enumerate(arguments)]
    pieces = [(0, hd), (hw, 2 * hd), (3 * hw, 3 * hd), (2 * hw, 4 * hd)]
    local = []
    for i, (start, to) in enumerate(pieces):
        begin = pl.multiple_of(start + y * hd, hd)
        local.append(
            pltpu.make_async_copy(wp_ref.at[:, pl.ds(begin, hd)], wall.at[y, x, z, :, pl.ds(to, hd)], lsem.at[i])
        )
    table_copy = pltpu.make_async_copy(table_hbm, table, lsem.at[4])
    for copy in inputs + local:
        copy.start()
    table_copy.start()
    for copy in inputs:
        copy.wait()

    tokens = tok_ref[...].astype(F32)
    normed_raw, factor_in = normalize(tokens)
    xn[y] = (normed_raw * gin_ref[...]).astype(BF16)

    own_row = own_ref[...]
    expand = one_hot(lax.div(iota((ndp, rows), 1), cap) == iota((ndp, rows), 0))
    own_rep = dot(jnp.broadcast_to(own_row.astype(F32).astype(BF16), (8, ndp)), expand)[0:1, :]
    to_owner = one_hot(iota((ndp, rows), 0).astype(F32) == own_rep)
    lane = iota((128, rows), 0)
    inside = (lax.div(lane, 2) == lax.rem(iota((128, rows), 1), cap)) & (lane < 2 * cap)
    both = jnp.where(lax.rem(lane, 2) == 0, cand_ref[0:1, :], cand_ref[1:2, :])
    high, low = small_parts(jnp.where(inside, both, 0))
    requests = dot_nt(to_owner, high) * 16.0 + dot_nt(to_owner, low)
    for p in range(ndp):
        req_send[p // NZ, p % NZ] = requests[p : p + 1, :]
    sides = [wo_ref[:, pl.ds(pl.multiple_of(i * (width // 2) + y * hd, hd), hd)].astype(F32) for i in range(2)]
    wall[y, x, z, :, :hd] = jnp.concatenate(sides, axis=0).astype(BF16)

    for copy in local:
        copy.wait()
    pl.semaphore_wait(barrier, len(partners))

    x_copies = []
    for d in range(1, nx):
        copy = rcopy(wall.at[y, x, z], wall.at[y, x, z], xs.at[d - 1], xr.at[d - 1], beside_x(d))
        copy.start()
        x_copies.append(copy)

    def y_copies(part, send, recv):
        return [
            rcopy(part(y, 0), part(y, 0), send.at[0], recv.at[0], up),
            rcopy(part(y, 1), part(y, 1), send.at[1], recv.at[1], down),
            rcopy(part(y, 1), part(y, 1), send.at[2], recv.at[2], up),
            rcopy(part(y, 0), part(y, 0), send.at[3], recv.at[3], down),
            rcopy(part(ym, 0), part(ym, 0), send.at[4], recv.at[4], up),
            rcopy(part(yp, 1), part(yp, 1), send.at[5], recv.at[5], down),
        ]

    def y_start(copies):
        for copy in copies[:4]:
            copy.start()

    def y_forward(copies):
        copies[0].wait_recv()
        copies[4].start()
        copies[1].wait_recv()
        copies[5].start()

    tok_copies = y_copies(lambda at, h: xn.at[at, pl.ds(h * (rows // 2), rows // 2), :], ts, tr)

    request_x = []
    for d in range(1, nx):
        block = req_send.at[lax.rem(x + d, nx)]
        request_x.append(rcopy(block, req_mid.at[x], qxs.at[d - 1], qxr.at[d - 1], beside_x(d)))
    for copy in request_x:
        copy.start()
    req_mid[x] = req_send[x]

    def at_z(distance):
        return lax.rem(z - way * distance + NZ, NZ)

    ahead = (x * NZ + lax.rem(z + way + NZ, NZ), sq)
    z_copies, relays = [], []
    for k in range(half):
        src = wall.at[y, :, at_z(k)]
        z_copies.append(rcopy(src, src, zs.at[k], zr.at[k], ahead))
        if k < half - 1:
            got = wall.at[y, :, at_z(k + 1)]
            relays.append(rcopy(got, got, rs.at[k], rr.at[k], sibling))

    def ring_step(k):
        z_copies[k].wait_recv()
        if k + 1 < half:
            z_copies[k + 1].start()
            relays[k].start()

    for copy in x_copies:
        copy.wait_recv()
    z_copies[0].start()
    y_start(tok_copies)
    for copy in request_x:
        copy.wait_recv()
    request_z = []
    for d in range(1, NZ):
        block = req_mid.at[:, lax.rem(z + d, NZ)]
        request_z.append(rcopy(block, req_recv.at[:, z], qzs.at[d - 1], qzr.at[d - 1], beside_z(d)))
    for copy in request_z:
        copy.start()
    req_recv[:, z] = req_mid[:, z]
    first = min(2, half)
    for k in range(first):
        ring_step(k)

    for copy in request_z:
        copy.wait_recv()
    for p in range(ndp):
        rq[p : p + 1, :] = req_recv[p // NZ, p % NZ]
    table_copy.wait()
    high, low = small_parts(rq[...])
    chunk = NZ * TILE
    diff_x = []
    for d in range(nx):
        side = lax.rem(x + d + 1, nx)
        row = iota((chunk, 128), 0)
        spread = one_hot(lax.div(iota((chunk, ndp), 0), TILE) + side * NZ == iota((chunk, ndp), 1))
        wanted = dot(spread, high) * 16.0 + dot(spread, low)
        place = 2 * lax.rem(row, cap)
        lanes = iota((chunk, 128), 1)
        first_item = jnp.sum(jnp.where(lanes == place, wanted, 0.0), axis=1, keepdims=True)
        second_item = jnp.sum(jnp.where(lanes == place + 1, wanted, 0.0), axis=1, keepdims=True)
        items = iota((chunk, table.shape[0]), 1).astype(F32)
        signs = jnp.where(items == first_item, 1.0, 0.0) - jnp.where(items == second_item, 1.0, 0.0)
        signs = signs.astype(BF16)
        group = lax.div(lax.rem(iota((chunk, quarter), 0), TILE), cap)
        total = jnp.zeros((chunk, quarter), F32)
        for g in range(4):
            term = dot(signs, table[:, g * quarter : (g + 1) * quarter])
            total = jnp.where(group == g, term, total)
        total = total.astype(BF16).reshape(NZ, TILE, quarter)
        if d + 1 < nx:
            dsend[side] = total
            diff_x.append(rcopy(dsend.at[side], dmid.at[x], dxs.at[d], dxr.at[d], beside_x(d + 1)))
            diff_x[d].start()
        else:
            dmid[x] = total
        if first + d < half:
            ring_step(first + d)
    y_forward(tok_copies)
    first = first + nx
    if first < half:
        ring_step(first)

    for copy in diff_x:
        copy.wait_recv()
    diff_z = []
    for d in range(1, NZ):
        block = dmid.at[:, lax.rem(z + d, NZ)]
        diff_z.append(rcopy(block, drecv.at[:, z], dzs.at[d - 1], dzr.at[d - 1], beside_z(d)))
    for copy in diff_z:
        copy.start()
    drecv[:, z] = dmid[:, z]
    for k in range(first + 1, half):
        ring_step(k)
    for copy in relays:
        copy.wait_recv()

    near = pl.ds(0, 2 * hd)
    far = pl.ds(2 * hd, 3 * hd)
    per_core = nx // CORES

    def weight_part(columns):
        def part(at, h):
            return wall.at[at, pl.ds(c * per_core, per_core), pl.ds(h * half, half), :, columns]

        return part

    def weight_relay(at, index, columns, send, recv):
        block = wall.at[at, pl.ds(c * per_core, per_core), :, :, columns]
        return rcopy(block, block, send.at[index], recv.at[index], sibling)

    near_copies = y_copies(weight_part(near), ws, wr)
    near_relays = [weight_relay(at, i, near, wrs, wrr) for i, at in enumerate((ym, yp, yo))]
    far_copies = y_copies(weight_part(far), vs, vr)
    far_relays = [weight_relay(at, i, far, vrs, vrr) for i, at in enumerate((ym, yp, yo))]

    def relay_start(copies, relayed):
        copies[2].wait_recv()
        relayed[0].start()
        copies[3].wait_recv()
        relayed[1].start()
        copies[4].wait_recv()
        copies[5].wait_recv()
        relayed[2].start()

    y_start(near_copies)

    length = jnp.sum(jnp.where(iota((1, ndp), 1) == dp, len_ref[...], 0), axis=1, keepdims=True)
    live_total = jnp.sum(len_ref[...], axis=1, keepdims=True).astype(F32)
    index = iota((rows, 1), 0)
    w_head = wall[y, :, :, :, 2 * hd : 5 * hd].reshape(width, 3 * hd)
    kv_copies = []

    def alive_of(block):
        return jnp.where(index + block * rows < length, 1.0, 0.0)

    def project(at, order):
        projected = dot(xn[at], w_head)
        proj[at] = projected
        activated = projected * jax.nn.sigmoid(projected)
        value, key = activated[:, :hd], activated[:, hd : 2 * hd] * alive_of(CORES * at + c)
        query = activated[:, 2 * hd :]
        kv[CORES * at + c, :, :hd] = value.astype(BF16)
        kv[CORES * at + c, :, hd:] = key.astype(BF16)
        copy = rcopy(kv.at[CORES * at + c], kv.at[CORES * at + c], ks.at[order], kr.at[order], sibling)
        copy.start()
        kv_copies.append(copy)
        vt[CORES * at + c] = value.T.astype(BF16)
        kt[CORES * at + c] = key.T.astype(BF16)
        qs[at] = query.astype(BF16)
        qt[at] = query.T.astype(BF16)

    project(y, 0)
    tok_copies[2].wait_recv()
    project(ym, 1)
    tok_copies[3].wait_recv()
    project(yp, 2)
    tok_copies[4].wait_recv()
    tok_copies[5].wait_recv()
    project(yo, 3)
    y_forward(near_copies)
    y_start(far_copies)
    for copy in kv_copies:
        copy.wait_recv()
    for u in range(HEADS):
        block = CORES * u + other
        both = kv[block].astype(F32)
        vt[block] = both[:, :hd].T.astype(BF16)
        kt[block] = both[:, hd:].T.astype(BF16)

    def send_when(t, src, dst, send, recv):
        @pl.when(y != t)
        def _():
            rcopy(src, dst, send.at[t], recv.at[y], (dp, t * CORES + c)).start()

        @pl.when(y == t)
        def _():
            dst[...] = src[...]

    def wait_when(t, ref, send, recv):
        @pl.when(y != t)
        def _():
            rcopy(ref, ref, send.at[t], recv.at[t], (dp, t * CORES + c)).wait_recv()

    def done_when(t, ref, send, recv):
        @pl.when(y != t)
        def _():
            rcopy(ref, ref, send.at[t], recv.at[t], (dp, t * CORES + c)).wait_send()

    causal = jnp.where(iota((rows, rows), 0) <= iota((rows, rows), 1), 1.0, 0.0)
    before = c.astype(F32)
    for t in reversed(range(HEADS)):
        total = jnp.zeros((hd, rows), F32)
        for parity in range(2):
            for u in range(t + 1):
                block = CORES * u + (c if parity == 0 else other)
                scores = dot(kv[block, :, hd:], qt[t]) * scale
                sigma = jax.nn.sigmoid(scores)
                weights = scores * sigma
                change = (sigma + weights * (1.0 - sigma)) * (scale / history)
                weights = weights * (1.0 / history)
                if u == t:
                    mask = causal if parity == 0 else before
                    weights, change = weights * mask, change * mask
                weights = weights.astype(BF16)
                wst[pair(t, u, parity)] = weights
                slope[pair(t, u, parity)] = change
                total = total + dot(vt[block], weights)
        att_send[t] = total.T.astype(BF16)
        send_when(t, att_send.at[t], att_recv.at[y], as_, ar)

    relay_start(near_copies, near_relays)
    y_forward(far_copies)
    for copy in diff_z:
        copy.wait_recv()
    own_col = jnp.sum(
        jnp.where(iota((rows, ndp), 1) == lax.div(iota((rows, ndp), 0), cap), own_row, 0), axis=1, keepdims=True
    )
    received = drecv[...].reshape(ndp * TILE, quarter)
    source = own_col * TILE + lax.rem(index, cap)
    for g in range(4):
        pick = one_hot(iota((rows, ndp * TILE), 1) == source + g * cap)
        idiff[:, g * quarter : (g + 1) * quarter] = dot(pick, received).astype(BF16)
    for copy in near_relays:
        copy.wait_recv()
    for t in range(HEADS):
        gproj[:, t * hd : (t + 1) * hd] = dot(xn[y], wall[t, :, :, :, hd : 2 * hd].reshape(width, hd))
    shard = TILE // 2
    line, spot = iota((hw, width), 0), iota((hw, width), 1)
    origin = lax.div(line, shard) * TILE + lax.rem(line, shard)
    for side in range(2):
        select = one_hot(spot == origin + side * shard)
        for t in range(HEADS):
            begin = side * (width // 2) + t * hd
            wout[:, begin : begin + hd] = dot(select, wall[t, :, :, :, :hd].reshape(width, hd)).astype(BF16)

    eye = iota((rows, rows), 0) == iota((rows, rows), 1)
    teacher = jnp.sum(jnp.where(eye, teach_ref[...], 0.0), axis=1, keepdims=True)
    alive = alive_of(sq)
    projected = gproj[...]
    gate = (projected * jax.nn.sigmoid(projected)).astype(BF16).astype(F32)
    gain_mid = gmid_ref[...]
    for t in range(HEADS):
        wait_when(t, att_recv.at[t], as_, ar)
    attended = jnp.concatenate([att_recv[t].astype(F32) for t in range(HEADS)], axis=1)
    normed_mid, factor_mid = normalize(attended)
    gated = (normed_mid * gain_mid * gate).astype(BF16)
    layer_out = (tok_ref[...].astype(F32) + dot(gated, wout[...])).astype(BF16).astype(F32)
    difference = idiff[...].astype(F32)
    errors = (jnp.sum(layer_out * difference, axis=1, keepdims=True) - teacher) * alive
    grad_out = (2.0 / live_total * errors * difference).astype(BF16)
    gout[...] = grad_out
    grad_gated = dot_nt(grad_out, wout[...])
    grad_normed = grad_gated * gain_mid * gate
    grad_attended = normalize_back(grad_normed, normed_mid, factor_mid).astype(BF16)
    for t in range(HEADS):
        da_send[t] = grad_attended[:, t * hd : (t + 1) * hd]
        send_when(t, da_send.at[t], da_recv.at[y], gs, gr)
    gpg[...] = (grad_gated * normed_mid * gain_mid * silu_slope(projected)).astype(BF16)

    def loss_send(buffer, place, send, recv, devices):
        copies = [
            rcopy(buffer.at[place], buffer.at[place], send.at[i], recv.at[i], device)
            for i, device in enumerate(devices)
        ]
        for copy in copies:
            copy.start()
        return copies

    lby[y] = jnp.broadcast_to(jnp.sum(errors * errors, axis=0, keepdims=True), (8, 128))
    loss_y = loss_send(lby, y, lys, lyr, [beside_y(d) for d in range(1, HEADS)])
    for t in range(HEADS):
        wait_when(t, da_recv.at[t], gs, gr)
    for t in range(HEADS):
        dat[t] = da_recv[t].astype(F32).T.astype(BF16)

    def backward(u, parity):
        block = CORES * u + (c if parity == 0 else other)
        grad_value = jnp.zeros((rows, hd), F32)
        grad_key = jnp.zeros((rows, hd), F32)
        for t in range(u, HEADS):
            n = pair(t, u, parity)
            grad_weights = dot(kv[block, :, :hd], dat[t])
            grad_scores = (grad_weights * slope[n]).astype(BF16)
            grad_value = grad_value + dot(wst[n], da_recv[t])
            grad_key = grad_key + dot(grad_scores, qs[t])
            term = dot(kt[block], grad_scores)
            if parity == 1 and u == 0:
                dqt[t] = term
            else:
                dqt[t] = dqt[t] + term
        return grad_value, grad_key

    part_copies = []
    for u in range(HEADS):
        grad_value, grad_key = backward(u, 1)
        dvk_send[u, :, :hd] = grad_value
        dvk_send[u, :, hd:] = grad_key
        copy = rcopy(dvk_send.at[u], dvk_recv.at[u], ps.at[u], pr.at[u], sibling)
        copy.start()
        part_copies.append(copy)
    relay_start(far_copies, far_relays)
    for copy in loss_y:
        copy.wait_recv()
    lbc[c] = jnp.sum(lby[...], axis=0)
    loss_c = loss_send(lbc, c, lcs, lcr, [sibling])
    for u in range(HEADS):
        grad_value, grad_key = backward(u, 0)
        part_copies[u].wait_recv()
        keep = alive_of(CORES * u + c)
        grad_value = (grad_value + dvk_recv[u, :, :hd]) * keep
        grad_key = (grad_key + dvk_recv[u, :, hd:]) * keep
        grad_query = dqt[u].T
        gps[u, :, :hd] = (grad_value * silu_slope(proj[u, :, :hd])).astype(BF16)
        gps[u, :, hd : 2 * hd] = (grad_key * silu_slope(proj[u, :, hd : 2 * hd])).astype(BF16)
        gps[u, :, 2 * hd :] = (grad_query * silu_slope(proj[u, :, 2 * hd :])).astype(BF16)
        send_when(u, gps.at[u], gpr.at[y], fs, fr)
        if u == 0:
            loss_c[0].wait_recv()
            lbx[x] = jnp.sum(lbc[...], axis=0)
            loss_x = loss_send(lbx, x, lxs, lxr, [beside_x(d) for d in range(1, nx)])

    for copy in loss_x:
        copy.wait_recv()
    lbz[z] = jnp.sum(lbx[...], axis=0)
    loss_z = loss_send(lbz, z, lzs, lzr, [beside_z(d) for d in range(1, NZ)])

    for copy in far_relays:
        copy.wait_recv()
    grad_in = jnp.zeros((rows, width), F32)
    for t in range(HEADS):
        grad_in = grad_in + dot_nt(
            gpg[:, t * hd : (t + 1) * hd], wall[t, :, :, :, hd : 2 * hd].reshape(width, hd)
        )
    for t in range(HEADS):
        wait_when(t, gpr.at[t], fs, fr)
        grad_in = grad_in + dot_nt(gpr[t], wall[t, :, :, :, 2 * hd :].reshape(width, 3 * hd))
    normed_raw, factor_in = normalize(tok_ref[...].astype(F32))
    grad_norm = normalize_back(grad_in * gin_ref[...], normed_raw, factor_in)
    out_ref[...] = (gout[...].astype(F32) + grad_norm).astype(BF16)

    for copy in loss_z:
        copy.wait_recv()
    loss_ref[...] = jnp.sum(lbz[...], axis=0)[0:1, 0:1] / live_total

    for copy in x_copies + z_copies + relays + tok_copies + near_copies + near_relays + far_copies + far_relays:
        copy.wait_send()
    for copy in kv_copies + part_copies + loss_y + loss_c + loss_x + loss_z:
        copy.wait_send()
    for copy in request_x + request_z + diff_x + diff_z:
        copy.wait_send()
    for t in range(HEADS):
        done_when(t, att_send.at[t], as_, ar)
        done_when(t, da_send.at[t], gs, gr)
        done_when(t, gps.at[t], fs, fr)


def on_device(
    tokens, teacher, cand_items, owner_map, lengths, w_proj, w_out, gain_in, gain_mid, item_table
):
    rows, width = tokens.shape
    ndp = lax.axis_size("dp")
    nx = ndp // NZ
    hw = gain_mid.shape[0]
    hd = hw // HEADS
    blocks = HEADS * CORES
    pairs = HEADS * (HEADS + 1)
    half = NZ // 2
    quarter = width // 4

    vmem = pltpu.VMEM
    dma = pltpu.SemaphoreType.DMA
    scratch = [
        vmem((rows, width), BF16),
        vmem((1, rows), F32),
        vmem((2, rows), jnp.int32),
        vmem((1, ndp), jnp.int32),
        vmem((1, ndp), jnp.int32),
        vmem(w_out.shape, BF16),
        vmem((1, width), F32),
        vmem((1, hw), F32),
        vmem((HEADS, nx, NZ, TILE, 5 * hd), BF16),
        vmem((HEADS, rows, width), BF16),
        vmem(item_table.shape, BF16),
        vmem((nx, NZ, 1, 128), F32),
        vmem((nx, NZ, 1, 128), F32),
        vmem((nx, NZ, 1, 128), F32),
        vmem((ndp, 128), F32),
        vmem((nx, NZ, TILE, quarter), BF16),
        vmem((nx, NZ, TILE, quarter), BF16),
        vmem((nx, NZ, TILE, quarter), BF16),
        vmem((rows, width), BF16),
        vmem((HEADS, rows, 3 * hd), F32),
        vmem((blocks, rows, 2 * hd), BF16),
        vmem((blocks, hd, rows), BF16),
        vmem((blocks, hd, rows), BF16),
        vmem((HEADS, rows, hd), BF16),
        vmem((HEADS, hd, rows), BF16),
        vmem((pairs, rows, rows), BF16),
        vmem((pairs, rows, rows), F32),
        vmem((HEADS, rows, hd), BF16),
        vmem((HEADS, rows, hd), BF16),
        vmem((rows, hw), F32),
        vmem((hw, width), BF16),
        vmem((rows, width), BF16),
        vmem((rows, hw), BF16),
        vmem((HEADS, rows, hd), BF16),
        vmem((HEADS, rows, hd), BF16),
        vmem((HEADS, hd, rows), BF16),
        vmem((HEADS, rows, 2 * hd), F32),
        vmem((HEADS, rows, 2 * hd), F32),
        vmem((HEADS, hd, rows), F32),
        vmem((HEADS, rows, 3 * hd), BF16),
        vmem((HEADS, rows, 3 * hd), BF16),
        vmem((HEADS, 8, 128), F32),
        vmem((CORES, 8, 128), F32),
        vmem((nx, 8, 128), F32),
        vmem((NZ, 8, 128), F32),
        dma((5,)),
        dma((8,)),
        dma((nx,)), dma((nx,)),
        dma((half,)), dma((half,)),
        dma((half,)), dma((half,)),
        dma((6,)), dma((6,)),
        dma((nx,)), dma((nx,)), dma((NZ,)), dma((NZ,)),
        dma((nx,)), dma((nx,)), dma((NZ,)), dma((NZ,)),
        dma((6,)), dma((6,)), dma((3,)), dma((3,)),
        dma((6,)), dma((6,)), dma((3,)), dma((3,)),
        dma((HEADS,)), dma((HEADS,)),
        dma((HEADS,)), dma((HEADS,)),
        dma((HEADS,)), dma((HEADS,)),
        dma((HEADS,)), dma((HEADS,)),
        dma((HEADS,)), dma((HEADS,)),
        dma((HEADS,)), dma((HEADS,)), dma((1,)), dma((1,)), dma((nx,)), dma((nx,)), dma((NZ,)), dma((NZ,)),
    ]
    whole = pl.BlockSpec(memory_space=pltpu.VMEM)
    anywhere = pl.BlockSpec(memory_space=pl.ANY)
    grads, loss = pl.pallas_call(
        kernel,
        out_shape=(jax.ShapeDtypeStruct(tokens.shape, BF16), jax.ShapeDtypeStruct((1, 1), F32)),
        in_specs=[anywhere] * 10,
        out_specs=(whole, whole),
        scratch_shapes=scratch,
        compiler_params=pltpu.CompilerParams(
            collective_id=0, has_side_effects=True, vmem_limit_bytes=56 * 1024 * 1024
        ),
    )(
        tokens,
        teacher.reshape(1, rows),
        cand_items.T,
        owner_map.reshape(1, ndp),
        lengths.reshape(1, ndp),
        w_proj,
        w_out,
        gain_in.reshape(1, width),
        gain_mid.reshape(1, hw),
        item_table,
    )
    return (grads, loss[0, 0])


def solution(mesh):
    in_specs = (
        P(("dp", "seq"), None),
        P(("dp", "seq")),
        P(("dp", "seq"), None),
        P(("dp", "seq")),
        P(),
        P("dp", None),
        P("dp", None),
        P(),
        P(),
        P("dp", None),
    )
    out_specs = (P(("dp", "seq"), None), P())
    return jax.shard_map(
        on_device, mesh=mesh, in_specs=in_specs, out_specs=out_specs, check_vma=False
    )
```

```python
import functools

import jax
import jax.numpy as jnp
from jax import lax
from jax.experimental import pallas as pl
from jax.experimental.pallas import tpu as pltpu
from jax.sharding import PartitionSpec as P

MESH = pl.DeviceIdType.MESH
F32 = jnp.float32
BF16 = jnp.bfloat16
HEADS = 4
NZ = 16
CORES = 2
TILE = 16
EPSILON = 1e-05


def dot(a, b):
    return jnp.dot(a, b, preferred_element_type=F32)


def dot_nt(a, b):
    return lax.dot_general(a, b, (((1,), (1,)), ((), ())), preferred_element_type=F32)


def iota(shape, axis):
    return lax.broadcasted_iota(jnp.int32, shape, axis)


def one_hot(condition):
    return jnp.where(condition, 1.0, 0.0).astype(BF16)


def silu_slope(inputs):
    sigma = jax.nn.sigmoid(inputs)
    return sigma * (1.0 + inputs * (1.0 - sigma))


def normalize(inputs):
    centered = inputs - jnp.mean(inputs, axis=-1, keepdims=True)
    factor = lax.rsqrt(jnp.mean(centered * centered, axis=-1, keepdims=True) + EPSILON)
    return (centered * factor, factor)


def normalize_back(upstream, normed, factor):
    inner = jnp.mean(upstream * normed, axis=-1, keepdims=True)
    return (upstream - jnp.mean(upstream, axis=-1, keepdims=True) - normed * inner) * factor


def small_parts(values):
    whole = values.astype(jnp.int32)
    return (whole >> 4).astype(F32).astype(BF16), (whole & 15).astype(F32).astype(BF16)


def kernel(
    tok_hbm, teach_hbm, cand_hbm, own_hbm, len_hbm, wp_ref, wo_hbm, gin_hbm, gmid_hbm, table_hbm,
    out_ref, loss_ref,
    tok_ref, teach_ref, cand_ref, own_ref, len_ref, wo_ref, gin_ref, gmid_ref,
    wall, xn, table, req_send, req_mid, req_recv, rq, dsend, dmid, drecv, idiff, proj, kv, kt, vt, qs, qt, wst, slope,
    att_send, att_recv, gproj, wout, gout, gpg, da_send, da_recv, dat, dvk_send, dvk_recv, dst,
    gps, gpr, lby, lbc, lbx, lbz,
    lsem, isem, xs, xr, zs, zr, rs, rr, ts, tr, qxs, qxr, qzs, qzr, dxs, dxr, dzs, dzr, ezs, ezr,
    ws, wr, wrs, wrr, vs, vr, vrs, vrr, ks, kr, as_, ar, gs, gr, ps, pr, fs, fr, lys, lyr, lcs, lcr, lxs, lxr, lzs, lzr,
):
    rows, width = tok_ref.shape
    hd = kv.shape[2] // 2
    nx = req_send.shape[0]
    ndp = nx * NZ
    nseq = HEADS * CORES
    half = NZ // 2
    cap = rows // ndp
    quarter = width // 4
    history = rows * nseq
    scale = float(hd) ** -0.5

    dp = lax.axis_index("dp")
    sq = lax.axis_index("seq")
    x, z = lax.div(dp, NZ), lax.rem(dp, NZ)
    y, c = lax.div(sq, CORES), lax.rem(sq, CORES)
    other = 1 - c
    way = 1 - 2 * c
    yp, ym = lax.rem(y + 1, HEADS), lax.rem(y + HEADS - 1, HEADS)
    yo = lax.rem(y + 2, HEADS)
    up, down = (dp, yp * CORES + c), (dp, ym * CORES + c)
    sibling = (dp, y * CORES + other)

    def rcopy(src, dst, send, recv, device):
        return pltpu.make_async_remote_copy(
            src_ref=src, dst_ref=dst, send_sem=send, recv_sem=recv, device_id=device, device_id_type=MESH
        )

    def beside_x(d):
        return (lax.rem(x + d, nx) * NZ + z, sq)

    def beside_z(d):
        return (x * NZ + lax.rem(z + d, NZ), sq)

    def beside_y(d):
        return (dp, lax.rem(y + d, HEADS) * CORES + c)

    barrier = pltpu.get_barrier_semaphore()
    partners = [sibling] + [beside_y(d) for d in range(1, HEADS)]
    partners += [beside_x(d) for d in range(1, nx)] + [beside_z(d) for d in range(1, NZ)]
    for device in partners:
        pl.semaphore_signal(barrier, inc=1, device_id=device, device_id_type=MESH)

    hw = HEADS * hd
    arguments = [
        (tok_hbm, tok_ref), (gin_hbm, gin_ref), (own_hbm, own_ref), (cand_hbm, cand_ref),
        (wo_hbm, wo_ref), (len_hbm, len_ref), (teach_hbm, teach_ref), (gmid_hbm, gmid_ref),
    ]
    inputs = [pltpu.make_async_copy(src, dst, isem.at[i]) for i, (src, dst) in enumerate(arguments)]
    pieces = [(0, hd), (hw, 2 * hd), (3 * hw, 3 * hd), (2 * hw, 4 * hd)]
    local = []
    for i, (start, to) in enumerate(pieces):
        begin = pl.multiple_of(start + y * hd, hd)
        local.append(
            pltpu.make_async_copy(wp_ref.at[:, pl.ds(begin, hd)], wall.at[y, x, z, :, pl.ds(to, hd)], lsem.at[i])
        )
    table_copy = pltpu.make_async_copy(table_hbm, table, lsem.at[4])
    for copy in inputs + local:
        copy.start()
    table_copy.start()
    for copy in inputs:
        copy.wait()

    tokens = tok_ref[...].astype(F32)
    normed_raw, factor_in = normalize(tokens)
    xn[y] = (normed_raw * gin_ref[...]).astype(BF16)

    own_row = own_ref[...]
    expand = one_hot(lax.div(iota((ndp, rows), 1), cap) == iota((ndp, rows), 0))
    own_rep = dot(jnp.broadcast_to(own_row.astype(F32).astype(BF16), (8, ndp)), expand)[0:1, :]
    to_owner = one_hot(iota((ndp, rows), 0).astype(F32) == own_rep)
    lane = iota((128, rows), 0)
    inside = (lax.div(lane, 2) == lax.rem(iota((128, rows), 1), cap)) & (lane < 2 * cap)
    both = jnp.where(lax.rem(lane, 2) == 0, cand_ref[0:1, :], cand_ref[1:2, :])
    high, low = small_parts(jnp.where(inside, both, 0))
    requests = dot_nt(to_owner, high) * 16.0 + dot_nt(to_owner, low)
    for p in range(ndp):
        req_send[p // NZ, p % NZ] = requests[p : p + 1, :]
    sides = [wo_ref[:, pl.ds(pl.multiple_of(i * (width // 2) + y * hd, hd), hd)].astype(F32) for i in range(2)]
    wall[y, x, z, :, :hd] = jnp.concatenate(sides, axis=0).astype(BF16)

    for copy in local:
        copy.wait()
    pl.semaphore_wait(barrier, len(partners))

    def y_copies(part, send, recv):
        return [
            rcopy(part(y, 0), part(y, 0), send.at[0], recv.at[0], up),
            rcopy(part(y, 1), part(y, 1), send.at[1], recv.at[1], down),
            rcopy(part(y, 1), part(y, 1), send.at[2], recv.at[2], up),
            rcopy(part(y, 0), part(y, 0), send.at[3], recv.at[3], down),
            rcopy(part(ym, 0), part(ym, 0), send.at[4], recv.at[4], up),
            rcopy(part(yp, 1), part(yp, 1), send.at[5], recv.at[5], down),
        ]

    def y_start(copies):
        for copy in copies[:4]:
            copy.start()

    def y_forward(copies):
        copies[0].wait_recv()
        copies[4].start()
        copies[1].wait_recv()
        copies[5].start()

    tok_copies = y_copies(lambda at, h: xn.at[at, pl.ds(h * (rows // 2), rows // 2), :], ts, tr)

    request_x = []
    for d in range(1, nx):
        block = req_send.at[lax.rem(x + d, nx)]
        request_x.append(rcopy(block, req_mid.at[x], qxs.at[d - 1], qxr.at[d - 1], beside_x(d)))
    for copy in request_x:
        copy.start()
    req_mid[x] = req_send[x]
    x_copies = []
    for d in range(1, nx):
        copy = rcopy(wall.at[y, x, z], wall.at[y, x, z], xs.at[d - 1], xr.at[d - 1], beside_x(d))
        copy.start()
        x_copies.append(copy)
    y_start(tok_copies)

    for copy in request_x:
        copy.wait_recv()
    request_z = []
    for d in range(1, NZ):
        block = req_mid.at[:, lax.rem(z + d, NZ)]
        request_z.append(rcopy(block, req_recv.at[:, z], qzs.at[d - 1], qzr.at[d - 1], beside_z(d)))
    for copy in request_z:
        copy.start()
    req_recv[:, z] = req_mid[:, z]

    def at_z(distance):
        return lax.rem(z - way * distance + NZ, NZ)

    ahead = (x * NZ + lax.rem(z + way + NZ, NZ), sq)
    z_copies, relays = [], []
    for k in range(half):
        src = wall.at[y, :, at_z(k)]
        z_copies.append(rcopy(src, src, zs.at[k], zr.at[k], ahead))
        if k < half - 1:
            got = wall.at[y, :, at_z(k + 1)]
            relays.append(rcopy(got, got, rs.at[k], rr.at[k], sibling))

    def ring_step(k):
        z_copies[k].wait_recv()
        if k + 1 < half:
            z_copies[k + 1].start()
            relays[k].start()

    for copy in x_copies:
        copy.wait_recv()
    z_copies[0].start()

    for copy in request_z:
        copy.wait_recv()
    for p in range(ndp):
        rq[p : p + 1, :] = req_recv[p // NZ, p % NZ]
    table_copy.wait()
    high, low = small_parts(rq[...])
    chunk = NZ * TILE
    row = iota((chunk, 128), 0)
    place = 2 * lax.rem(row, cap)
    lanes = iota((chunk, 128), 1)
    group = lax.div(lax.rem(iota((chunk, quarter), 0), TILE), cap)

    def differences(side):
        spread = one_hot(lax.div(iota((chunk, ndp), 0), TILE) + side * NZ == iota((chunk, ndp), 1))
        wanted = dot(spread, high) * 16.0 + dot(spread, low)
        first_item = jnp.sum(jnp.where(lanes == place, wanted, 0.0), axis=1, keepdims=True)
        second_item = jnp.sum(jnp.where(lanes == place + 1, wanted, 0.0), axis=1, keepdims=True)
        items = iota((chunk, table.shape[0]), 1).astype(F32)
        signs = jnp.where(items == first_item, 1.0, 0.0) - jnp.where(items == second_item, 1.0, 0.0)
        signs = signs.astype(BF16)
        total = jnp.zeros((chunk, quarter), F32)
        for g in range(4):
            term = dot(signs, table[:, g * quarter : (g + 1) * quarter])
            total = jnp.where(group == g, term, total)
        return total.astype(BF16).reshape(NZ, TILE, quarter)

    def along_z(hops, send, recv):
        copies = []
        for d in range(1, NZ):
            block = dmid.at[hops, lax.rem(z + d, NZ)]
            copies.append(rcopy(block, drecv.at[hops, z], send.at[d - 1], recv.at[d - 1], beside_z(d)))
        for copy in copies:
            copy.start()
        drecv[hops, z] = dmid[hops, z]
        return copies

    dmid[0] = differences(x)
    diff_z = along_z(pl.ds(0, 1), dzs, dzr)
    diff_x = []
    for d in range(1, nx):
        side = lax.rem(x + d, nx)
        dsend[side] = differences(side)
        copy = rcopy(dsend.at[side], dmid.at[d], dxs.at[d - 1], dxr.at[d - 1], beside_x(d))
        copy.start()
        diff_x.append(copy)
        if d - 1 < half:
            ring_step(d - 1)
    y_forward(tok_copies)
    first = nx - 1
    if first < half:
        ring_step(first)
    for copy in diff_x:
        copy.wait_recv()
    diff_z += along_z(pl.ds(1, nx - 1), ezs, ezr)
    for k in range(first + 1, half):
        ring_step(k)
    for copy in relays:
        copy.wait_recv()

    near = pl.ds(0, 2 * hd)
    far = pl.ds(2 * hd, 3 * hd)
    per_core = nx // CORES

    def weight_part(columns):
        def part(at, h):
            return wall.at[at, pl.ds(c * per_core, per_core), pl.ds(h * half, half), :, columns]

        return part

    def weight_relay(at, index, columns, send, recv):
        block = wall.at[at, pl.ds(c * per_core, per_core), :, :, columns]
        return rcopy(block, block, send.at[index], recv.at[index], sibling)

    near_copies = y_copies(weight_part(near), ws, wr)
    near_relays = [weight_relay(at, i, near, wrs, wrr) for i, at in enumerate((ym, yp, yo))]
    far_copies = y_copies(weight_part(far), vs, vr)
    far_relays = [weight_relay(at, i, far, vrs, vrr) for i, at in enumerate((ym, yp, yo))]

    def relay_start(copies, relayed):
        copies[2].wait_recv()
        relayed[0].start()
        copies[3].wait_recv()
        relayed[1].start()
        copies[4].wait_recv()
        copies[5].wait_recv()
        relayed[2].start()

    y_start(near_copies)

    length = jnp.sum(jnp.where(iota((1, ndp), 1) == dp, len_ref[...], 0), axis=1, keepdims=True)
    live_total = jnp.sum(len_ref[...], axis=1, keepdims=True).astype(F32)
    index = iota((rows, 1), 0)
    w_head = wall[y, :, :, :, 2 * hd : 5 * hd].reshape(width, 3 * hd)
    kv_copies = []

    def alive_of(block):
        return jnp.where(index + block * rows < length, 1.0, 0.0)

    def block_span(block):
        return pl.ds(pl.multiple_of(block * rows, rows), rows)

    def project(at, order):
        projected = dot(xn[at], w_head)
        proj[at] = projected
        activated = projected * jax.nn.sigmoid(projected)
        value, key = activated[:, :hd], activated[:, hd : 2 * hd] * alive_of(CORES * at + c)
        query = activated[:, 2 * hd :]
        kv[CORES * at + c, :, :hd] = value.astype(BF16)
        kv[CORES * at + c, :, hd:] = key.astype(BF16)
        copy = rcopy(kv.at[CORES * at + c], kv.at[CORES * at + c], ks.at[order], kr.at[order], sibling)
        copy.start()
        kv_copies.append(copy)
        span = block_span(CORES * at + c)
        vt[:, span] = value.T.astype(BF16)
        kt[:, span] = key.T.astype(BF16)
        qs[block_span(at), :] = query.astype(BF16)
        qt[:, block_span(at)] = query.T.astype(BF16)

    project(y, 0)
    tok_copies[2].wait_recv()
    project(ym, 1)
    tok_copies[3].wait_recv()
    project(yp, 2)
    tok_copies[4].wait_recv()
    tok_copies[5].wait_recv()
    project(yo, 3)
    y_forward(near_copies)
    y_start(far_copies)
    for copy in kv_copies:
        copy.wait_recv()
    for u in range(HEADS):
        block = CORES * u + other
        both = kv[block].astype(F32)
        vt[:, block_span(block)] = both[:, :hd].T.astype(BF16)
        kt[:, block_span(block)] = both[:, hd:].T.astype(BF16)

    def send_when(t, src, dst, send, recv):
        @pl.when(y != t)
        def _():
            rcopy(src, dst, send.at[t], recv.at[y], (dp, t * CORES + c)).start()

        @pl.when(y == t)
        def _():
            dst[...] = src[...]

    def wait_when(t, ref, send, recv):
        @pl.when(y != t)
        def _():
            rcopy(ref, ref, send.at[t], recv.at[t], (dp, t * CORES + c)).wait_recv()

    def done_when(t, ref, send, recv):
        @pl.when(y != t)
        def _():
            rcopy(ref, ref, send.at[t], recv.at[t], (dp, t * CORES + c)).wait_send()

    causal = jnp.where(iota((rows, rows), 0) <= iota((rows, rows), 1), 1.0, 0.0)
    before = c.astype(F32)

    def weigh(block, low, high, mask):
        scores = dot(kv[block, :, hd:], qt[:, low:high]) * scale
        sigma = jax.nn.sigmoid(scores)
        weights = scores * sigma
        change = (sigma + weights * (1.0 - sigma)) * (scale / history)
        weights = weights * (1.0 / history)
        if mask is not None:
            weights, change = weights * mask, change * mask
        wst[block_span(block), low:high] = weights.astype(BF16)
        slope[block_span(block), low:high] = change

    queries = HEADS * rows
    for u in range(HEADS):
        low, high = u * rows, (u + 1) * rows
        for parity in range(2):
            block = CORES * u + (c if parity == 0 else other)
            weigh(block, low, high, causal if parity == 0 else before)
            if high < queries:
                weigh(block, high, queries, None)
        keys = CORES * (u + 1) * rows
        att_send[u] = dot(vt[:, :keys], wst[:keys, low:high]).T.astype(BF16)
        send_when(u, att_send.at[u], att_recv.at[y], as_, ar)

    relay_start(near_copies, near_relays)
    for copy in near_relays:
        copy.wait_recv()
    for t in range(HEADS):
        gproj[:, t * hd : (t + 1) * hd] = dot(xn[y], wall[t, :, :, :, hd : 2 * hd].reshape(width, hd))
    shard = TILE // 2
    line, spot = iota((hw, width), 0), iota((hw, width), 1)
    origin = lax.div(line, shard) * TILE + lax.rem(line, shard)
    for side in range(2):
        select = one_hot(spot == origin + side * shard)
        for t in range(HEADS):
            begin = side * (width // 2) + t * hd
            wout[:, begin : begin + hd] = dot(select, wall[t, :, :, :, :hd].reshape(width, hd)).astype(BF16)

    y_forward(far_copies)
    for copy in diff_z:
        copy.wait_recv()
    own_col = jnp.sum(
        jnp.where(iota((rows, ndp), 1) == lax.div(iota((rows, ndp), 0), cap), own_row, 0), axis=1, keepdims=True
    )
    received = drecv[...].reshape(ndp * TILE, quarter)
    hops = lax.rem(x - lax.div(own_col, NZ) + nx, nx)
    source = (hops * NZ + lax.rem(own_col, NZ)) * TILE + lax.rem(index, cap)
    for g in range(4):
        pick = one_hot(iota((rows, ndp * TILE), 1) == source + g * cap)
        idiff[:, g * quarter : (g + 1) * quarter] = dot(pick, received).astype(BF16)
    eye = iota((rows, rows), 0) == iota((rows, rows), 1)
    teacher = jnp.sum(jnp.where(eye, teach_ref[...], 0.0), axis=1, keepdims=True)
    alive = alive_of(sq)
    projected = gproj[...]
    gate = (projected * jax.nn.sigmoid(projected)).astype(BF16).astype(F32)
    gain_mid = gmid_ref[...]
    for t in range(HEADS):
        wait_when(t, att_recv.at[t], as_, ar)
    attended = jnp.concatenate([att_recv[t].astype(F32) for t in range(HEADS)], axis=1)
    normed_mid, factor_mid = normalize(attended)
    gated = (normed_mid * gain_mid * gate).astype(BF16)
    layer_out = (tok_ref[...].astype(F32) + dot(gated, wout[...])).astype(BF16).astype(F32)
    difference = idiff[...].astype(F32)
    errors = (jnp.sum(layer_out * difference, axis=1, keepdims=True) - teacher) * alive
    grad_out = (2.0 / live_total * errors * difference).astype(BF16)
    gout[...] = grad_out
    grad_gated = dot_nt(grad_out, wout[...])
    grad_normed = grad_gated * gain_mid * gate
    grad_attended = normalize_back(grad_normed, normed_mid, factor_mid).astype(BF16)
    for t in range(HEADS):
        da_send[t] = grad_attended[:, t * hd : (t + 1) * hd]
        send_when(t, da_send.at[t], da_recv.at[y], gs, gr)
    gpg[...] = (grad_gated * normed_mid * gain_mid * silu_slope(projected)).astype(BF16)

    def loss_send(buffer, place, send, recv, devices):
        copies = [
            rcopy(buffer.at[place], buffer.at[place], send.at[i], recv.at[i], device)
            for i, device in enumerate(devices)
        ]
        for copy in copies:
            copy.start()
        return copies

    lby[y] = jnp.broadcast_to(jnp.sum(errors * errors, axis=0, keepdims=True), (8, 128))
    loss_y = loss_send(lby, y, lys, lyr, [beside_y(d) for d in range(1, HEADS)])
    for t in range(HEADS):
        wait_when(t, da_recv.at[t], gs, gr)
    for t in range(HEADS):
        dat[:, t * rows : (t + 1) * rows] = da_recv[t].astype(F32).T.astype(BF16)

    def backward(u, parity):
        block = CORES * u + (c if parity == 0 else other)
        span, low = block_span(block), u * rows
        grad_weights = dot(kv[block, :, :hd], dat[:, low:])
        grad_scores = (grad_weights * slope[span, low:]).astype(BF16)
        dst[span, low:] = grad_scores
        grad_attended = da_recv[u:].reshape((HEADS - u) * rows, hd)
        grad_value = dot(wst[span, low:], grad_attended)
        grad_key = dot(grad_scores, qs[low:, :])
        return grad_value, grad_key

    part_copies = []
    for u in range(HEADS):
        grad_value, grad_key = backward(u, 1)
        dvk_send[u, :, :hd] = grad_value
        dvk_send[u, :, hd:] = grad_key
        copy = rcopy(dvk_send.at[u], dvk_recv.at[u], ps.at[u], pr.at[u], sibling)
        copy.start()
        part_copies.append(copy)
    relay_start(far_copies, far_relays)
    for copy in loss_y:
        copy.wait_recv()
    lbc[c] = jnp.sum(lby[...], axis=0)
    loss_c = loss_send(lbc, c, lcs, lcr, [sibling])
    for u in range(HEADS):
        grad_value, grad_key = backward(u, 0)
        part_copies[u].wait_recv()
        keep = alive_of(CORES * u + c)
        grad_value = (grad_value + dvk_recv[u, :, :hd]) * keep
        grad_key = (grad_key + dvk_recv[u, :, hd:]) * keep
        keys = CORES * (u + 1) * rows
        grad_query = dot(kt[:, :keys], dst[:keys, u * rows : (u + 1) * rows]).T
        gps[u, :, :hd] = (grad_value * silu_slope(proj[u, :, :hd])).astype(BF16)
        gps[u, :, hd : 2 * hd] = (grad_key * silu_slope(proj[u, :, hd : 2 * hd])).astype(BF16)
        gps[u, :, 2 * hd :] = (grad_query * silu_slope(proj[u, :, 2 * hd :])).astype(BF16)
        send_when(u, gps.at[u], gpr.at[y], fs, fr)
        if u == 0:
            loss_c[0].wait_recv()
            lbx[x] = jnp.sum(lbc[...], axis=0)
            loss_x = loss_send(lbx, x, lxs, lxr, [beside_x(d) for d in range(1, nx)])

    for copy in loss_x:
        copy.wait_recv()
    lbz[z] = jnp.sum(lbx[...], axis=0)
    loss_z = loss_send(lbz, z, lzs, lzr, [beside_z(d) for d in range(1, NZ)])

    for copy in far_relays:
        copy.wait_recv()
    grad_in = jnp.zeros((rows, width), F32)
    for t in range(HEADS):
        grad_in = grad_in + dot_nt(
            gpg[:, t * hd : (t + 1) * hd], wall[t, :, :, :, hd : 2 * hd].reshape(width, hd)
        )
    for t in range(HEADS):
        wait_when(t, gpr.at[t], fs, fr)
        grad_in = grad_in + dot_nt(gpr[t], wall[t, :, :, :, 2 * hd :].reshape(width, 3 * hd))
    normed_raw, factor_in = normalize(tok_ref[...].astype(F32))
    grad_norm = normalize_back(grad_in * gin_ref[...], normed_raw, factor_in)
    out_ref[...] = (gout[...].astype(F32) + grad_norm).astype(BF16)

    for copy in loss_z:
        copy.wait_recv()
    loss_ref[...] = jnp.sum(lbz[...], axis=0)[0:1, 0:1] / live_total

    for copy in x_copies + z_copies + relays + tok_copies + near_copies + near_relays + far_copies + far_relays:
        copy.wait_send()
    for copy in kv_copies + part_copies + loss_y + loss_c + loss_x + loss_z:
        copy.wait_send()
    for copy in request_x + request_z + diff_x + diff_z:
        copy.wait_send()
    for t in range(HEADS):
        done_when(t, att_send.at[t], as_, ar)
        done_when(t, da_send.at[t], gs, gr)
        done_when(t, gps.at[t], fs, fr)


def on_device(
    tokens, teacher, cand_items, owner_map, lengths, w_proj, w_out, gain_in, gain_mid, item_table
):
    rows, width = tokens.shape
    ndp = lax.axis_size("dp")
    nx = ndp // NZ
    hw = gain_mid.shape[0]
    hd = hw // HEADS
    blocks = HEADS * CORES
    half = NZ // 2
    quarter = width // 4

    vmem = pltpu.VMEM
    dma = pltpu.SemaphoreType.DMA
    scratch = [
        vmem((rows, width), BF16),
        vmem((1, rows), F32),
        vmem((2, rows), jnp.int32),
        vmem((1, ndp), jnp.int32),
        vmem((1, ndp), jnp.int32),
        vmem(w_out.shape, BF16),
        vmem((1, width), F32),
        vmem((1, hw), F32),
        vmem((HEADS, nx, NZ, TILE, 5 * hd), BF16),
        vmem((HEADS, rows, width), BF16),
        vmem(item_table.shape, BF16),
        vmem((nx, NZ, 1, 128), F32),
        vmem((nx, NZ, 1, 128), F32),
        vmem((nx, NZ, 1, 128), F32),
        vmem((ndp, 128), F32),
        vmem((nx, NZ, TILE, quarter), BF16),
        vmem((nx, NZ, TILE, quarter), BF16),
        vmem((nx, NZ, TILE, quarter), BF16),
        vmem((rows, width), BF16),
        vmem((HEADS, rows, 3 * hd), F32),
        vmem((blocks, rows, 2 * hd), BF16),
        vmem((hd, blocks * rows), BF16),
        vmem((hd, blocks * rows), BF16),
        vmem((HEADS * rows, hd), BF16),
        vmem((hd, HEADS * rows), BF16),
        vmem((blocks * rows, HEADS * rows), BF16),
        vmem((blocks * rows, HEADS * rows), F32),
        vmem((HEADS, rows, hd), BF16),
        vmem((HEADS, rows, hd), BF16),
        vmem((rows, hw), F32),
        vmem((hw, width), BF16),
        vmem((rows, width), BF16),
        vmem((rows, hw), BF16),
        vmem((HEADS, rows, hd), BF16),
        vmem((HEADS, rows, hd), BF16),
        vmem((hd, HEADS * rows), BF16),
        vmem((HEADS, rows, 2 * hd), F32),
        vmem((HEADS, rows, 2 * hd), F32),
        vmem((blocks * rows, HEADS * rows), BF16),
        vmem((HEADS, rows, 3 * hd), BF16),
        vmem((HEADS, rows, 3 * hd), BF16),
        vmem((HEADS, 8, 128), F32),
        vmem((CORES, 8, 128), F32),
        vmem((nx, 8, 128), F32),
        vmem((NZ, 8, 128), F32),
        dma((5,)),
        dma((8,)),
        dma((nx,)), dma((nx,)),
        dma((half,)), dma((half,)),
        dma((half,)), dma((half,)),
        dma((6,)), dma((6,)),
        dma((nx,)), dma((nx,)), dma((NZ,)), dma((NZ,)),
        dma((nx,)), dma((nx,)), dma((NZ,)), dma((NZ,)), dma((NZ,)), dma((NZ,)),
        dma((6,)), dma((6,)), dma((3,)), dma((3,)),
        dma((6,)), dma((6,)), dma((3,)), dma((3,)),
        dma((HEADS,)), dma((HEADS,)),
        dma((HEADS,)), dma((HEADS,)),
        dma((HEADS,)), dma((HEADS,)),
        dma((HEADS,)), dma((HEADS,)),
        dma((HEADS,)), dma((HEADS,)),
        dma((HEADS,)), dma((HEADS,)), dma((1,)), dma((1,)), dma((nx,)), dma((nx,)), dma((NZ,)), dma((NZ,)),
    ]
    whole = pl.BlockSpec(memory_space=pltpu.VMEM)
    anywhere = pl.BlockSpec(memory_space=pl.ANY)
    grads, loss = pl.pallas_call(
        kernel,
        out_shape=(jax.ShapeDtypeStruct(tokens.shape, BF16), jax.ShapeDtypeStruct((1, 1), F32)),
        in_specs=[anywhere] * 10,
        out_specs=(whole, whole),
        scratch_shapes=scratch,
        compiler_params=pltpu.CompilerParams(
            collective_id=0, has_side_effects=True, vmem_limit_bytes=56 * 1024 * 1024
        ),
    )(
        tokens,
        teacher.reshape(1, rows),
        cand_items.T,
        owner_map.reshape(1, ndp),
        lengths.reshape(1, ndp),
        w_proj,
        w_out,
        gain_in.reshape(1, width),
        gain_mid.reshape(1, hw),
        item_table,
    )
    return (grads, loss[0, 0])


def solution(mesh):
    in_specs = (
        P(("dp", "seq"), None),
        P(("dp", "seq")),
        P(("dp", "seq"), None),
        P(("dp", "seq")),
        P(),
        P("dp", None),
        P("dp", None),
        P(),
        P(),
        P("dp", None),
    )
    out_specs = (P(("dp", "seq"), None), P())
    return jax.shard_map(
        on_device, mesh=mesh, in_specs=in_specs, out_specs=out_specs, check_vma=False
    )
```

```python
import functools

import jax
import jax.numpy as jnp
from jax import lax
from jax.experimental import pallas as pl
from jax.experimental.pallas import tpu as pltpu
from jax.sharding import PartitionSpec as P

MESH = pl.DeviceIdType.MESH
F32 = jnp.float32
BF16 = jnp.bfloat16
HEADS = 4
NZ = 16
CORES = 2
TILE = 16
EPSILON = 1e-05


def dot(a, b):
    return jnp.dot(a, b, preferred_element_type=F32)


def dot_nt(a, b):
    return lax.dot_general(a, b, (((1,), (1,)), ((), ())), preferred_element_type=F32)


def iota(shape, axis):
    return lax.broadcasted_iota(jnp.int32, shape, axis)


def one_hot(condition):
    return jnp.where(condition, 1.0, 0.0).astype(BF16)


def silu_slope(inputs):
    sigma = jax.nn.sigmoid(inputs)
    return sigma * (1.0 + inputs * (1.0 - sigma))


def normalize(inputs):
    centered = inputs - jnp.mean(inputs, axis=-1, keepdims=True)
    factor = lax.rsqrt(jnp.mean(centered * centered, axis=-1, keepdims=True) + EPSILON)
    return (centered * factor, factor)


def normalize_back(upstream, normed, factor):
    inner = jnp.mean(upstream * normed, axis=-1, keepdims=True)
    return (upstream - jnp.mean(upstream, axis=-1, keepdims=True) - normed * inner) * factor


def small_parts(values):
    whole = values.astype(jnp.int32)
    return (whole >> 4).astype(F32).astype(BF16), (whole & 15).astype(F32).astype(BF16)


def kernel(
    tok_hbm, teach_hbm, cand_hbm, own_hbm, len_hbm, wp_ref, wo_hbm, gin_hbm, gmid_hbm, table_hbm,
    out_ref, loss_ref,
    tok_ref, teach_ref, cand_ref, own_ref, len_ref, wo_ref, gin_ref, gmid_ref,
    wall, piece, xn, table, req_send, req_mid, req_recv, rq, dsend, dmid, drecv, idiff, proj, kv, kt, vt, qs, qt, wst, slope,
    att_send, att_recv, gproj, wout, gout, gpg, da_send, da_recv, dat, dvk_send, dvk_recv, dst,
    gps, gpr, lby, lbc, lbx, lbz,
    lsem, isem, xs, xr, zs, zr, rs, rr, ts, tr, qxs, qxr, qzs, qzr, dxs, dxr, dzs, dzr,
    ws, wr, wrs, wrr, vs, vr, vrs, vrr, ks, kr, as_, ar, gs, gr, ps, pr, fs, fr, lys, lyr, lcs, lcr, lxs, lxr, lzs, lzr,
):
    rows, width = tok_ref.shape
    hd = kv.shape[2] // 2
    nx = req_send.shape[0]
    ndp = nx * NZ
    nseq = HEADS * CORES
    half = NZ // 2
    cap = rows // ndp
    quarter = width // 4
    history = rows * nseq
    scale = float(hd) ** -0.5

    dp = lax.axis_index("dp")
    sq = lax.axis_index("seq")
    x, z = lax.div(dp, NZ), lax.rem(dp, NZ)
    y, c = lax.div(sq, CORES), lax.rem(sq, CORES)
    other = 1 - c
    yp, ym = lax.rem(y + 1, HEADS), lax.rem(y + HEADS - 1, HEADS)
    yo = lax.rem(y + 2, HEADS)
    up, down = (dp, yp * CORES + c), (dp, ym * CORES + c)
    sibling = (dp, y * CORES + other)

    def rcopy(src, dst, send, recv, device):
        return pltpu.make_async_remote_copy(
            src_ref=src, dst_ref=dst, send_sem=send, recv_sem=recv, device_id=device, device_id_type=MESH
        )

    def beside_x(d):
        return (lax.rem(x + d, nx) * NZ + z, sq)

    def beside_z(d):
        return (x * NZ + lax.rem(z + d, NZ), sq)

    def beside_y(d):
        return (dp, lax.rem(y + d, HEADS) * CORES + c)

    barrier = pltpu.get_barrier_semaphore()
    partners = [sibling] + [beside_y(d) for d in range(1, HEADS)]
    partners += [beside_x(d) for d in range(1, nx)] + [beside_z(d) for d in range(1, NZ)]
    partners += [(device, y * CORES + other) for device, _ in [beside_z(d) for d in range(1, NZ)]]
    for device in partners:
        pl.semaphore_signal(barrier, inc=1, device_id=device, device_id_type=MESH)

    hw = HEADS * hd
    arguments = [
        (tok_hbm, tok_ref), (gin_hbm, gin_ref), (own_hbm, own_ref), (cand_hbm, cand_ref),
        (wo_hbm, wo_ref), (len_hbm, len_ref), (teach_hbm, teach_ref), (gmid_hbm, gmid_ref),
    ]
    inputs = [pltpu.make_async_copy(src, dst, isem.at[i]) for i, (src, dst) in enumerate(arguments)]
    pieces = [(0, hd), (hw, 2 * hd), (3 * hw, 3 * hd), (2 * hw, 4 * hd)]
    local = []
    for i, (start, to) in enumerate(pieces):
        begin = pl.multiple_of(start + y * hd, hd)
        local.append(
            pltpu.make_async_copy(wp_ref.at[:, pl.ds(begin, hd)], piece.at[:, pl.ds(to, hd)], lsem.at[i])
        )
    table_copy = pltpu.make_async_copy(table_hbm, table, lsem.at[4])
    for copy in inputs + local:
        copy.start()
    table_copy.start()
    for copy in inputs + local:
        copy.wait()
    sides = [wo_ref[:, pl.ds(pl.multiple_of(i * (width // 2) + y * hd, hd), hd)].astype(F32) for i in range(2)]
    piece[:, :hd] = jnp.concatenate(sides, axis=0).astype(BF16)

    @pl.when(c == lax.div(z, half))
    def _():
        wall[y, x, z] = piece[...]

    pl.semaphore_wait(barrier, len(partners))

    shard = wall.at[y, x, z]
    collector = y * CORES + lax.div(z, half)

    def shard_copy(i):
        device = (x * NZ + lax.rem(z + 1 + i + c * half, NZ), collector)
        return rcopy(piece, shard, zs.at[i], zr.at[lax.rem(z, half)], device)

    for i in range(half - 1):
        shard_copy(i).start()

    @pl.when(c == 0)
    def _():
        shard_copy(half - 1).start()

    own_row = own_ref[...]
    expand = one_hot(lax.div(iota((ndp, rows), 1), cap) == iota((ndp, rows), 0))
    own_rep = dot(jnp.broadcast_to(own_row.astype(F32).astype(BF16), (8, ndp)), expand)[0:1, :]
    to_owner = one_hot(iota((ndp, rows), 0).astype(F32) == own_rep)
    lane = iota((128, rows), 0)
    inside = (lax.div(lane, 2) == lax.rem(iota((128, rows), 1), cap)) & (lane < 2 * cap)
    both = jnp.where(lax.rem(lane, 2) == 0, cand_ref[0:1, :], cand_ref[1:2, :])
    high, low = small_parts(jnp.where(inside, both, 0))
    requests = dot_nt(to_owner, high) * 16.0 + dot_nt(to_owner, low)
    for p in range(ndp):
        req_send[p // NZ, p % NZ] = requests[p : p + 1, :]
    request_x = []
    for d in range(1, nx):
        block = req_send.at[lax.rem(x + d, nx)]
        request_x.append(rcopy(block, req_mid.at[x], qxs.at[d - 1], qxr.at[d - 1], beside_x(d)))
    for copy in request_x:
        copy.start()
    req_mid[x] = req_send[x]

    tokens = tok_ref[...].astype(F32)
    normed_raw, factor_in = normalize(tokens)
    xn[y] = (normed_raw * gin_ref[...]).astype(BF16)

    def y_copies(part, send, recv):
        return [
            rcopy(part(y, 0), part(y, 0), send.at[0], recv.at[0], up),
            rcopy(part(y, 1), part(y, 1), send.at[1], recv.at[1], down),
            rcopy(part(y, 1), part(y, 1), send.at[2], recv.at[2], up),
            rcopy(part(y, 0), part(y, 0), send.at[3], recv.at[3], down),
            rcopy(part(ym, 0), part(ym, 0), send.at[4], recv.at[4], up),
            rcopy(part(yp, 1), part(yp, 1), send.at[5], recv.at[5], down),
        ]

    def y_start(copies):
        for copy in copies[:4]:
            copy.start()

    def y_forward(copies):
        copies[0].wait_recv()
        copies[4].start()
        copies[1].wait_recv()
        copies[5].start()

    tok_copies = y_copies(lambda at, h: xn.at[at, pl.ds(h * (rows // 2), rows // 2), :], ts, tr)

    y_start(tok_copies)

    for copy in request_x:
        copy.wait_recv()
    request_z = []
    for d in range(1, NZ):
        block = req_mid.at[:, lax.rem(z + d, NZ)]
        request_z.append(rcopy(block, req_recv.at[:, z], qzs.at[d - 1], qzr.at[d - 1], beside_z(d)))
    for copy in request_z:
        copy.start()
    req_recv[:, z] = req_mid[:, z]

    def collected(d):
        return wall.at[y, lax.rem(x - d + nx, nx), pl.ds(c * half, half)]

    for j in range(half):

        @pl.when(z != c * half + j)
        def _():
            rcopy(shard, shard, zs.at[0], zr.at[j], sibling).wait_recv()

    x_copies = []
    for d in range(1, nx):
        x_copies.append(rcopy(collected(0), collected(0), xs.at[d - 1], xr.at[d - 1], beside_x(d)))
    relays = [rcopy(collected(d), collected(d), rs.at[d], rr.at[d], sibling) for d in range(nx)]
    for copy in x_copies:
        copy.start()
    relays[0].start()

    for copy in request_z:
        copy.wait_recv()
    for p in range(ndp):
        rq[p : p + 1, :] = req_recv[p // NZ, p % NZ]
    table_copy.wait()
    high, low = small_parts(rq[...])
    chunk = NZ * TILE
    row = iota((chunk, 128), 0)
    place = 2 * lax.rem(row, cap)
    lanes = iota((chunk, 128), 1)
    group = lax.div(lax.rem(iota((chunk, quarter), 0), TILE), cap)

    def differences(side):
        spread = one_hot(lax.div(iota((chunk, ndp), 0), TILE) + side * NZ == iota((chunk, ndp), 1))
        wanted = dot(spread, high) * 16.0 + dot(spread, low)
        first_item = jnp.sum(jnp.where(lanes == place, wanted, 0.0), axis=1, keepdims=True)
        second_item = jnp.sum(jnp.where(lanes == place + 1, wanted, 0.0), axis=1, keepdims=True)
        items = iota((chunk, table.shape[0]), 1).astype(F32)
        signs = jnp.where(items == first_item, 1.0, 0.0) - jnp.where(items == second_item, 1.0, 0.0)
        signs = signs.astype(BF16)
        total = jnp.zeros((chunk, quarter), F32)
        for g in range(4):
            term = dot(signs, table[:, g * quarter : (g + 1) * quarter])
            total = jnp.where(group == g, term, total)
        return total.astype(BF16).reshape(NZ, TILE, quarter)

    diff_x = []
    for d in range(1, nx):
        side = lax.rem(x + d, nx)
        dsend[side] = differences(side)
        copy = rcopy(dsend.at[side], dmid.at[d], dxs.at[d - 1], dxr.at[d - 1], beside_x(d))
        copy.start()
        diff_x.append(copy)
    dmid[0] = differences(x)
    for d in range(1, nx):
        x_copies[d - 1].wait_recv()
        relays[d].start()

    for copy in diff_x:
        copy.wait_recv()
    diff_z = []
    for d in range(1, NZ):
        block = dmid.at[:, lax.rem(z + d, NZ)]
        diff_z.append(rcopy(block, drecv.at[:, z], dzs.at[d - 1], dzr.at[d - 1], beside_z(d)))
    for copy in diff_z:
        copy.start()
    drecv[:, z] = dmid[:, z]
    y_forward(tok_copies)
    for copy in relays:
        copy.wait_recv()

    near = pl.ds(0, 2 * hd)
    far = pl.ds(2 * hd, 3 * hd)
    per_core = nx // CORES

    def weight_part(columns):
        def part(at, h):
            return wall.at[at, pl.ds(c * per_core, per_core), pl.ds(h * half, half), :, columns]

        return part

    def weight_relay(at, index, columns, send, recv):
        block = wall.at[at, pl.ds(c * per_core, per_core), :, :, columns]
        return rcopy(block, block, send.at[index], recv.at[index], sibling)

    near_copies = y_copies(weight_part(near), ws, wr)
    near_relays = [weight_relay(at, i, near, wrs, wrr) for i, at in enumerate((ym, yp, yo))]
    far_copies = y_copies(weight_part(far), vs, vr)
    far_relays = [weight_relay(at, i, far, vrs, vrr) for i, at in enumerate((ym, yp, yo))]

    def relay_start(copies, relayed):
        copies[2].wait_recv()
        relayed[0].start()
        copies[3].wait_recv()
        relayed[1].start()
        copies[4].wait_recv()
        copies[5].wait_recv()
        relayed[2].start()

    y_start(near_copies)

    length = jnp.sum(jnp.where(iota((1, ndp), 1) == dp, len_ref[...], 0), axis=1, keepdims=True)
    live_total = jnp.sum(len_ref[...], axis=1, keepdims=True).astype(F32)
    index = iota((rows, 1), 0)
    w_head = wall[y, :, :, :, 2 * hd : 5 * hd].reshape(width, 3 * hd)
    kv_copies = []

    def alive_of(block):
        return jnp.where(index + block * rows < length, 1.0, 0.0)

    def block_span(block):
        return pl.ds(pl.multiple_of(block * rows, rows), rows)

    def project(at, order):
        projected = dot(xn[at], w_head)
        proj[at] = projected
        activated = projected * jax.nn.sigmoid(projected)
        value, key = activated[:, :hd], activated[:, hd : 2 * hd] * alive_of(CORES * at + c)
        query = activated[:, 2 * hd :]
        kv[CORES * at + c, :, :hd] = value.astype(BF16)
        kv[CORES * at + c, :, hd:] = key.astype(BF16)
        copy = rcopy(kv.at[CORES * at + c], kv.at[CORES * at + c], ks.at[order], kr.at[order], sibling)
        copy.start()
        kv_copies.append(copy)
        span = block_span(CORES * at + c)
        vt[:, span] = value.T.astype(BF16)
        kt[:, span] = key.T.astype(BF16)
        qs[block_span(at), :] = query.astype(BF16)
        qt[:, block_span(at)] = query.T.astype(BF16)

    project(y, 0)
    tok_copies[2].wait_recv()
    project(ym, 1)
    tok_copies[3].wait_recv()
    project(yp, 2)
    tok_copies[4].wait_recv()
    tok_copies[5].wait_recv()
    project(yo, 3)
    y_forward(near_copies)
    y_start(far_copies)
    for copy in kv_copies:
        copy.wait_recv()
    for u in range(HEADS):
        block = CORES * u + other
        both = kv[block].astype(F32)
        vt[:, block_span(block)] = both[:, :hd].T.astype(BF16)
        kt[:, block_span(block)] = both[:, hd:].T.astype(BF16)

    def send_when(t, src, dst, send, recv):
        @pl.when(y != t)
        def _():
            rcopy(src, dst, send.at[t], recv.at[y], (dp, t * CORES + c)).start()

        @pl.when(y == t)
        def _():
            dst[...] = src[...]

    def wait_when(t, ref, send, recv):
        @pl.when(y != t)
        def _():
            rcopy(ref, ref, send.at[t], recv.at[t], (dp, t * CORES + c)).wait_recv()

    def done_when(t, ref, send, recv):
        @pl.when(y != t)
        def _():
            rcopy(ref, ref, send.at[t], recv.at[t], (dp, t * CORES + c)).wait_send()

    causal = jnp.where(iota((rows, rows), 0) <= iota((rows, rows), 1), 1.0, 0.0)
    before = c.astype(F32)

    def weigh(block, low, high, mask):
        scores = dot(kv[block, :, hd:], qt[:, low:high]) * scale
        sigma = jax.nn.sigmoid(scores)
        weights = scores * sigma
        change = (sigma + weights * (1.0 - sigma)) * (scale / history)
        weights = weights * (1.0 / history)
        if mask is not None:
            weights, change = weights * mask, change * mask
        wst[block_span(block), low:high] = weights.astype(BF16)
        slope[block_span(block), low:high] = change

    queries = HEADS * rows
    for u in range(HEADS):
        low, high = u * rows, (u + 1) * rows
        for parity in range(2):
            block = CORES * u + (c if parity == 0 else other)
            weigh(block, low, high, causal if parity == 0 else before)
            if high < queries:
                weigh(block, high, queries, None)
        keys = CORES * (u + 1) * rows
        att_send[u] = dot(vt[:, :keys], wst[:keys, low:high]).T.astype(BF16)
        send_when(u, att_send.at[u], att_recv.at[y], as_, ar)

    relay_start(near_copies, near_relays)
    for copy in near_relays:
        copy.wait_recv()
    for t in range(HEADS):
        gproj[:, t * hd : (t + 1) * hd] = dot(xn[y], wall[t, :, :, :, hd : 2 * hd].reshape(width, hd))
    lines = TILE // 2
    line, spot = iota((hw, width), 0), iota((hw, width), 1)
    origin = lax.div(line, lines) * TILE + lax.rem(line, lines)
    for side in range(2):
        select = one_hot(spot == origin + side * lines)
        for t in range(HEADS):
            begin = side * (width // 2) + t * hd
            wout[:, begin : begin + hd] = dot(select, wall[t, :, :, :, :hd].reshape(width, hd)).astype(BF16)

    y_forward(far_copies)
    for copy in diff_z:
        copy.wait_recv()
    own_col = jnp.sum(
        jnp.where(iota((rows, ndp), 1) == lax.div(iota((rows, ndp), 0), cap), own_row, 0), axis=1, keepdims=True
    )
    received = drecv[...].reshape(ndp * TILE, quarter)
    hops = lax.rem(x - lax.div(own_col, NZ) + nx, nx)
    source = (hops * NZ + lax.rem(own_col, NZ)) * TILE + lax.rem(index, cap)
    for g in range(4):
        pick = one_hot(iota((rows, ndp * TILE), 1) == source + g * cap)
        idiff[:, g * quarter : (g + 1) * quarter] = dot(pick, received).astype(BF16)
    eye = iota((rows, rows), 0) == iota((rows, rows), 1)
    teacher = jnp.sum(jnp.where(eye, teach_ref[...], 0.0), axis=1, keepdims=True)
    alive = alive_of(sq)
    projected = gproj[...]
    gate = (projected * jax.nn.sigmoid(projected)).astype(BF16).astype(F32)
    gain_mid = gmid_ref[...]
    for t in range(HEADS):
        wait_when(t, att_recv.at[t], as_, ar)
    attended = jnp.concatenate([att_recv[t].astype(F32) for t in range(HEADS)], axis=1)
    normed_mid, factor_mid = normalize(attended)
    gated = (normed_mid * gain_mid * gate).astype(BF16)
    layer_out = (tok_ref[...].astype(F32) + dot(gated, wout[...])).astype(BF16).astype(F32)
    difference = idiff[...].astype(F32)
    errors = (jnp.sum(layer_out * difference, axis=1, keepdims=True) - teacher) * alive
    grad_out = (2.0 / live_total * errors * difference).astype(BF16)
    gout[...] = grad_out
    grad_gated = dot_nt(grad_out, wout[...])
    grad_normed = grad_gated * gain_mid * gate
    grad_attended = normalize_back(grad_normed, normed_mid, factor_mid).astype(BF16)
    for t in range(HEADS):
        da_send[t] = grad_attended[:, t * hd : (t + 1) * hd]
        send_when(t, da_send.at[t], da_recv.at[y], gs, gr)
    gpg[...] = (grad_gated * normed_mid * gain_mid * silu_slope(projected)).astype(BF16)

    def loss_send(buffer, place, send, recv, devices):
        copies = [
            rcopy(buffer.at[place], buffer.at[place], send.at[i], recv.at[i], device)
            for i, device in enumerate(devices)
        ]
        for copy in copies:
            copy.start()
        return copies

    lby[y] = jnp.broadcast_to(jnp.sum(errors * errors, axis=0, keepdims=True), (8, 128))
    loss_y = loss_send(lby, y, lys, lyr, [beside_y(d) for d in range(1, HEADS)])
    for t in range(HEADS):
        wait_when(t, da_recv.at[t], gs, gr)
    for t in range(HEADS):
        dat[:, t * rows : (t + 1) * rows] = da_recv[t].astype(F32).T.astype(BF16)

    def backward(u, parity):
        block = CORES * u + (c if parity == 0 else other)
        span, low = block_span(block), u * rows
        grad_weights = dot(kv[block, :, :hd], dat[:, low:])
        grad_scores = (grad_weights * slope[span, low:]).astype(BF16)
        dst[span, low:] = grad_scores
        grad_attended = da_recv[u:].reshape((HEADS - u) * rows, hd)
        grad_value = dot(wst[span, low:], grad_attended)
        grad_key = dot(grad_scores, qs[low:, :])
        return grad_value, grad_key

    part_copies = []
    for u in range(HEADS):
        grad_value, grad_key = backward(u, 1)
        dvk_send[u, :, :hd] = grad_value
        dvk_send[u, :, hd:] = grad_key
        copy = rcopy(dvk_send.at[u], dvk_recv.at[u], ps.at[u], pr.at[u], sibling)
        copy.start()
        part_copies.append(copy)
    relay_start(far_copies, far_relays)
    for copy in loss_y:
        copy.wait_recv()
    lbc[c] = jnp.sum(lby[...], axis=0)
    loss_c = loss_send(lbc, c, lcs, lcr, [sibling])
    for u in range(HEADS):
        grad_value, grad_key = backward(u, 0)
        part_copies[u].wait_recv()
        keep = alive_of(CORES * u + c)
        grad_value = (grad_value + dvk_recv[u, :, :hd]) * keep
        grad_key = (grad_key + dvk_recv[u, :, hd:]) * keep
        keys = CORES * (u + 1) * rows
        grad_query = dot(kt[:, :keys], dst[:keys, u * rows : (u + 1) * rows]).T
        gps[u, :, :hd] = (grad_value * silu_slope(proj[u, :, :hd])).astype(BF16)
        gps[u, :, hd : 2 * hd] = (grad_key * silu_slope(proj[u, :, hd : 2 * hd])).astype(BF16)
        gps[u, :, 2 * hd :] = (grad_query * silu_slope(proj[u, :, 2 * hd :])).astype(BF16)
        send_when(u, gps.at[u], gpr.at[y], fs, fr)
        if u == 0:
            loss_c[0].wait_recv()
            lbx[x] = jnp.sum(lbc[...], axis=0)
            loss_x = loss_send(lbx, x, lxs, lxr, [beside_x(d) for d in range(1, nx)])

    for copy in loss_x:
        copy.wait_recv()
    lbz[z] = jnp.sum(lbx[...], axis=0)
    loss_z = loss_send(lbz, z, lzs, lzr, [beside_z(d) for d in range(1, NZ)])

    for copy in far_relays:
        copy.wait_recv()
    grad_in = jnp.zeros((rows, width), F32)
    for t in range(HEADS):
        grad_in = grad_in + dot_nt(
            gpg[:, t * hd : (t + 1) * hd], wall[t, :, :, :, hd : 2 * hd].reshape(width, hd)
        )
    for t in range(HEADS):
        wait_when(t, gpr.at[t], fs, fr)
        grad_in = grad_in + dot_nt(gpr[t], wall[t, :, :, :, 2 * hd :].reshape(width, 3 * hd))
    normed_raw, factor_in = normalize(tok_ref[...].astype(F32))
    grad_norm = normalize_back(grad_in * gin_ref[...], normed_raw, factor_in)
    out_ref[...] = (gout[...].astype(F32) + grad_norm).astype(BF16)

    for copy in loss_z:
        copy.wait_recv()
    loss_ref[...] = jnp.sum(lbz[...], axis=0)[0:1, 0:1] / live_total

    for i in range(half - 1):
        shard_copy(i).wait_send()

    @pl.when(c == 0)
    def _():
        shard_copy(half - 1).wait_send()

    for copy in x_copies + relays + tok_copies + near_copies + near_relays + far_copies + far_relays:
        copy.wait_send()
    for copy in kv_copies + part_copies + loss_y + loss_c + loss_x + loss_z:
        copy.wait_send()
    for copy in request_x + request_z + diff_x + diff_z:
        copy.wait_send()
    for t in range(HEADS):
        done_when(t, att_send.at[t], as_, ar)
        done_when(t, da_send.at[t], gs, gr)
        done_when(t, gps.at[t], fs, fr)


def on_device(
    tokens, teacher, cand_items, owner_map, lengths, w_proj, w_out, gain_in, gain_mid, item_table
):
    rows, width = tokens.shape
    ndp = lax.axis_size("dp")
    nx = ndp // NZ
    hw = gain_mid.shape[0]
    hd = hw // HEADS
    blocks = HEADS * CORES
    half = NZ // 2
    quarter = width // 4

    vmem = pltpu.VMEM
    dma = pltpu.SemaphoreType.DMA
    scratch = [
        vmem((rows, width), BF16),
        vmem((1, rows), F32),
        vmem((2, rows), jnp.int32),
        vmem((1, ndp), jnp.int32),
        vmem((1, ndp), jnp.int32),
        vmem(w_out.shape, BF16),
        vmem((1, width), F32),
        vmem((1, hw), F32),
        vmem((HEADS, nx, NZ, TILE, 5 * hd), BF16),
        vmem((TILE, 5 * hd), BF16),
        vmem((HEADS, rows, width), BF16),
        vmem(item_table.shape, BF16),
        vmem((nx, NZ, 1, 128), F32),
        vmem((nx, NZ, 1, 128), F32),
        vmem((nx, NZ, 1, 128), F32),
        vmem((ndp, 128), F32),
        vmem((nx, NZ, TILE, quarter), BF16),
        vmem((nx, NZ, TILE, quarter), BF16),
        vmem((nx, NZ, TILE, quarter), BF16),
        vmem((rows, width), BF16),
        vmem((HEADS, rows, 3 * hd), F32),
        vmem((blocks, rows, 2 * hd), BF16),
        vmem((hd, blocks * rows), BF16),
        vmem((hd, blocks * rows), BF16),
        vmem((HEADS * rows, hd), BF16),
        vmem((hd, HEADS * rows), BF16),
        vmem((blocks * rows, HEADS * rows), BF16),
        vmem((blocks * rows, HEADS * rows), F32),
        vmem((HEADS, rows, hd), BF16),
        vmem((HEADS, rows, hd), BF16),
        vmem((rows, hw), F32),
        vmem((hw, width), BF16),
        vmem((rows, width), BF16),
        vmem((rows, hw), BF16),
        vmem((HEADS, rows, hd), BF16),
        vmem((HEADS, rows, hd), BF16),
        vmem((hd, HEADS * rows), BF16),
        vmem((HEADS, rows, 2 * hd), F32),
        vmem((HEADS, rows, 2 * hd), F32),
        vmem((blocks * rows, HEADS * rows), BF16),
        vmem((HEADS, rows, 3 * hd), BF16),
        vmem((HEADS, rows, 3 * hd), BF16),
        vmem((HEADS, 8, 128), F32),
        vmem((CORES, 8, 128), F32),
        vmem((nx, 8, 128), F32),
        vmem((NZ, 8, 128), F32),
        dma((5,)),
        dma((8,)),
        dma((nx,)), dma((nx,)),
        dma((half,)), dma((half,)),
        dma((nx,)), dma((nx,)),
        dma((6,)), dma((6,)),
        dma((nx,)), dma((nx,)), dma((NZ,)), dma((NZ,)),
        dma((nx,)), dma((nx,)), dma((NZ,)), dma((NZ,)),
        dma((6,)), dma((6,)), dma((3,)), dma((3,)),
        dma((6,)), dma((6,)), dma((3,)), dma((3,)),
        dma((HEADS,)), dma((HEADS,)),
        dma((HEADS,)), dma((HEADS,)),
        dma((HEADS,)), dma((HEADS,)),
        dma((HEADS,)), dma((HEADS,)),
        dma((HEADS,)), dma((HEADS,)),
        dma((HEADS,)), dma((HEADS,)), dma((1,)), dma((1,)), dma((nx,)), dma((nx,)), dma((NZ,)), dma((NZ,)),
    ]
    whole = pl.BlockSpec(memory_space=pltpu.VMEM)
    anywhere = pl.BlockSpec(memory_space=pl.ANY)
    grads, loss = pl.pallas_call(
        kernel,
        out_shape=(jax.ShapeDtypeStruct(tokens.shape, BF16), jax.ShapeDtypeStruct((1, 1), F32)),
        in_specs=[anywhere] * 10,
        out_specs=(whole, whole),
        scratch_shapes=scratch,
        compiler_params=pltpu.CompilerParams(
            collective_id=0, has_side_effects=True, vmem_limit_bytes=56 * 1024 * 1024
        ),
    )(
        tokens,
        teacher.reshape(1, rows),
        cand_items.T,
        owner_map.reshape(1, ndp),
        lengths.reshape(1, ndp),
        w_proj,
        w_out,
        gain_in.reshape(1, width),
        gain_mid.reshape(1, hw),
        item_table,
    )
    return (grads, loss[0, 0])


def solution(mesh):
    in_specs = (
        P(("dp", "seq"), None),
        P(("dp", "seq")),
        P(("dp", "seq"), None),
        P(("dp", "seq")),
        P(),
        P("dp", None),
        P("dp", None),
        P(),
        P(),
        P("dp", None),
    )
    out_specs = (P(("dp", "seq"), None), P())
    return jax.shard_map(
        on_device, mesh=mesh, in_specs=in_specs, out_specs=out_specs, check_vma=False
    )
```

```python
import functools

import jax
import jax.numpy as jnp
from jax import lax
from jax.experimental import pallas as pl
from jax.experimental.pallas import tpu as pltpu
from jax.sharding import PartitionSpec as P

MESH = pl.DeviceIdType.MESH
F32 = jnp.float32
BF16 = jnp.bfloat16
HEADS = 4
NZ = 16
CORES = 2
TILE = 16
EPSILON = 1e-05


def dot(a, b):
    return jnp.dot(a, b, preferred_element_type=F32)


def dot_nt(a, b):
    return lax.dot_general(a, b, (((1,), (1,)), ((), ())), preferred_element_type=F32)


def iota(shape, axis):
    return lax.broadcasted_iota(jnp.int32, shape, axis)


def one_hot(condition):
    return jnp.where(condition, 1.0, 0.0).astype(BF16)


def silu_slope(inputs):
    sigma = jax.nn.sigmoid(inputs)
    return sigma * (1.0 + inputs * (1.0 - sigma))


def normalize(inputs):
    centered = inputs - jnp.mean(inputs, axis=-1, keepdims=True)
    factor = lax.rsqrt(jnp.mean(centered * centered, axis=-1, keepdims=True) + EPSILON)
    return (centered * factor, factor)


def normalize_back(upstream, normed, factor):
    inner = jnp.mean(upstream * normed, axis=-1, keepdims=True)
    return (upstream - jnp.mean(upstream, axis=-1, keepdims=True) - normed * inner) * factor


def small_parts(values):
    whole = values.astype(jnp.int32)
    return (whole >> 4).astype(F32).astype(BF16), (whole & 15).astype(F32).astype(BF16)


def kernel(
    tok_hbm, teach_hbm, cand_hbm, own_hbm, len_hbm, wp_ref, wo_hbm, gin_hbm, gmid_hbm, table_hbm,
    out_ref, loss_ref,
    tok_ref, teach_ref, cand_ref, own_ref, len_ref, wo_ref, gin_ref, gmid_ref,
    wall, piece, xn, table, req_send, req_mid, req_recv, rq, dsend, dmid, drecv, picks, idiff, proj, kv, kt, vt, qs, qt, wst, slope,
    att_send, att_recv, gproj, wout, gout, gpg, da_send, da_recv, dat, dvk_send, dvk_recv, dst,
    gps, gpr, lby, lbc, lbx, lbz,
    lsem, isem, xs, xr, zs, zr, rs, rr, ts, tr, qxs, qxr, qzs, qzr, dxs, dxr, dzs, dzr,
    ws, wr, wrs, wrr, vs, vr, vrs, vrr, ks, kr, as_, ar, gs, gr, ps, pr, fs, fr, lys, lyr, lcs, lcr, lxs, lxr, lzs, lzr,
):
    rows, width = tok_ref.shape
    hd = kv.shape[2] // 2
    nx = req_send.shape[0]
    ndp = nx * NZ
    nseq = HEADS * CORES
    half = NZ // 2
    cap = rows // ndp
    quarter = width // 4
    history = rows * nseq
    scale = float(hd) ** -0.5

    dp = lax.axis_index("dp")
    sq = lax.axis_index("seq")
    x, z = lax.div(dp, NZ), lax.rem(dp, NZ)
    y, c = lax.div(sq, CORES), lax.rem(sq, CORES)
    other = 1 - c
    yp, ym = lax.rem(y + 1, HEADS), lax.rem(y + HEADS - 1, HEADS)
    yo = lax.rem(y + 2, HEADS)
    up, down = (dp, yp * CORES + c), (dp, ym * CORES + c)
    sibling = (dp, y * CORES + other)

    def rcopy(src, dst, send, recv, device):
        return pltpu.make_async_remote_copy(
            src_ref=src, dst_ref=dst, send_sem=send, recv_sem=recv, device_id=device, device_id_type=MESH
        )

    def beside_x(d):
        return (lax.rem(x + d, nx) * NZ + z, sq)

    def beside_z(d):
        return (x * NZ + lax.rem(z + d, NZ), sq)

    def beside_y(d):
        return (dp, lax.rem(y + d, HEADS) * CORES + c)

    barrier = pltpu.get_barrier_semaphore()
    partners = [sibling] + [beside_y(d) for d in range(1, HEADS)]
    partners += [beside_x(d) for d in range(1, nx)] + [beside_z(d) for d in range(1, NZ)]
    partners += [(device, y * CORES + other) for device, _ in [beside_z(d) for d in range(1, NZ)]]
    for device in partners:
        pl.semaphore_signal(barrier, inc=1, device_id=device, device_id_type=MESH)

    hw = HEADS * hd
    arguments = [
        (tok_hbm, tok_ref), (gin_hbm, gin_ref), (own_hbm, own_ref), (cand_hbm, cand_ref),
        (wo_hbm, wo_ref), (len_hbm, len_ref), (teach_hbm, teach_ref), (gmid_hbm, gmid_ref),
    ]
    inputs = [pltpu.make_async_copy(src, dst, isem.at[i]) for i, (src, dst) in enumerate(arguments)]
    pieces = [(0, hd), (hw, 2 * hd), (3 * hw, 3 * hd), (2 * hw, 4 * hd)]
    local = []
    for i, (start, to) in enumerate(pieces):
        begin = pl.multiple_of(start + y * hd, hd)
        local.append(
            pltpu.make_async_copy(wp_ref.at[:, pl.ds(begin, hd)], piece.at[:, pl.ds(to, hd)], lsem.at[i])
        )
    table_copy = pltpu.make_async_copy(table_hbm, table, lsem.at[4])
    for copy in inputs + local:
        copy.start()
    table_copy.start()
    for copy in inputs + local:
        copy.wait()
    sides = [wo_ref[:, pl.ds(pl.multiple_of(i * (width // 2) + y * hd, hd), hd)].astype(F32) for i in range(2)]
    piece[:, :hd] = jnp.concatenate(sides, axis=0).astype(BF16)

    @pl.when(c == lax.div(z, half))
    def _():
        wall[y, x, z] = piece[...]

    pl.semaphore_wait(barrier, len(partners))

    shard = wall.at[y, x, z]
    collector = y * CORES + lax.div(z, half)

    def shard_copy(i):
        device = (x * NZ + lax.rem(z + 1 + i + c * half, NZ), collector)
        return rcopy(piece, shard, zs.at[i], zr.at[lax.rem(z, half)], device)

    for i in range(half - 1):
        shard_copy(i).start()

    @pl.when(c == 0)
    def _():
        shard_copy(half - 1).start()

    own_row = own_ref[...]
    expand = one_hot(lax.div(iota((ndp, rows), 1), cap) == iota((ndp, rows), 0))
    own_rep = dot(jnp.broadcast_to(own_row.astype(F32).astype(BF16), (8, ndp)), expand)[0:1, :]
    to_owner = one_hot(iota((ndp, rows), 0).astype(F32) == own_rep)
    lane = iota((128, rows), 0)
    inside = (lax.div(lane, 2) == lax.rem(iota((128, rows), 1), cap)) & (lane < 2 * cap)
    both = jnp.where(lax.rem(lane, 2) == 0, cand_ref[0:1, :], cand_ref[1:2, :])
    high, low = small_parts(jnp.where(inside, both, 0))
    requests = dot_nt(to_owner, high) * 16.0 + dot_nt(to_owner, low)
    for p in range(ndp):
        req_send[p // NZ, p % NZ] = requests[p : p + 1, :]
    request_x = []
    for d in range(1, nx):
        block = req_send.at[lax.rem(x + d, nx)]
        request_x.append(rcopy(block, req_mid.at[x], qxs.at[d - 1], qxr.at[d - 1], beside_x(d)))
    for copy in request_x:
        copy.start()
    req_mid[x] = req_send[x]

    tokens = tok_ref[...].astype(F32)
    normed_raw, factor_in = normalize(tokens)
    xn[y] = (normed_raw * gin_ref[...]).astype(BF16)

    def y_copies(part, send, recv):
        return [
            rcopy(part(y, 0), part(y, 0), send.at[0], recv.at[0], up),
            rcopy(part(y, 1), part(y, 1), send.at[1], recv.at[1], down),
            rcopy(part(y, 1), part(y, 1), send.at[2], recv.at[2], up),
            rcopy(part(y, 0), part(y, 0), send.at[3], recv.at[3], down),
            rcopy(part(ym, 0), part(ym, 0), send.at[4], recv.at[4], up),
            rcopy(part(yp, 1), part(yp, 1), send.at[5], recv.at[5], down),
        ]

    def y_start(copies):
        for copy in copies[:4]:
            copy.start()

    def y_forward(copies):
        copies[0].wait_recv()
        copies[4].start()
        copies[1].wait_recv()
        copies[5].start()

    tok_copies = y_copies(lambda at, h: xn.at[at, pl.ds(h * (rows // 2), rows // 2), :], ts, tr)

    y_start(tok_copies)

    for copy in request_x:
        copy.wait_recv()
    request_z = []
    for d in range(1, NZ):
        block = req_mid.at[:, lax.rem(z + d, NZ)]
        request_z.append(rcopy(block, req_recv.at[:, z], qzs.at[d - 1], qzr.at[d - 1], beside_z(d)))
    for copy in request_z:
        copy.start()
    req_recv[:, z] = req_mid[:, z]

    def collected(d):
        return wall.at[y, lax.rem(x - d + nx, nx), pl.ds(c * half, half)]

    for j in range(half):

        @pl.when(z != c * half + j)
        def _():
            rcopy(shard, shard, zs.at[0], zr.at[j], sibling).wait_recv()

    x_copies = []
    for d in range(1, nx):
        x_copies.append(rcopy(collected(0), collected(0), xs.at[d - 1], xr.at[d - 1], beside_x(d)))
    relays = [rcopy(collected(d), collected(d), rs.at[d], rr.at[d], sibling) for d in range(nx)]
    for copy in x_copies:
        copy.start()
    relays[0].start()

    for copy in request_z:
        copy.wait_recv()
    for p in range(ndp):
        rq[p : p + 1, :] = req_recv[p // NZ, p % NZ]
    table_copy.wait()
    high, low = small_parts(rq[...])
    chunk = NZ * TILE
    row = iota((chunk, 128), 0)
    place = 2 * lax.rem(row, cap)
    lanes = iota((chunk, 128), 1)
    group = lax.div(lax.rem(iota((chunk, quarter), 0), TILE), cap)

    def differences(side):
        spread = one_hot(lax.div(iota((chunk, ndp), 0), TILE) + side * NZ == iota((chunk, ndp), 1))
        wanted = dot(spread, high) * 16.0 + dot(spread, low)
        first_item = jnp.sum(jnp.where(lanes == place, wanted, 0.0), axis=1, keepdims=True)
        second_item = jnp.sum(jnp.where(lanes == place + 1, wanted, 0.0), axis=1, keepdims=True)
        items = iota((chunk, table.shape[0]), 1).astype(F32)
        signs = jnp.where(items == first_item, 1.0, 0.0) - jnp.where(items == second_item, 1.0, 0.0)
        signs = signs.astype(BF16)
        total = jnp.zeros((chunk, quarter), F32)
        for g in range(4):
            term = dot(signs, table[:, g * quarter : (g + 1) * quarter])
            total = jnp.where(group == g, term, total)
        return total.astype(BF16).reshape(NZ, TILE, quarter)

    hops = [0, 1] + [nx - 1] * (nx > 2) + list(range(2, nx - 1))
    rounds = [(0, 1), (1, min(3, nx))] + [(3, nx)] * (nx > 3)
    diff_z = []

    def along_z(i):
        low, high = rounds[i]
        slots = pl.ds(low, high - low)
        copies = []
        for d in range(1, NZ):
            block = dmid.at[slots, lax.rem(z + d, NZ)]
            copies.append(rcopy(block, drecv.at[slots, z], dzs.at[i, d - 1], dzr.at[i, d - 1], beside_z(d)))
        for copy in copies:
            copy.start()
        drecv[slots, z] = dmid[slots, z]
        diff_z.extend(copies)

    dmid[0] = differences(x)
    along_z(0)
    diff_x = []
    for slot in range(1, nx):
        d = hops[slot]
        side = lax.rem(x + d, nx)
        dsend[side] = differences(side)
        copy = rcopy(dsend.at[side], dmid.at[slot], dxs.at[slot - 1], dxr.at[slot - 1], beside_x(d))
        copy.start()
        diff_x.append(copy)
        if slot == 1:
            y_forward(tok_copies)

    for d in range(1, nx):
        if d < len(rounds):
            for slot in range(*rounds[d]):
                diff_x[slot - 1].wait_recv()
            along_z(d)
        x_copies[hops[d] - 1].wait_recv()
        relays[hops[d]].start()
    for copy in relays:
        copy.wait_recv()

    near = pl.ds(0, 2 * hd)
    far = pl.ds(2 * hd, 3 * hd)
    per_core = nx // CORES

    def weight_part(columns):
        def part(at, h):
            return wall.at[at, pl.ds(c * per_core, per_core), pl.ds(h * half, half), :, columns]

        return part

    def weight_relay(at, index, columns, send, recv):
        block = wall.at[at, pl.ds(c * per_core, per_core), :, :, columns]
        return rcopy(block, block, send.at[index], recv.at[index], sibling)

    near_copies = y_copies(weight_part(near), ws, wr)
    near_relays = [weight_relay(at, i, near, wrs, wrr) for i, at in enumerate((ym, yp, yo))]
    far_copies = y_copies(weight_part(far), vs, vr)
    far_relays = [weight_relay(at, i, far, vrs, vrr) for i, at in enumerate((ym, yp, yo))]

    def relay_start(copies, relayed):
        copies[2].wait_recv()
        relayed[0].start()
        copies[3].wait_recv()
        relayed[1].start()
        copies[4].wait_recv()
        copies[5].wait_recv()
        relayed[2].start()

    y_start(near_copies)

    length = jnp.sum(jnp.where(iota((1, ndp), 1) == dp, len_ref[...], 0), axis=1, keepdims=True)
    live_total = jnp.sum(len_ref[...], axis=1, keepdims=True).astype(F32)
    index = iota((rows, 1), 0)
    w_head = wall[y, :, :, :, 2 * hd : 5 * hd].reshape(width, 3 * hd)
    kv_copies = []

    def alive_of(block):
        return jnp.where(index + block * rows < length, 1.0, 0.0)

    def block_span(block):
        return pl.ds(pl.multiple_of(block * rows, rows), rows)

    def project(at, order):
        projected = dot(xn[at], w_head)
        proj[at] = projected
        activated = projected * jax.nn.sigmoid(projected)
        value, key = activated[:, :hd], activated[:, hd : 2 * hd] * alive_of(CORES * at + c)
        query = activated[:, 2 * hd :]
        kv[CORES * at + c, :, :hd] = value.astype(BF16)
        kv[CORES * at + c, :, hd:] = key.astype(BF16)
        copy = rcopy(kv.at[CORES * at + c], kv.at[CORES * at + c], ks.at[order], kr.at[order], sibling)
        copy.start()
        kv_copies.append(copy)
        span = block_span(CORES * at + c)
        vt[:, span] = value.T.astype(BF16)
        kt[:, span] = key.T.astype(BF16)
        qs[block_span(at), :] = query.astype(BF16)
        qt[:, block_span(at)] = query.T.astype(BF16)

    project(y, 0)
    tok_copies[2].wait_recv()
    project(ym, 1)
    tok_copies[3].wait_recv()
    project(yp, 2)
    tok_copies[4].wait_recv()
    tok_copies[5].wait_recv()
    project(yo, 3)
    y_forward(near_copies)
    y_start(far_copies)
    for copy in kv_copies:
        copy.wait_recv()
    for u in range(HEADS):
        block = CORES * u + other
        both = kv[block].astype(F32)
        vt[:, block_span(block)] = both[:, :hd].T.astype(BF16)
        kt[:, block_span(block)] = both[:, hd:].T.astype(BF16)

    def send_when(t, src, dst, send, recv):
        @pl.when(y != t)
        def _():
            rcopy(src, dst, send.at[t], recv.at[y], (dp, t * CORES + c)).start()

        @pl.when(y == t)
        def _():
            dst[...] = src[...]

    def wait_when(t, ref, send, recv):
        @pl.when(y != t)
        def _():
            rcopy(ref, ref, send.at[t], recv.at[t], (dp, t * CORES + c)).wait_recv()

    def done_when(t, ref, send, recv):
        @pl.when(y != t)
        def _():
            rcopy(ref, ref, send.at[t], recv.at[t], (dp, t * CORES + c)).wait_send()

    causal = jnp.where(iota((rows, rows), 0) <= iota((rows, rows), 1), 1.0, 0.0)
    before = c.astype(F32)

    def weigh(block, low, high, mask):
        scores = dot(kv[block, :, hd:], qt[:, low:high]) * scale
        sigma = jax.nn.sigmoid(scores)
        weights = scores * sigma
        change = (sigma + weights * (1.0 - sigma)) * (scale / history)
        weights = weights * (1.0 / history)
        if mask is not None:
            weights, change = weights * mask, change * mask
        wst[block_span(block), low:high] = weights.astype(BF16)
        slope[block_span(block), low:high] = change

    queries = HEADS * rows
    for u in range(HEADS):
        low, high = u * rows, (u + 1) * rows
        for parity in range(2):
            block = CORES * u + (c if parity == 0 else other)
            weigh(block, low, high, causal if parity == 0 else before)
            if high < queries:
                weigh(block, high, queries, None)
        keys = CORES * (u + 1) * rows
        att_send[u] = dot(vt[:, :keys], wst[:keys, low:high]).T.astype(BF16)
        send_when(u, att_send.at[u], att_recv.at[y], as_, ar)

    relay_start(near_copies, near_relays)
    for copy in near_relays:
        copy.wait_recv()
    for t in range(HEADS):
        gproj[:, t * hd : (t + 1) * hd] = dot(xn[y], wall[t, :, :, :, hd : 2 * hd].reshape(width, hd))
    lines = TILE // 2
    line, spot = iota((hw, width), 0), iota((hw, width), 1)
    origin = lax.div(line, lines) * TILE + lax.rem(line, lines)
    for side in range(2):
        select = one_hot(spot == origin + side * lines)
        for t in range(HEADS):
            begin = side * (width // 2) + t * hd
            wout[:, begin : begin + hd] = dot(select, wall[t, :, :, :, :hd].reshape(width, hd)).astype(BF16)

    y_forward(far_copies)
    own_col = jnp.sum(
        jnp.where(iota((rows, ndp), 1) == lax.div(iota((rows, ndp), 0), cap), own_row, 0), axis=1, keepdims=True
    )
    away = lax.rem(x - lax.div(own_col, NZ) + nx, nx)
    slot_of = sum(jnp.where(away == hop, slot, 0) for slot, hop in enumerate(hops))
    source = (slot_of * NZ + lax.rem(own_col, NZ)) * TILE + lax.rem(index, cap)
    for g in range(4):
        picks[g] = one_hot(iota((rows, ndp * TILE), 1) == source + g * cap)
    for copy in diff_z:
        copy.wait_recv()
    received = drecv[...].reshape(ndp * TILE, quarter)
    for g in range(4):
        idiff[:, g * quarter : (g + 1) * quarter] = dot(picks[g], received).astype(BF16)

    eye = iota((rows, rows), 0) == iota((rows, rows), 1)
    teacher = jnp.sum(jnp.where(eye, teach_ref[...], 0.0), axis=1, keepdims=True)
    alive = alive_of(sq)
    projected = gproj[...]
    gate = (projected * jax.nn.sigmoid(projected)).astype(BF16).astype(F32)
    gain_mid = gmid_ref[...]
    for t in range(HEADS):
        wait_when(t, att_recv.at[t], as_, ar)
    attended = jnp.concatenate([att_recv[t].astype(F32) for t in range(HEADS)], axis=1)
    normed_mid, factor_mid = normalize(attended)
    gated = (normed_mid * gain_mid * gate).astype(BF16)
    layer_out = (tok_ref[...].astype(F32) + dot(gated, wout[...])).astype(BF16).astype(F32)
    difference = idiff[...].astype(F32)
    errors = (jnp.sum(layer_out * difference, axis=1, keepdims=True) - teacher) * alive
    grad_out = (2.0 / live_total * errors * difference).astype(BF16)
    gout[...] = grad_out
    grad_gated = dot_nt(grad_out, wout[...])
    grad_normed = grad_gated * gain_mid * gate
    grad_attended = normalize_back(grad_normed, normed_mid, factor_mid).astype(BF16)
    for t in range(HEADS):
        da_send[t] = grad_attended[:, t * hd : (t + 1) * hd]
        send_when(t, da_send.at[t], da_recv.at[y], gs, gr)
    gpg[...] = (grad_gated * normed_mid * gain_mid * silu_slope(projected)).astype(BF16)

    def loss_send(buffer, place, send, recv, devices):
        copies = [
            rcopy(buffer.at[place], buffer.at[place], send.at[i], recv.at[i], device)
            for i, device in enumerate(devices)
        ]
        for copy in copies:
            copy.start()
        return copies

    lby[y] = jnp.broadcast_to(jnp.sum(errors * errors, axis=0, keepdims=True), (8, 128))
    loss_y = loss_send(lby, y, lys, lyr, [beside_y(d) for d in range(1, HEADS)])
    for t in range(HEADS):
        wait_when(t, da_recv.at[t], gs, gr)
    for t in range(HEADS):
        dat[:, t * rows : (t + 1) * rows] = da_recv[t].astype(F32).T.astype(BF16)

    def backward(u, parity):
        block = CORES * u + (c if parity == 0 else other)
        span, low = block_span(block), u * rows
        grad_weights = dot(kv[block, :, :hd], dat[:, low:])
        grad_scores = (grad_weights * slope[span, low:]).astype(BF16)
        dst[span, low:] = grad_scores
        grad_attended = da_recv[u:].reshape((HEADS - u) * rows, hd)
        grad_value = dot(wst[span, low:], grad_attended)
        grad_key = dot(grad_scores, qs[low:, :])
        return grad_value, grad_key

    part_copies = []
    for u in range(HEADS):
        grad_value, grad_key = backward(u, 1)
        dvk_send[u, :, :hd] = grad_value
        dvk_send[u, :, hd:] = grad_key
        copy = rcopy(dvk_send.at[u], dvk_recv.at[u], ps.at[u], pr.at[u], sibling)
        copy.start()
        part_copies.append(copy)
    relay_start(far_copies, far_relays)
    for copy in loss_y:
        copy.wait_recv()
    lbc[c] = jnp.sum(lby[...], axis=0)
    loss_c = loss_send(lbc, c, lcs, lcr, [sibling])
    for u in range(HEADS):
        grad_value, grad_key = backward(u, 0)
        part_copies[u].wait_recv()
        keep = alive_of(CORES * u + c)
        grad_value = (grad_value + dvk_recv[u, :, :hd]) * keep
        grad_key = (grad_key + dvk_recv[u, :, hd:]) * keep
        keys = CORES * (u + 1) * rows
        grad_query = dot(kt[:, :keys], dst[:keys, u * rows : (u + 1) * rows]).T
        gps[u, :, :hd] = (grad_value * silu_slope(proj[u, :, :hd])).astype(BF16)
        gps[u, :, hd : 2 * hd] = (grad_key * silu_slope(proj[u, :, hd : 2 * hd])).astype(BF16)
        gps[u, :, 2 * hd :] = (grad_query * silu_slope(proj[u, :, 2 * hd :])).astype(BF16)
        send_when(u, gps.at[u], gpr.at[y], fs, fr)
        if u == 0:
            loss_c[0].wait_recv()
            lbx[x] = jnp.sum(lbc[...], axis=0)
            loss_x = loss_send(lbx, x, lxs, lxr, [beside_x(d) for d in range(1, nx)])

    for copy in loss_x:
        copy.wait_recv()
    lbz[z] = jnp.sum(lbx[...], axis=0)
    loss_z = loss_send(lbz, z, lzs, lzr, [beside_z(d) for d in range(1, NZ)])

    for copy in far_relays:
        copy.wait_recv()
    grad_in = jnp.zeros((rows, width), F32)
    for t in range(HEADS):
        grad_in = grad_in + dot_nt(
            gpg[:, t * hd : (t + 1) * hd], wall[t, :, :, :, hd : 2 * hd].reshape(width, hd)
        )
    for t in range(HEADS):
        wait_when(t, gpr.at[t], fs, fr)
        grad_in = grad_in + dot_nt(gpr[t], wall[t, :, :, :, 2 * hd :].reshape(width, 3 * hd))
    normed_raw, factor_in = normalize(tok_ref[...].astype(F32))
    grad_norm = normalize_back(grad_in * gin_ref[...], normed_raw, factor_in)
    out_ref[...] = (gout[...].astype(F32) + grad_norm).astype(BF16)

    for copy in loss_z:
        copy.wait_recv()
    loss_ref[...] = jnp.sum(lbz[...], axis=0)[0:1, 0:1] / live_total

    for i in range(half - 1):
        shard_copy(i).wait_send()

    @pl.when(c == 0)
    def _():
        shard_copy(half - 1).wait_send()

    for copy in x_copies + relays + tok_copies + near_copies + near_relays + far_copies + far_relays:
        copy.wait_send()
    for copy in kv_copies + part_copies + loss_y + loss_c + loss_x + loss_z:
        copy.wait_send()
    for copy in request_x + request_z + diff_x + diff_z:
        copy.wait_send()
    for t in range(HEADS):
        done_when(t, att_send.at[t], as_, ar)
        done_when(t, da_send.at[t], gs, gr)
        done_when(t, gps.at[t], fs, fr)


def on_device(
    tokens, teacher, cand_items, owner_map, lengths, w_proj, w_out, gain_in, gain_mid, item_table
):
    rows, width = tokens.shape
    ndp = lax.axis_size("dp")
    nx = ndp // NZ
    hw = gain_mid.shape[0]
    hd = hw // HEADS
    blocks = HEADS * CORES
    half = NZ // 2
    quarter = width // 4

    vmem = pltpu.VMEM
    dma = pltpu.SemaphoreType.DMA
    scratch = [
        vmem((rows, width), BF16),
        vmem((1, rows), F32),
        vmem((2, rows), jnp.int32),
        vmem((1, ndp), jnp.int32),
        vmem((1, ndp), jnp.int32),
        vmem(w_out.shape, BF16),
        vmem((1, width), F32),
        vmem((1, hw), F32),
        vmem((HEADS, nx, NZ, TILE, 5 * hd), BF16),
        vmem((TILE, 5 * hd), BF16),
        vmem((HEADS, rows, width), BF16),
        vmem(item_table.shape, BF16),
        vmem((nx, NZ, 1, 128), F32),
        vmem((nx, NZ, 1, 128), F32),
        vmem((nx, NZ, 1, 128), F32),
        vmem((ndp, 128), F32),
        vmem((nx, NZ, TILE, quarter), BF16),
        vmem((nx, NZ, TILE, quarter), BF16),
        vmem((nx, NZ, TILE, quarter), BF16),
        vmem((4, rows, ndp * TILE), BF16),
        vmem((rows, width), BF16),
        vmem((HEADS, rows, 3 * hd), F32),
        vmem((blocks, rows, 2 * hd), BF16),
        vmem((hd, blocks * rows), BF16),
        vmem((hd, blocks * rows), BF16),
        vmem((HEADS * rows, hd), BF16),
        vmem((hd, HEADS * rows), BF16),
        vmem((blocks * rows, HEADS * rows), BF16),
        vmem((blocks * rows, HEADS * rows), F32),
        vmem((HEADS, rows, hd), BF16),
        vmem((HEADS, rows, hd), BF16),
        vmem((rows, hw), F32),
        vmem((hw, width), BF16),
        vmem((rows, width), BF16),
        vmem((rows, hw), BF16),
        vmem((HEADS, rows, hd), BF16),
        vmem((HEADS, rows, hd), BF16),
        vmem((hd, HEADS * rows), BF16),
        vmem((HEADS, rows, 2 * hd), F32),
        vmem((HEADS, rows, 2 * hd), F32),
        vmem((blocks * rows, HEADS * rows), BF16),
        vmem((HEADS, rows, 3 * hd), BF16),
        vmem((HEADS, rows, 3 * hd), BF16),
        vmem((HEADS, 8, 128), F32),
        vmem((CORES, 8, 128), F32),
        vmem((nx, 8, 128), F32),
        vmem((NZ, 8, 128), F32),
        dma((5,)),
        dma((8,)),
        dma((nx,)), dma((nx,)),
        dma((half,)), dma((half,)),
        dma((nx,)), dma((nx,)),
        dma((6,)), dma((6,)),
        dma((nx,)), dma((nx,)), dma((NZ,)), dma((NZ,)),
        dma((nx,)), dma((nx,)), dma((3, NZ)), dma((3, NZ)),
        dma((6,)), dma((6,)), dma((3,)), dma((3,)),
        dma((6,)), dma((6,)), dma((3,)), dma((3,)),
        dma((HEADS,)), dma((HEADS,)),
        dma((HEADS,)), dma((HEADS,)),
        dma((HEADS,)), dma((HEADS,)),
        dma((HEADS,)), dma((HEADS,)),
        dma((HEADS,)), dma((HEADS,)),
        dma((HEADS,)), dma((HEADS,)), dma((1,)), dma((1,)), dma((nx,)), dma((nx,)), dma((NZ,)), dma((NZ,)),
    ]
    whole = pl.BlockSpec(memory_space=pltpu.VMEM)
    anywhere = pl.BlockSpec(memory_space=pl.ANY)
    grads, loss = pl.pallas_call(
        kernel,
        out_shape=(jax.ShapeDtypeStruct(tokens.shape, BF16), jax.ShapeDtypeStruct((1, 1), F32)),
        in_specs=[anywhere] * 10,
        out_specs=(whole, whole),
        scratch_shapes=scratch,
        compiler_params=pltpu.CompilerParams(
            collective_id=0, has_side_effects=True, vmem_limit_bytes=56 * 1024 * 1024
        ),
    )(
        tokens,
        teacher.reshape(1, rows),
        cand_items.T,
        owner_map.reshape(1, ndp),
        lengths.reshape(1, ndp),
        w_proj,
        w_out,
        gain_in.reshape(1, width),
        gain_mid.reshape(1, hw),
        item_table,
    )
    return (grads, loss[0, 0])


def solution(mesh):
    in_specs = (
        P(("dp", "seq"), None),
        P(("dp", "seq")),
        P(("dp", "seq"), None),
        P(("dp", "seq")),
        P(),
        P("dp", None),
        P("dp", None),
        P(),
        P(),
        P("dp", None),
    )
    out_specs = (P(("dp", "seq"), None), P())
    return jax.shard_map(
        on_device, mesh=mesh, in_specs=in_specs, out_specs=out_specs, check_vma=False
    )
```

```python
import functools

import jax
import jax.numpy as jnp
from jax import lax
from jax.experimental import pallas as pl
from jax.experimental.pallas import tpu as pltpu
from jax.sharding import PartitionSpec as P

MESH = pl.DeviceIdType.MESH
F32 = jnp.float32
BF16 = jnp.bfloat16
HEADS = 4
NZ = 16
CORES = 2
TILE = 16
EPSILON = 1e-05


def dot(a, b):
    return jnp.dot(a, b, preferred_element_type=F32)


def dot_nt(a, b):
    return lax.dot_general(a, b, (((1,), (1,)), ((), ())), preferred_element_type=F32)


def iota(shape, axis):
    return lax.broadcasted_iota(jnp.int32, shape, axis)


def one_hot(condition):
    return jnp.where(condition, 1.0, 0.0).astype(BF16)


def silu_slope(inputs):
    sigma = jax.nn.sigmoid(inputs)
    return sigma * (1.0 + inputs * (1.0 - sigma))


def normalize(inputs):
    centered = inputs - jnp.mean(inputs, axis=-1, keepdims=True)
    factor = lax.rsqrt(jnp.mean(centered * centered, axis=-1, keepdims=True) + EPSILON)
    return (centered * factor, factor)


def normalize_back(upstream, normed, factor):
    inner = jnp.mean(upstream * normed, axis=-1, keepdims=True)
    return (upstream - jnp.mean(upstream, axis=-1, keepdims=True) - normed * inner) * factor


def small_parts(values):
    whole = values.astype(jnp.int32)
    return (whole >> 4).astype(F32).astype(BF16), (whole & 15).astype(F32).astype(BF16)


def kernel(
    tok_hbm, teach_hbm, cand_hbm, own_hbm, len_hbm, wp_ref, wo_hbm, gin_hbm, gmid_hbm, table_hbm,
    out_ref, loss_ref,
    tok_ref, teach_ref, cand_ref, own_ref, len_ref, wo_ref, gin_ref, gmid_ref,
    wall, piece, xn, table, req_send, req_mid, req_recv, rq, dsend, dmid, drecv, picks, idiff, proj, kv, kt, vt, qs, qt, wst, slope,
    att_send, att_recv, gproj, wout, gout, gpg, da_send, da_recv, dat, dvk_send, dvk_recv, dst,
    gps, gpr, lby, lbc, lbx, lbz,
    lsem, isem, xs, xr, zs, zr, rs, rr, ts, tr, qxs, qxr, qzs, qzr, dxs, dxr, dzs, dzr,
    ws, wr, wrs, wrr, vs, vr, vrs, vrr, ks, kr, as_, ar, gs, gr, ps, pr, fs, fr, lys, lyr, lcs, lcr, lxs, lxr, lzs, lzr,
):
    rows, width = tok_ref.shape
    hd = kv.shape[2] // 2
    nx = req_send.shape[0]
    ndp = nx * NZ
    nseq = HEADS * CORES
    half = NZ // 2
    cap = rows // ndp
    quarter = width // 4
    history = rows * nseq
    scale = float(hd) ** -0.5

    dp = lax.axis_index("dp")
    sq = lax.axis_index("seq")
    x, z = lax.div(dp, NZ), lax.rem(dp, NZ)
    y, c = lax.div(sq, CORES), lax.rem(sq, CORES)
    other = 1 - c
    yp, ym = lax.rem(y + 1, HEADS), lax.rem(y + HEADS - 1, HEADS)
    yo = lax.rem(y + 2, HEADS)
    up, down = (dp, yp * CORES + c), (dp, ym * CORES + c)
    sibling = (dp, y * CORES + other)

    def rcopy(src, dst, send, recv, device):
        return pltpu.make_async_remote_copy(
            src_ref=src, dst_ref=dst, send_sem=send, recv_sem=recv, device_id=device, device_id_type=MESH
        )

    def beside_x(d):
        return (lax.rem(x + d, nx) * NZ + z, sq)

    def beside_z(d):
        return (x * NZ + lax.rem(z + d, NZ), sq)

    def beside_y(d):
        return (dp, lax.rem(y + d, HEADS) * CORES + c)

    barrier = pltpu.get_barrier_semaphore()
    partners = [sibling] + [beside_y(d) for d in range(1, HEADS)]
    partners += [beside_x(d) for d in range(1, nx)] + [beside_z(d) for d in range(1, NZ)]
    partners += [(device, y * CORES + other) for device, _ in [beside_z(d) for d in range(1, NZ)]]
    for device in partners:
        pl.semaphore_signal(barrier, inc=1, device_id=device, device_id_type=MESH)

    hw = HEADS * hd
    arguments = [
        (tok_hbm, tok_ref), (gin_hbm, gin_ref), (own_hbm, own_ref), (cand_hbm, cand_ref),
        (wo_hbm, wo_ref), (len_hbm, len_ref), (teach_hbm, teach_ref), (gmid_hbm, gmid_ref),
    ]
    inputs = [pltpu.make_async_copy(src, dst, isem.at[i]) for i, (src, dst) in enumerate(arguments)]
    pieces = [(0, hd), (hw, 2 * hd), (3 * hw, 3 * hd), (2 * hw, 4 * hd)]
    local = []
    for i, (start, to) in enumerate(pieces):
        begin = pl.multiple_of(start + y * hd, hd)
        local.append(
            pltpu.make_async_copy(wp_ref.at[:, pl.ds(begin, hd)], piece.at[:, pl.ds(to, hd)], lsem.at[i])
        )
    table_copy = pltpu.make_async_copy(table_hbm, table, lsem.at[4])
    for copy in inputs + local:
        copy.start()
    table_copy.start()
    for copy in inputs + local:
        copy.wait()
    sides = [wo_ref[:, pl.ds(pl.multiple_of(i * (width // 2) + y * hd, hd), hd)].astype(F32) for i in range(2)]
    piece[:, :hd] = jnp.concatenate(sides, axis=0).astype(BF16)

    @pl.when(c == lax.div(z, half))
    def _():
        wall[y, x, z] = piece[...]

    pl.semaphore_wait(barrier, len(partners))

    shard = wall.at[y, x, z]
    collector = y * CORES + lax.div(z, half)

    def shard_copy(i):
        device = (x * NZ + lax.rem(z + 1 + i + c * half, NZ), collector)
        return rcopy(piece, shard, zs.at[i], zr.at[lax.rem(z, half)], device)

    for i in range(half - 1):
        shard_copy(i).start()

    @pl.when(c == 0)
    def _():
        shard_copy(half - 1).start()

    own_row = own_ref[...]
    expand = one_hot(lax.div(iota((ndp, rows), 1), cap) == iota((ndp, rows), 0))
    own_rep = dot(jnp.broadcast_to(own_row.astype(F32).astype(BF16), (8, ndp)), expand)[0:1, :]
    to_owner = one_hot(iota((ndp, rows), 0).astype(F32) == own_rep)
    lane = iota((128, rows), 0)
    inside = (lax.div(lane, 2) == lax.rem(iota((128, rows), 1), cap)) & (lane < 2 * cap)
    both = jnp.where(lax.rem(lane, 2) == 0, cand_ref[0:1, :], cand_ref[1:2, :])
    high, low = small_parts(jnp.where(inside, both, 0))
    requests = dot_nt(to_owner, high) * 16.0 + dot_nt(to_owner, low)
    for p in range(ndp):
        req_send[p // NZ, p % NZ] = requests[p : p + 1, :]
    request_x = []
    for d in range(1, nx):
        block = req_send.at[lax.rem(x + d, nx)]
        request_x.append(rcopy(block, req_mid.at[x], qxs.at[d - 1], qxr.at[d - 1], beside_x(d)))
    for copy in request_x:
        copy.start()
    req_mid[x] = req_send[x]

    tokens = tok_ref[...].astype(F32)
    normed_raw, factor_in = normalize(tokens)
    xn[y] = (normed_raw * gin_ref[...]).astype(BF16)

    def y_copies(part, send, recv):
        return [
            rcopy(part(y, 0), part(y, 0), send.at[0], recv.at[0], up),
            rcopy(part(y, 1), part(y, 1), send.at[1], recv.at[1], down),
            rcopy(part(y, 1), part(y, 1), send.at[2], recv.at[2], up),
            rcopy(part(y, 0), part(y, 0), send.at[3], recv.at[3], down),
            rcopy(part(ym, 0), part(ym, 0), send.at[4], recv.at[4], up),
            rcopy(part(yp, 1), part(yp, 1), send.at[5], recv.at[5], down),
        ]

    def y_start(copies):
        for copy in copies[:4]:
            copy.start()

    def y_forward(copies):
        copies[0].wait_recv()
        copies[4].start()
        copies[1].wait_recv()
        copies[5].start()

    tok_copies = y_copies(lambda at, h: xn.at[at, pl.ds(h * (rows // 2), rows // 2), :], ts, tr)

    y_start(tok_copies)

    for copy in request_x:
        copy.wait_recv()
    request_z = []
    for d in range(1, NZ):
        block = req_mid.at[:, lax.rem(z + d, NZ)]
        request_z.append(rcopy(block, req_recv.at[:, z], qzs.at[d - 1], qzr.at[d - 1], beside_z(d)))
    for copy in request_z:
        copy.start()
    req_recv[:, z] = req_mid[:, z]

    def collected(d):
        return wall.at[y, lax.rem(x - d + nx, nx), pl.ds(c * half, half)]

    for j in range(half):

        @pl.when(z != c * half + j)
        def _():
            rcopy(shard, shard, zs.at[0], zr.at[j], sibling).wait_recv()

    x_copies = []
    for d in range(1, nx):
        x_copies.append(rcopy(collected(0), collected(0), xs.at[d - 1], xr.at[d - 1], beside_x(d)))
    relays = [rcopy(collected(d), collected(d), rs.at[d], rr.at[d], sibling) for d in range(nx)]
    for copy in x_copies:
        copy.start()
    relays[0].start()

    for copy in request_z:
        copy.wait_recv()
    for p in range(ndp):
        rq[p : p + 1, :] = req_recv[p // NZ, p % NZ]
    table_copy.wait()
    high, low = small_parts(rq[...])
    chunk = NZ * TILE
    row = iota((chunk, 128), 0)
    place = 2 * lax.rem(row, cap)
    lanes = iota((chunk, 128), 1)
    group = lax.div(lax.rem(iota((chunk, quarter), 0), TILE), cap)

    def differences(side):
        spread = one_hot(lax.div(iota((chunk, ndp), 0), TILE) + side * NZ == iota((chunk, ndp), 1))
        wanted = dot(spread, high) * 16.0 + dot(spread, low)
        first_item = jnp.sum(jnp.where(lanes == place, wanted, 0.0), axis=1, keepdims=True)
        second_item = jnp.sum(jnp.where(lanes == place + 1, wanted, 0.0), axis=1, keepdims=True)
        items = iota((chunk, table.shape[0]), 1).astype(F32)
        signs = jnp.where(items == first_item, 1.0, 0.0) - jnp.where(items == second_item, 1.0, 0.0)
        signs = signs.astype(BF16)
        total = jnp.zeros((chunk, quarter), F32)
        for g in range(4):
            term = dot(signs, table[:, g * quarter : (g + 1) * quarter])
            total = jnp.where(group == g, term, total)
        return total.astype(BF16).reshape(NZ, TILE, quarter)

    hops = [0, 1] + [nx - 1] * (nx > 2) + list(range(2, nx - 1))
    rounds = [(0, 1), (1, min(3, nx))] + [(3, nx)] * (nx > 3)
    diff_z = []

    def along_z(i):
        low, high = rounds[i]
        slots = pl.ds(low, high - low)
        copies = []
        for d in range(1, NZ):
            block = dmid.at[slots, lax.rem(z + d, NZ)]
            copies.append(rcopy(block, drecv.at[slots, z], dzs.at[i, d - 1], dzr.at[i, d - 1], beside_z(d)))
        for copy in copies:
            copy.start()
        drecv[slots, z] = dmid[slots, z]
        diff_z.extend(copies)

    dmid[0] = differences(x)
    along_z(0)
    diff_x = []
    for slot in range(1, nx):
        d = hops[slot]
        side = lax.rem(x + d, nx)
        dsend[side] = differences(side)
        copy = rcopy(dsend.at[side], dmid.at[slot], dxs.at[slot - 1], dxr.at[slot - 1], beside_x(d))
        copy.start()
        diff_x.append(copy)
        if slot == 1:
            y_forward(tok_copies)

    near = pl.ds(0, 2 * hd)
    far = pl.ds(2 * hd, 3 * hd)

    def weight_part(columns):
        def part(at, h):
            return wall.at[at, pl.ds(h * (nx // 2), nx // 2), pl.ds(c * half, half), :, columns]

        return part

    def weight_relay(at, index, columns, send, recv):
        block = wall.at[at, :, pl.ds(c * half, half), :, columns]
        return rcopy(block, block, send.at[index], recv.at[index], sibling)

    near_copies = y_copies(weight_part(near), ws, wr)
    near_relays = [weight_relay(at, i, near, wrs, wrr) for i, at in enumerate((ym, yp, yo))]
    far_copies = y_copies(weight_part(far), vs, vr)
    far_relays = [weight_relay(at, i, far, vrs, vrr) for i, at in enumerate((ym, yp, yo))]

    def relay_start(copies, relayed):
        copies[2].wait_recv()
        relayed[0].start()
        copies[3].wait_recv()
        relayed[1].start()
        copies[4].wait_recv()
        copies[5].wait_recv()
        relayed[2].start()

    for d in hops[1:]:
        x_copies[d - 1].wait_recv()
        relays[d].start()
    y_start(near_copies)

    for d in range(1, nx):
        if d < len(rounds):
            for slot in range(*rounds[d]):
                diff_x[slot - 1].wait_recv()
            along_z(d)
    for copy in relays:
        copy.wait_recv()

    length = jnp.sum(jnp.where(iota((1, ndp), 1) == dp, len_ref[...], 0), axis=1, keepdims=True)
    live_total = jnp.sum(len_ref[...], axis=1, keepdims=True).astype(F32)
    index = iota((rows, 1), 0)
    w_head = wall[y, :, :, :, 2 * hd : 5 * hd].reshape(width, 3 * hd)
    kv_copies = []

    def alive_of(block):
        return jnp.where(index + block * rows < length, 1.0, 0.0)

    def block_span(block):
        return pl.ds(pl.multiple_of(block * rows, rows), rows)

    def project(at, order):
        projected = dot(xn[at], w_head)
        proj[at] = projected
        activated = projected * jax.nn.sigmoid(projected)
        value, key = activated[:, :hd], activated[:, hd : 2 * hd] * alive_of(CORES * at + c)
        query = activated[:, 2 * hd :]
        kv[CORES * at + c, :, :hd] = value.astype(BF16)
        kv[CORES * at + c, :, hd:] = key.astype(BF16)
        copy = rcopy(kv.at[CORES * at + c], kv.at[CORES * at + c], ks.at[order], kr.at[order], sibling)
        copy.start()
        kv_copies.append(copy)
        span = block_span(CORES * at + c)
        vt[:, span] = value.T.astype(BF16)
        kt[:, span] = key.T.astype(BF16)
        qs[block_span(at), :] = query.astype(BF16)
        qt[:, block_span(at)] = query.T.astype(BF16)

    project(y, 0)
    tok_copies[2].wait_recv()
    project(ym, 1)
    tok_copies[3].wait_recv()
    project(yp, 2)
    tok_copies[4].wait_recv()
    tok_copies[5].wait_recv()
    project(yo, 3)
    y_forward(near_copies)
    y_start(far_copies)
    for copy in kv_copies:
        copy.wait_recv()
    for u in range(HEADS):
        block = CORES * u + other
        both = kv[block].astype(F32)
        vt[:, block_span(block)] = both[:, :hd].T.astype(BF16)
        kt[:, block_span(block)] = both[:, hd:].T.astype(BF16)

    def send_when(t, src, dst, send, recv):
        @pl.when(y != t)
        def _():
            rcopy(src, dst, send.at[t], recv.at[y], (dp, t * CORES + c)).start()

        @pl.when(y == t)
        def _():
            dst[...] = src[...]

    def wait_when(t, ref, send, recv):
        @pl.when(y != t)
        def _():
            rcopy(ref, ref, send.at[t], recv.at[t], (dp, t * CORES + c)).wait_recv()

    def done_when(t, ref, send, recv):
        @pl.when(y != t)
        def _():
            rcopy(ref, ref, send.at[t], recv.at[t], (dp, t * CORES + c)).wait_send()

    causal = jnp.where(iota((rows, rows), 0) <= iota((rows, rows), 1), 1.0, 0.0)
    before = c.astype(F32)

    def weigh(block, low, high, mask):
        scores = dot(kv[block, :, hd:], qt[:, low:high]) * scale
        sigma = jax.nn.sigmoid(scores)
        weights = scores * sigma
        change = (sigma + weights * (1.0 - sigma)) * (scale / history)
        weights = weights * (1.0 / history)
        if mask is not None:
            weights, change = weights * mask, change * mask
        wst[block_span(block), low:high] = weights.astype(BF16)
        slope[block_span(block), low:high] = change

    queries = HEADS * rows
    for u in range(HEADS):
        low, high = u * rows, (u + 1) * rows
        for parity in range(2):
            block = CORES * u + (c if parity == 0 else other)
            weigh(block, low, high, causal if parity == 0 else before)
            if high < queries:
                weigh(block, high, queries, None)
        keys = CORES * (u + 1) * rows
        att_send[u] = dot(vt[:, :keys], wst[:keys, low:high]).T.astype(BF16)
        send_when(u, att_send.at[u], att_recv.at[y], as_, ar)

    relay_start(near_copies, near_relays)
    for copy in near_relays:
        copy.wait_recv()
    for t in range(HEADS):
        gproj[:, t * hd : (t + 1) * hd] = dot(xn[y], wall[t, :, :, :, hd : 2 * hd].reshape(width, hd))
    lines = TILE // 2
    line, spot = iota((hw, width), 0), iota((hw, width), 1)
    origin = lax.div(line, lines) * TILE + lax.rem(line, lines)
    for side in range(2):
        select = one_hot(spot == origin + side * lines)
        for t in range(HEADS):
            begin = side * (width // 2) + t * hd
            wout[:, begin : begin + hd] = dot(select, wall[t, :, :, :, :hd].reshape(width, hd)).astype(BF16)

    y_forward(far_copies)
    own_col = jnp.sum(
        jnp.where(iota((rows, ndp), 1) == lax.div(iota((rows, ndp), 0), cap), own_row, 0), axis=1, keepdims=True
    )
    away = lax.rem(x - lax.div(own_col, NZ) + nx, nx)
    slot_of = sum(jnp.where(away == hop, slot, 0) for slot, hop in enumerate(hops))
    source = (slot_of * NZ + lax.rem(own_col, NZ)) * TILE + lax.rem(index, cap)
    for g in range(4):
        picks[g] = one_hot(iota((rows, ndp * TILE), 1) == source + g * cap)
    for copy in diff_z:
        copy.wait_recv()
    received = drecv[...].reshape(ndp * TILE, quarter)
    for g in range(4):
        idiff[:, g * quarter : (g + 1) * quarter] = dot(picks[g], received).astype(BF16)

    eye = iota((rows, rows), 0) == iota((rows, rows), 1)
    teacher = jnp.sum(jnp.where(eye, teach_ref[...], 0.0), axis=1, keepdims=True)
    alive = alive_of(sq)
    projected = gproj[...]
    gate = (projected * jax.nn.sigmoid(projected)).astype(BF16).astype(F32)
    gain_mid = gmid_ref[...]
    for t in range(HEADS):
        wait_when(t, att_recv.at[t], as_, ar)
    attended = jnp.concatenate([att_recv[t].astype(F32) for t in range(HEADS)], axis=1)
    normed_mid, factor_mid = normalize(attended)
    gated = (normed_mid * gain_mid * gate).astype(BF16)
    layer_out = (tok_ref[...].astype(F32) + dot(gated, wout[...])).astype(BF16).astype(F32)
    difference = idiff[...].astype(F32)
    errors = (jnp.sum(layer_out * difference, axis=1, keepdims=True) - teacher) * alive
    grad_out = (2.0 / live_total * errors * difference).astype(BF16)
    gout[...] = grad_out
    grad_gated = dot_nt(grad_out, wout[...])
    grad_normed = grad_gated * gain_mid * gate
    grad_attended = normalize_back(grad_normed, normed_mid, factor_mid).astype(BF16)
    for t in range(HEADS):
        da_send[t] = grad_attended[:, t * hd : (t + 1) * hd]
        send_when(t, da_send.at[t], da_recv.at[y], gs, gr)
    gpg[...] = (grad_gated * normed_mid * gain_mid * silu_slope(projected)).astype(BF16)

    def loss_send(buffer, place, send, recv, devices):
        copies = [
            rcopy(buffer.at[place], buffer.at[place], send.at[i], recv.at[i], device)
            for i, device in enumerate(devices)
        ]
        for copy in copies:
            copy.start()
        return copies

    lby[y] = jnp.broadcast_to(jnp.sum(errors * errors, axis=0, keepdims=True), (8, 128))
    loss_y = loss_send(lby, y, lys, lyr, [beside_y(d) for d in range(1, HEADS)])
    for t in range(HEADS):
        wait_when(t, da_recv.at[t], gs, gr)
    for t in range(HEADS):
        dat[:, t * rows : (t + 1) * rows] = da_recv[t].astype(F32).T.astype(BF16)

    def backward(u, parity):
        block = CORES * u + (c if parity == 0 else other)
        span, low = block_span(block), u * rows
        grad_weights = dot(kv[block, :, :hd], dat[:, low:])
        grad_scores = (grad_weights * slope[span, low:]).astype(BF16)
        dst[span, low:] = grad_scores
        grad_attended = da_recv[u:].reshape((HEADS - u) * rows, hd)
        grad_value = dot(wst[span, low:], grad_attended)
        grad_key = dot(grad_scores, qs[low:, :])
        return grad_value, grad_key

    part_copies = []
    for u in range(HEADS):
        grad_value, grad_key = backward(u, 1)
        dvk_send[u, :, :hd] = grad_value
        dvk_send[u, :, hd:] = grad_key
        copy = rcopy(dvk_send.at[u], dvk_recv.at[u], ps.at[u], pr.at[u], sibling)
        copy.start()
        part_copies.append(copy)
    relay_start(far_copies, far_relays)
    for copy in loss_y:
        copy.wait_recv()
    lbc[c] = jnp.sum(lby[...], axis=0)
    loss_c = loss_send(lbc, c, lcs, lcr, [sibling])
    for u in range(HEADS):
        grad_value, grad_key = backward(u, 0)
        part_copies[u].wait_recv()
        keep = alive_of(CORES * u + c)
        grad_value = (grad_value + dvk_recv[u, :, :hd]) * keep
        grad_key = (grad_key + dvk_recv[u, :, hd:]) * keep
        keys = CORES * (u + 1) * rows
        grad_query = dot(kt[:, :keys], dst[:keys, u * rows : (u + 1) * rows]).T
        gps[u, :, :hd] = (grad_value * silu_slope(proj[u, :, :hd])).astype(BF16)
        gps[u, :, hd : 2 * hd] = (grad_key * silu_slope(proj[u, :, hd : 2 * hd])).astype(BF16)
        gps[u, :, 2 * hd :] = (grad_query * silu_slope(proj[u, :, 2 * hd :])).astype(BF16)
        send_when(u, gps.at[u], gpr.at[y], fs, fr)
        if u == 0:
            loss_c[0].wait_recv()
            lbx[x] = jnp.sum(lbc[...], axis=0)
            loss_x = loss_send(lbx, x, lxs, lxr, [beside_x(d) for d in range(1, nx)])

    for copy in loss_x:
        copy.wait_recv()
    lbz[z] = jnp.sum(lbx[...], axis=0)
    loss_z = loss_send(lbz, z, lzs, lzr, [beside_z(d) for d in range(1, NZ)])

    for copy in far_relays:
        copy.wait_recv()
    grad_in = jnp.zeros((rows, width), F32)
    for t in range(HEADS):
        grad_in = grad_in + dot_nt(
            gpg[:, t * hd : (t + 1) * hd], wall[t, :, :, :, hd : 2 * hd].reshape(width, hd)
        )
    for t in range(HEADS):
        wait_when(t, gpr.at[t], fs, fr)
        grad_in = grad_in + dot_nt(gpr[t], wall[t, :, :, :, 2 * hd :].reshape(width, 3 * hd))
    normed_raw, factor_in = normalize(tok_ref[...].astype(F32))
    grad_norm = normalize_back(grad_in * gin_ref[...], normed_raw, factor_in)
    out_ref[...] = (gout[...].astype(F32) + grad_norm).astype(BF16)

    for copy in loss_z:
        copy.wait_recv()
    loss_ref[...] = jnp.sum(lbz[...], axis=0)[0:1, 0:1] / live_total

    for i in range(half - 1):
        shard_copy(i).wait_send()

    @pl.when(c == 0)
    def _():
        shard_copy(half - 1).wait_send()

    for copy in x_copies + relays + tok_copies + near_copies + near_relays + far_copies + far_relays:
        copy.wait_send()
    for copy in kv_copies + part_copies + loss_y + loss_c + loss_x + loss_z:
        copy.wait_send()
    for copy in request_x + request_z + diff_x + diff_z:
        copy.wait_send()
    for t in range(HEADS):
        done_when(t, att_send.at[t], as_, ar)
        done_when(t, da_send.at[t], gs, gr)
        done_when(t, gps.at[t], fs, fr)


def on_device(
    tokens, teacher, cand_items, owner_map, lengths, w_proj, w_out, gain_in, gain_mid, item_table
):
    rows, width = tokens.shape
    ndp = lax.axis_size("dp")
    nx = ndp // NZ
    hw = gain_mid.shape[0]
    hd = hw // HEADS
    blocks = HEADS * CORES
    half = NZ // 2
    quarter = width // 4

    vmem = pltpu.VMEM
    dma = pltpu.SemaphoreType.DMA
    scratch = [
        vmem((rows, width), BF16),
        vmem((1, rows), F32),
        vmem((2, rows), jnp.int32),
        vmem((1, ndp), jnp.int32),
        vmem((1, ndp), jnp.int32),
        vmem(w_out.shape, BF16),
        vmem((1, width), F32),
        vmem((1, hw), F32),
        vmem((HEADS, nx, NZ, TILE, 5 * hd), BF16),
        vmem((TILE, 5 * hd), BF16),
        vmem((HEADS, rows, width), BF16),
        vmem(item_table.shape, BF16),
        vmem((nx, NZ, 1, 128), F32),
        vmem((nx, NZ, 1, 128), F32),
        vmem((nx, NZ, 1, 128), F32),
        vmem((ndp, 128), F32),
        vmem((nx, NZ, TILE, quarter), BF16),
        vmem((nx, NZ, TILE, quarter), BF16),
        vmem((nx, NZ, TILE, quarter), BF16),
        vmem((4, rows, ndp * TILE), BF16),
        vmem((rows, width), BF16),
        vmem((HEADS, rows, 3 * hd), F32),
        vmem((blocks, rows, 2 * hd), BF16),
        vmem((hd, blocks * rows), BF16),
        vmem((hd, blocks * rows), BF16),
        vmem((HEADS * rows, hd), BF16),
        vmem((hd, HEADS * rows), BF16),
        vmem((blocks * rows, HEADS * rows), BF16),
        vmem((blocks * rows, HEADS * rows), F32),
        vmem((HEADS, rows, hd), BF16),
        vmem((HEADS, rows, hd), BF16),
        vmem((rows, hw), F32),
        vmem((hw, width), BF16),
        vmem((rows, width), BF16),
        vmem((rows, hw), BF16),
        vmem((HEADS, rows, hd), BF16),
        vmem((HEADS, rows, hd), BF16),
        vmem((hd, HEADS * rows), BF16),
        vmem((HEADS, rows, 2 * hd), F32),
        vmem((HEADS, rows, 2 * hd), F32),
        vmem((blocks * rows, HEADS * rows), BF16),
        vmem((HEADS, rows, 3 * hd), BF16),
        vmem((HEADS, rows, 3 * hd), BF16),
        vmem((HEADS, 8, 128), F32),
        vmem((CORES, 8, 128), F32),
        vmem((nx, 8, 128), F32),
        vmem((NZ, 8, 128), F32),
        dma((5,)),
        dma((8,)),
        dma((nx,)), dma((nx,)),
        dma((half,)), dma((half,)),
        dma((nx,)), dma((nx,)),
        dma((6,)), dma((6,)),
        dma((nx,)), dma((nx,)), dma((NZ,)), dma((NZ,)),
        dma((nx,)), dma((nx,)), dma((3, NZ)), dma((3, NZ)),
        dma((6,)), dma((6,)), dma((3,)), dma((3,)),
        dma((6,)), dma((6,)), dma((3,)), dma((3,)),
        dma((HEADS,)), dma((HEADS,)),
        dma((HEADS,)), dma((HEADS,)),
        dma((HEADS,)), dma((HEADS,)),
        dma((HEADS,)), dma((HEADS,)),
        dma((HEADS,)), dma((HEADS,)),
        dma((HEADS,)), dma((HEADS,)), dma((1,)), dma((1,)), dma((nx,)), dma((nx,)), dma((NZ,)), dma((NZ,)),
    ]
    whole = pl.BlockSpec(memory_space=pltpu.VMEM)
    anywhere = pl.BlockSpec(memory_space=pl.ANY)
    grads, loss = pl.pallas_call(
        kernel,
        out_shape=(jax.ShapeDtypeStruct(tokens.shape, BF16), jax.ShapeDtypeStruct((1, 1), F32)),
        in_specs=[anywhere] * 10,
        out_specs=(whole, whole),
        scratch_shapes=scratch,
        compiler_params=pltpu.CompilerParams(
            collective_id=0, has_side_effects=True, vmem_limit_bytes=56 * 1024 * 1024
        ),
    )(
        tokens,
        teacher.reshape(1, rows),
        cand_items.T,
        owner_map.reshape(1, ndp),
        lengths.reshape(1, ndp),
        w_proj,
        w_out,
        gain_in.reshape(1, width),
        gain_mid.reshape(1, hw),
        item_table,
    )
    return (grads, loss[0, 0])


def solution(mesh):
    in_specs = (
        P(("dp", "seq"), None),
        P(("dp", "seq")),
        P(("dp", "seq"), None),
        P(("dp", "seq")),
        P(),
        P("dp", None),
        P("dp", None),
        P(),
        P(),
        P("dp", None),
    )
    out_specs = (P(("dp", "seq"), None), P())
    return jax.shard_map(
        on_device, mesh=mesh, in_specs=in_specs, out_specs=out_specs, check_vma=False
    )
```

```python
import functools

import jax
import jax.numpy as jnp
from jax import lax
from jax.experimental import pallas as pl
from jax.experimental.pallas import tpu as pltpu
from jax.sharding import PartitionSpec as P

MESH = pl.DeviceIdType.MESH
F32 = jnp.float32
BF16 = jnp.bfloat16
HEADS = 4
NZ = 16
CORES = 2
TILE = 16
EPSILON = 1e-05


def dot(a, b):
    return jnp.dot(a, b, preferred_element_type=F32)


def dot_nt(a, b):
    return lax.dot_general(a, b, (((1,), (1,)), ((), ())), preferred_element_type=F32)


def iota(shape, axis):
    return lax.broadcasted_iota(jnp.int32, shape, axis)


def one_hot(condition):
    return jnp.where(condition, 1.0, 0.0).astype(BF16)


def silu_slope(inputs):
    sigma = jax.nn.sigmoid(inputs)
    return sigma * (1.0 + inputs * (1.0 - sigma))


def normalize(inputs):
    centered = inputs - jnp.mean(inputs, axis=-1, keepdims=True)
    factor = lax.rsqrt(jnp.mean(centered * centered, axis=-1, keepdims=True) + EPSILON)
    return (centered * factor, factor)


def normalize_back(upstream, normed, factor):
    inner = jnp.mean(upstream * normed, axis=-1, keepdims=True)
    return (upstream - jnp.mean(upstream, axis=-1, keepdims=True) - normed * inner) * factor


def small_parts(values):
    whole = values.astype(jnp.int32)
    return (whole >> 4).astype(F32).astype(BF16), (whole & 15).astype(F32).astype(BF16)


def kernel(
    tok_hbm, teach_hbm, cand_hbm, own_hbm, len_hbm, wp_ref, wo_hbm, gin_hbm, gmid_hbm, table_hbm,
    out_ref, loss_ref,
    tok_ref, teach_ref, cand_ref, own_ref, len_ref, wo_ref, gin_ref, gmid_ref,
    wall, piece, xn, table, req_send, req_mid, req_recv, rq, dsend, dmid, drecv, picks, idiff, proj, kv, kt, vt, qs, qt, wst, slope,
    att_send, att_recv, gproj, wout, gout, gpg, da_send, da_recv, dat, dvk_send, dvk_recv, dst,
    gps, gpr, lby, lbc, lbx, lbz,
    lsem, isem, xs, xr, zs, zr, rs, rr, ts, tr, qxs, qxr, qzs, qzr, dxs, dxr, dzs, dzr,
    ws, wr, wrs, wrr, vs, vr, vrs, vrr, ks, kr, as_, ar, gs, gr, ps, pr, fs, fr, lys, lyr, lcs, lcr, lxs, lxr, lzs, lzr,
):
    rows, width = tok_ref.shape
    hd = kv.shape[2] // 2
    nx = req_send.shape[0]
    ndp = nx * NZ
    nseq = HEADS * CORES
    half = NZ // 2
    cap = rows // ndp
    quarter = width // 4
    history = rows * nseq
    scale = float(hd) ** -0.5

    dp = lax.axis_index("dp")
    sq = lax.axis_index("seq")
    x, z = lax.div(dp, NZ), lax.rem(dp, NZ)
    y, c = lax.div(sq, CORES), lax.rem(sq, CORES)
    other = 1 - c
    yp, ym = lax.rem(y + 1, HEADS), lax.rem(y + HEADS - 1, HEADS)
    yo = lax.rem(y + 2, HEADS)
    up, down = (dp, yp * CORES + c), (dp, ym * CORES + c)
    sibling = (dp, y * CORES + other)

    def rcopy(src, dst, send, recv, device):
        return pltpu.make_async_remote_copy(
            src_ref=src, dst_ref=dst, send_sem=send, recv_sem=recv, device_id=device, device_id_type=MESH
        )

    def beside_x(d):
        return (lax.rem(x + d, nx) * NZ + z, sq)

    def beside_z(d):
        return (x * NZ + lax.rem(z + d, NZ), sq)

    def beside_y(d):
        return (dp, lax.rem(y + d, HEADS) * CORES + c)

    barrier = pltpu.get_barrier_semaphore()
    partners = [sibling] + [beside_y(d) for d in range(1, HEADS)]
    partners += [beside_x(d) for d in range(1, nx)] + [beside_z(d) for d in range(1, NZ)]
    partners += [(device, y * CORES + other) for device, _ in [beside_z(d) for d in range(1, NZ)]]
    for device in partners:
        pl.semaphore_signal(barrier, inc=1, device_id=device, device_id_type=MESH)

    hw = HEADS * hd
    arguments = [
        (tok_hbm, tok_ref), (gin_hbm, gin_ref), (own_hbm, own_ref), (cand_hbm, cand_ref),
        (wo_hbm, wo_ref), (len_hbm, len_ref), (teach_hbm, teach_ref), (gmid_hbm, gmid_ref),
    ]
    inputs = [pltpu.make_async_copy(src, dst, isem.at[i]) for i, (src, dst) in enumerate(arguments)]
    pieces = [(0, hd), (hw, 2 * hd), (3 * hw, 3 * hd), (2 * hw, 4 * hd)]
    local = []
    for i, (start, to) in enumerate(pieces):
        begin = pl.multiple_of(start + y * hd, hd)
        local.append(
            pltpu.make_async_copy(wp_ref.at[:, pl.ds(begin, hd)], piece.at[:, pl.ds(to, hd)], lsem.at[i])
        )
    table_copy = pltpu.make_async_copy(table_hbm, table, lsem.at[4])
    for copy in inputs + local:
        copy.start()
    table_copy.start()
    for copy in inputs + local:
        copy.wait()
    sides = [wo_ref[:, pl.ds(pl.multiple_of(i * (width // 2) + y * hd, hd), hd)].astype(F32) for i in range(2)]
    piece[:, :hd] = jnp.concatenate(sides, axis=0).astype(BF16)

    @pl.when(c == lax.div(z, half))
    def _():
        wall[y, x, z] = piece[...]

    pl.semaphore_wait(barrier, len(partners))

    shard = wall.at[y, x, z]
    collector = y * CORES + lax.div(z, half)

    def shard_copy(i):
        device = (x * NZ + lax.rem(z + 1 + i + c * half, NZ), collector)
        return rcopy(piece, shard, zs.at[i], zr.at[lax.rem(z, half)], device)

    for i in range(half - 1):
        shard_copy(i).start()

    @pl.when(c == 0)
    def _():
        shard_copy(half - 1).start()

    own_row = own_ref[...]
    expand = one_hot(lax.div(iota((ndp, rows), 1), cap) == iota((ndp, rows), 0))
    own_rep = dot(jnp.broadcast_to(own_row.astype(F32).astype(BF16), (8, ndp)), expand)[0:1, :]
    to_owner = one_hot(iota((ndp, rows), 0).astype(F32) == own_rep)
    lane = iota((128, rows), 0)
    inside = (lax.div(lane, 2) == lax.rem(iota((128, rows), 1), cap)) & (lane < 2 * cap)
    both = jnp.where(lax.rem(lane, 2) == 0, cand_ref[0:1, :], cand_ref[1:2, :])
    high, low = small_parts(jnp.where(inside, both, 0))
    requests = dot_nt(to_owner, high) * 16.0 + dot_nt(to_owner, low)
    for p in range(ndp):
        req_send[p // NZ, p % NZ] = requests[p : p + 1, :]
    request_x = []
    for d in range(1, nx):
        block = req_send.at[lax.rem(x + d, nx)]
        request_x.append(rcopy(block, req_mid.at[x], qxs.at[d - 1], qxr.at[d - 1], beside_x(d)))
    for copy in request_x:
        copy.start()
    req_mid[x] = req_send[x]

    tokens = tok_ref[...].astype(F32)
    normed_raw, factor_in = normalize(tokens)
    xn[y] = (normed_raw * gin_ref[...]).astype(BF16)

    def y_copies(part, send, recv):
        return [
            rcopy(part(y, 0), part(y, 0), send.at[0], recv.at[0], up),
            rcopy(part(y, 1), part(y, 1), send.at[1], recv.at[1], down),
            rcopy(part(y, 1), part(y, 1), send.at[2], recv.at[2], up),
            rcopy(part(y, 0), part(y, 0), send.at[3], recv.at[3], down),
            rcopy(part(ym, 0), part(ym, 0), send.at[4], recv.at[4], up),
            rcopy(part(yp, 1), part(yp, 1), send.at[5], recv.at[5], down),
        ]

    def y_start(copies):
        for copy in copies[:4]:
            copy.start()

    def y_forward(copies):
        copies[0].wait_recv()
        copies[4].start()
        copies[1].wait_recv()
        copies[5].start()

    tok_copies = y_copies(lambda at, h: xn.at[at, pl.ds(h * (rows // 2), rows // 2), :], ts, tr)

    y_start(tok_copies)

    for copy in request_x:
        copy.wait_recv()
    request_z = []
    for d in range(1, NZ):
        block = req_mid.at[:, lax.rem(z + d, NZ)]
        request_z.append(rcopy(block, req_recv.at[:, z], qzs.at[d - 1], qzr.at[d - 1], beside_z(d)))
    for copy in request_z:
        copy.start()
    req_recv[:, z] = req_mid[:, z]

    def collected(d):
        return wall.at[y, lax.rem(x - d + nx, nx), pl.ds(c * half, half)]

    for j in range(half):

        @pl.when(z != c * half + j)
        def _():
            rcopy(shard, shard, zs.at[0], zr.at[j], sibling).wait_recv()

    x_copies = []
    for d in range(1, nx):
        x_copies.append(rcopy(collected(0), collected(0), xs.at[d - 1], xr.at[d - 1], beside_x(d)))
    relays = [rcopy(collected(d), collected(d), rs.at[d], rr.at[d], sibling) for d in range(nx)]
    for copy in x_copies:
        copy.start()
    relays[0].start()

    for copy in request_z:
        copy.wait_recv()
    for p in range(ndp):
        rq[p : p + 1, :] = req_recv[p // NZ, p % NZ]
    table_copy.wait()
    high, low = small_parts(rq[...])
    chunk = NZ * TILE
    row = iota((chunk, 128), 0)
    place = 2 * lax.rem(row, cap)
    lanes = iota((chunk, 128), 1)
    group = lax.div(lax.rem(iota((chunk, quarter), 0), TILE), cap)

    def differences(side):
        spread = one_hot(lax.div(iota((chunk, ndp), 0), TILE) + side * NZ == iota((chunk, ndp), 1))
        wanted = dot(spread, high) * 16.0 + dot(spread, low)
        first_item = jnp.sum(jnp.where(lanes == place, wanted, 0.0), axis=1, keepdims=True)
        second_item = jnp.sum(jnp.where(lanes == place + 1, wanted, 0.0), axis=1, keepdims=True)
        items = iota((chunk, table.shape[0]), 1).astype(F32)
        signs = jnp.where(items == first_item, 1.0, 0.0) - jnp.where(items == second_item, 1.0, 0.0)
        signs = signs.astype(BF16)
        total = jnp.zeros((chunk, quarter), F32)
        for g in range(4):
            term = dot(signs, table[:, g * quarter : (g + 1) * quarter])
            total = jnp.where(group == g, term, total)
        return total.astype(BF16).reshape(NZ, TILE, quarter)

    hops = [0, 1] + [nx - 1] * (nx > 2) + list(range(2, nx - 1))
    rounds = [(0, 1), (1, min(3, nx))] + [(3, nx)] * (nx > 3)
    diff_z = []

    def along_z(i):
        low, high = rounds[i]
        slots = pl.ds(low, high - low)
        copies = []
        for d in range(1, NZ):
            block = dmid.at[slots, lax.rem(z + d, NZ)]
            copies.append(rcopy(block, drecv.at[slots, z], dzs.at[i, d - 1], dzr.at[i, d - 1], beside_z(d)))
        for copy in copies:
            copy.start()
        drecv[slots, z] = dmid[slots, z]
        diff_z.extend(copies)

    near = pl.ds(0, 2 * hd)
    far = pl.ds(2 * hd, 3 * hd)

    def weight_part(columns):
        def part(at, h):
            return wall.at[at, pl.ds(h * (nx // 2), nx // 2), pl.ds(c * half, half), :, columns]

        return part

    def weight_relay(at, index, columns, send, recv):
        block = wall.at[at, :, pl.ds(c * half, half), :, columns]
        return rcopy(block, block, send.at[index], recv.at[index], sibling)

    near_copies = y_copies(weight_part(near), ws, wr)
    near_relays = [weight_relay(at, i, near, wrs, wrr) for i, at in enumerate((ym, yp, yo))]
    far_copies = y_copies(weight_part(far), vs, vr)
    far_relays = [weight_relay(at, i, far, vrs, vrr) for i, at in enumerate((ym, yp, yo))]

    def relay_start(copies, relayed):
        copies[2].wait_recv()
        relayed[0].start()
        copies[3].wait_recv()
        relayed[1].start()
        copies[4].wait_recv()
        copies[5].wait_recv()
        relayed[2].start()

    dmid[0] = differences(x)
    along_z(0)
    diff_x = []
    for slot in range(1, nx):
        d = hops[slot]
        side = lax.rem(x + d, nx)
        dsend[side] = differences(side)
        copy = rcopy(dsend.at[side], dmid.at[slot], dxs.at[slot - 1], dxr.at[slot - 1], beside_x(d))
        copy.start()
        diff_x.append(copy)
        if slot == 1:
            y_forward(tok_copies)
            for d in hops[1:]:
                x_copies[d - 1].wait_recv()
                relays[d].start()
            y_start(near_copies)

    for d in range(1, nx):
        if d < len(rounds):
            for slot in range(*rounds[d]):
                diff_x[slot - 1].wait_recv()
            along_z(d)
    for copy in relays:
        copy.wait_recv()

    length = jnp.sum(jnp.where(iota((1, ndp), 1) == dp, len_ref[...], 0), axis=1, keepdims=True)
    live_total = jnp.sum(len_ref[...], axis=1, keepdims=True).astype(F32)
    index = iota((rows, 1), 0)
    w_head = wall[y, :, :, :, 2 * hd : 5 * hd].reshape(width, 3 * hd)
    kv_copies = []

    def alive_of(block):
        return jnp.where(index + block * rows < length, 1.0, 0.0)

    def block_span(block):
        return pl.ds(pl.multiple_of(block * rows, rows), rows)

    def project(at, order):
        projected = dot(xn[at], w_head)
        proj[at] = projected
        activated = projected * jax.nn.sigmoid(projected)
        value, key = activated[:, :hd], activated[:, hd : 2 * hd] * alive_of(CORES * at + c)
        query = activated[:, 2 * hd :]
        kv[CORES * at + c, :, :hd] = value.astype(BF16)
        kv[CORES * at + c, :, hd:] = key.astype(BF16)
        copy = rcopy(kv.at[CORES * at + c], kv.at[CORES * at + c], ks.at[order], kr.at[order], sibling)
        copy.start()
        kv_copies.append(copy)
        span = block_span(CORES * at + c)
        vt[:, span] = value.T.astype(BF16)
        kt[:, span] = key.T.astype(BF16)
        qs[block_span(at), :] = query.astype(BF16)
        qt[:, block_span(at)] = query.T.astype(BF16)

    project(y, 0)
    tok_copies[2].wait_recv()
    project(ym, 1)
    tok_copies[3].wait_recv()
    project(yp, 2)
    tok_copies[4].wait_recv()
    tok_copies[5].wait_recv()
    project(yo, 3)
    y_forward(near_copies)
    y_start(far_copies)
    for copy in kv_copies:
        copy.wait_recv()
    for u in range(HEADS):
        block = CORES * u + other
        both = kv[block].astype(F32)
        vt[:, block_span(block)] = both[:, :hd].T.astype(BF16)
        kt[:, block_span(block)] = both[:, hd:].T.astype(BF16)

    def send_when(t, src, dst, send, recv):
        @pl.when(y != t)
        def _():
            rcopy(src, dst, send.at[t], recv.at[y], (dp, t * CORES + c)).start()

        @pl.when(y == t)
        def _():
            dst[...] = src[...]

    def wait_when(t, ref, send, recv):
        @pl.when(y != t)
        def _():
            rcopy(ref, ref, send.at[t], recv.at[t], (dp, t * CORES + c)).wait_recv()

    def done_when(t, ref, send, recv):
        @pl.when(y != t)
        def _():
            rcopy(ref, ref, send.at[t], recv.at[t], (dp, t * CORES + c)).wait_send()

    causal = jnp.where(iota((rows, rows), 0) <= iota((rows, rows), 1), 1.0, 0.0)
    before = c.astype(F32)

    def weigh(block, low, high, mask):
        scores = dot(kv[block, :, hd:], qt[:, low:high]) * scale
        sigma = jax.nn.sigmoid(scores)
        weights = scores * sigma
        change = (sigma + weights * (1.0 - sigma)) * (scale / history)
        weights = weights * (1.0 / history)
        if mask is not None:
            weights, change = weights * mask, change * mask
        wst[block_span(block), low:high] = weights.astype(BF16)
        slope[block_span(block), low:high] = change

    queries = HEADS * rows
    for u in range(HEADS):
        low, high = u * rows, (u + 1) * rows
        for parity in range(2):
            block = CORES * u + (c if parity == 0 else other)
            weigh(block, low, high, causal if parity == 0 else before)
            if high < queries:
                weigh(block, high, queries, None)
        keys = CORES * (u + 1) * rows
        att_send[u] = dot(vt[:, :keys], wst[:keys, low:high]).T.astype(BF16)
        send_when(u, att_send.at[u], att_recv.at[y], as_, ar)

    relay_start(near_copies, near_relays)
    for copy in near_relays:
        copy.wait_recv()
    for t in range(HEADS):
        gproj[:, t * hd : (t + 1) * hd] = dot(xn[y], wall[t, :, :, :, hd : 2 * hd].reshape(width, hd))
    lines = TILE // 2
    line, spot = iota((hw, width), 0), iota((hw, width), 1)
    origin = lax.div(line, lines) * TILE + lax.rem(line, lines)
    for side in range(2):
        select = one_hot(spot == origin + side * lines)
        for t in range(HEADS):
            begin = side * (width // 2) + t * hd
            wout[:, begin : begin + hd] = dot(select, wall[t, :, :, :, :hd].reshape(width, hd)).astype(BF16)

    y_forward(far_copies)
    own_col = jnp.sum(
        jnp.where(iota((rows, ndp), 1) == lax.div(iota((rows, ndp), 0), cap), own_row, 0), axis=1, keepdims=True
    )
    away = lax.rem(x - lax.div(own_col, NZ) + nx, nx)
    slot_of = sum(jnp.where(away == hop, slot, 0) for slot, hop in enumerate(hops))
    source = (slot_of * NZ + lax.rem(own_col, NZ)) * TILE + lax.rem(index, cap)
    for g in range(4):
        picks[g] = one_hot(iota((rows, ndp * TILE), 1) == source + g * cap)
    for copy in diff_z:
        copy.wait_recv()
    received = drecv[...].reshape(ndp * TILE, quarter)
    for g in range(4):
        idiff[:, g * quarter : (g + 1) * quarter] = dot(picks[g], received).astype(BF16)

    eye = iota((rows, rows), 0) == iota((rows, rows), 1)
    teacher = jnp.sum(jnp.where(eye, teach_ref[...], 0.0), axis=1, keepdims=True)
    alive = alive_of(sq)
    projected = gproj[...]
    gate = (projected * jax.nn.sigmoid(projected)).astype(BF16).astype(F32)
    gain_mid = gmid_ref[...]
    for t in range(HEADS):
        wait_when(t, att_recv.at[t], as_, ar)
    attended = jnp.concatenate([att_recv[t].astype(F32) for t in range(HEADS)], axis=1)
    normed_mid, factor_mid = normalize(attended)
    gated = (normed_mid * gain_mid * gate).astype(BF16)
    layer_out = (tok_ref[...].astype(F32) + dot(gated, wout[...])).astype(BF16).astype(F32)
    difference = idiff[...].astype(F32)
    errors = (jnp.sum(layer_out * difference, axis=1, keepdims=True) - teacher) * alive
    grad_out = (2.0 / live_total * errors * difference).astype(BF16)
    gout[...] = grad_out
    grad_gated = dot_nt(grad_out, wout[...])
    grad_normed = grad_gated * gain_mid * gate
    grad_attended = normalize_back(grad_normed, normed_mid, factor_mid).astype(BF16)
    for t in range(HEADS):
        da_send[t] = grad_attended[:, t * hd : (t + 1) * hd]
        send_when(t, da_send.at[t], da_recv.at[y], gs, gr)
    gpg[...] = (grad_gated * normed_mid * gain_mid * silu_slope(projected)).astype(BF16)

    def loss_send(buffer, place, send, recv, devices):
        copies = [
            rcopy(buffer.at[place], buffer.at[place], send.at[i], recv.at[i], device)
            for i, device in enumerate(devices)
        ]
        for copy in copies:
            copy.start()
        return copies

    lby[y] = jnp.broadcast_to(jnp.sum(errors * errors, axis=0, keepdims=True), (8, 128))
    loss_y = loss_send(lby, y, lys, lyr, [beside_y(d) for d in range(1, HEADS)])
    for t in range(HEADS):
        wait_when(t, da_recv.at[t], gs, gr)
    for t in range(HEADS):
        dat[:, t * rows : (t + 1) * rows] = da_recv[t].astype(F32).T.astype(BF16)

    def backward(u, parity):
        block = CORES * u + (c if parity == 0 else other)
        span, low = block_span(block), u * rows
        grad_weights = dot(kv[block, :, :hd], dat[:, low:])
        grad_scores = (grad_weights * slope[span, low:]).astype(BF16)
        dst[span, low:] = grad_scores
        grad_attended = da_recv[u:].reshape((HEADS - u) * rows, hd)
        grad_value = dot(wst[span, low:], grad_attended)
        grad_key = dot(grad_scores, qs[low:, :])
        return grad_value, grad_key

    part_copies = []
    for u in range(HEADS):
        grad_value, grad_key = backward(u, 1)
        dvk_send[u, :, :hd] = grad_value
        dvk_send[u, :, hd:] = grad_key
        copy = rcopy(dvk_send.at[u], dvk_recv.at[u], ps.at[u], pr.at[u], sibling)
        copy.start()
        part_copies.append(copy)
    relay_start(far_copies, far_relays)
    for copy in loss_y:
        copy.wait_recv()
    lbc[c] = jnp.sum(lby[...], axis=0)
    loss_c = loss_send(lbc, c, lcs, lcr, [sibling])
    for u in range(HEADS):
        grad_value, grad_key = backward(u, 0)
        part_copies[u].wait_recv()
        keep = alive_of(CORES * u + c)
        grad_value = (grad_value + dvk_recv[u, :, :hd]) * keep
        grad_key = (grad_key + dvk_recv[u, :, hd:]) * keep
        keys = CORES * (u + 1) * rows
        grad_query = dot(kt[:, :keys], dst[:keys, u * rows : (u + 1) * rows]).T
        gps[u, :, :hd] = (grad_value * silu_slope(proj[u, :, :hd])).astype(BF16)
        gps[u, :, hd : 2 * hd] = (grad_key * silu_slope(proj[u, :, hd : 2 * hd])).astype(BF16)
        gps[u, :, 2 * hd :] = (grad_query * silu_slope(proj[u, :, 2 * hd :])).astype(BF16)
        send_when(u, gps.at[u], gpr.at[y], fs, fr)
        if u == 0:
            loss_c[0].wait_recv()
            lbx[x] = jnp.sum(lbc[...], axis=0)
            loss_x = loss_send(lbx, x, lxs, lxr, [beside_x(d) for d in range(1, nx)])

    for copy in loss_x:
        copy.wait_recv()
    lbz[z] = jnp.sum(lbx[...], axis=0)
    loss_z = loss_send(lbz, z, lzs, lzr, [beside_z(d) for d in range(1, NZ)])

    for copy in far_relays:
        copy.wait_recv()
    grad_in = jnp.zeros((rows, width), F32)
    for t in range(HEADS):
        grad_in = grad_in + dot_nt(
            gpg[:, t * hd : (t + 1) * hd], wall[t, :, :, :, hd : 2 * hd].reshape(width, hd)
        )
    for t in range(HEADS):
        wait_when(t, gpr.at[t], fs, fr)
        grad_in = grad_in + dot_nt(gpr[t], wall[t, :, :, :, 2 * hd :].reshape(width, 3 * hd))
    normed_raw, factor_in = normalize(tok_ref[...].astype(F32))
    grad_norm = normalize_back(grad_in * gin_ref[...], normed_raw, factor_in)
    out_ref[...] = (gout[...].astype(F32) + grad_norm).astype(BF16)

    for copy in loss_z:
        copy.wait_recv()
    loss_ref[...] = jnp.sum(lbz[...], axis=0)[0:1, 0:1] / live_total

    for i in range(half - 1):
        shard_copy(i).wait_send()

    @pl.when(c == 0)
    def _():
        shard_copy(half - 1).wait_send()

    for copy in x_copies + relays + tok_copies + near_copies + near_relays + far_copies + far_relays:
        copy.wait_send()
    for copy in kv_copies + part_copies + loss_y + loss_c + loss_x + loss_z:
        copy.wait_send()
    for copy in request_x + request_z + diff_x + diff_z:
        copy.wait_send()
    for t in range(HEADS):
        done_when(t, att_send.at[t], as_, ar)
        done_when(t, da_send.at[t], gs, gr)
        done_when(t, gps.at[t], fs, fr)


def on_device(
    tokens, teacher, cand_items, owner_map, lengths, w_proj, w_out, gain_in, gain_mid, item_table
):
    rows, width = tokens.shape
    ndp = lax.axis_size("dp")
    nx = ndp // NZ
    hw = gain_mid.shape[0]
    hd = hw // HEADS
    blocks = HEADS * CORES
    half = NZ // 2
    quarter = width // 4

    vmem = pltpu.VMEM
    dma = pltpu.SemaphoreType.DMA
    scratch = [
        vmem((rows, width), BF16),
        vmem((1, rows), F32),
        vmem((2, rows), jnp.int32),
        vmem((1, ndp), jnp.int32),
        vmem((1, ndp), jnp.int32),
        vmem(w_out.shape, BF16),
        vmem((1, width), F32),
        vmem((1, hw), F32),
        vmem((HEADS, nx, NZ, TILE, 5 * hd), BF16),
        vmem((TILE, 5 * hd), BF16),
        vmem((HEADS, rows, width), BF16),
        vmem(item_table.shape, BF16),
        vmem((nx, NZ, 1, 128), F32),
        vmem((nx, NZ, 1, 128), F32),
        vmem((nx, NZ, 1, 128), F32),
        vmem((ndp, 128), F32),
        vmem((nx, NZ, TILE, quarter), BF16),
        vmem((nx, NZ, TILE, quarter), BF16),
        vmem((nx, NZ, TILE, quarter), BF16),
        vmem((4, rows, ndp * TILE), BF16),
        vmem((rows, width), BF16),
        vmem((HEADS, rows, 3 * hd), F32),
        vmem((blocks, rows, 2 * hd), BF16),
        vmem((hd, blocks * rows), BF16),
        vmem((hd, blocks * rows), BF16),
        vmem((HEADS * rows, hd), BF16),
        vmem((hd, HEADS * rows), BF16),
        vmem((blocks * rows, HEADS * rows), BF16),
        vmem((blocks * rows, HEADS * rows), F32),
        vmem((HEADS, rows, hd), BF16),
        vmem((HEADS, rows, hd), BF16),
        vmem((rows, hw), F32),
        vmem((hw, width), BF16),
        vmem((rows, width), BF16),
        vmem((rows, hw), BF16),
        vmem((HEADS, rows, hd), BF16),
        vmem((HEADS, rows, hd), BF16),
        vmem((hd, HEADS * rows), BF16),
        vmem((HEADS, rows, 2 * hd), F32),
        vmem((HEADS, rows, 2 * hd), F32),
        vmem((blocks * rows, HEADS * rows), BF16),
        vmem((HEADS, rows, 3 * hd), BF16),
        vmem((HEADS, rows, 3 * hd), BF16),
        vmem((HEADS, 8, 128), F32),
        vmem((CORES, 8, 128), F32),
        vmem((nx, 8, 128), F32),
        vmem((NZ, 8, 128), F32),
        dma((5,)),
        dma((8,)),
        dma((nx,)), dma((nx,)),
        dma((half,)), dma((half,)),
        dma((nx,)), dma((nx,)),
        dma((6,)), dma((6,)),
        dma((nx,)), dma((nx,)), dma((NZ,)), dma((NZ,)),
        dma((nx,)), dma((nx,)), dma((3, NZ)), dma((3, NZ)),
        dma((6,)), dma((6,)), dma((3,)), dma((3,)),
        dma((6,)), dma((6,)), dma((3,)), dma((3,)),
        dma((HEADS,)), dma((HEADS,)),
        dma((HEADS,)), dma((HEADS,)),
        dma((HEADS,)), dma((HEADS,)),
        dma((HEADS,)), dma((HEADS,)),
        dma((HEADS,)), dma((HEADS,)),
        dma((HEADS,)), dma((HEADS,)), dma((1,)), dma((1,)), dma((nx,)), dma((nx,)), dma((NZ,)), dma((NZ,)),
    ]
    whole = pl.BlockSpec(memory_space=pltpu.VMEM)
    anywhere = pl.BlockSpec(memory_space=pl.ANY)
    grads, loss = pl.pallas_call(
        kernel,
        out_shape=(jax.ShapeDtypeStruct(tokens.shape, BF16), jax.ShapeDtypeStruct((1, 1), F32)),
        in_specs=[anywhere] * 10,
        out_specs=(whole, whole),
        scratch_shapes=scratch,
        compiler_params=pltpu.CompilerParams(
            collective_id=0, has_side_effects=True, vmem_limit_bytes=56 * 1024 * 1024
        ),
    )(
        tokens,
        teacher.reshape(1, rows),
        cand_items.T,
        owner_map.reshape(1, ndp),
        lengths.reshape(1, ndp),
        w_proj,
        w_out,
        gain_in.reshape(1, width),
        gain_mid.reshape(1, hw),
        item_table,
    )
    return (grads, loss[0, 0])


def solution(mesh):
    in_specs = (
        P(("dp", "seq"), None),
        P(("dp", "seq")),
        P(("dp", "seq"), None),
        P(("dp", "seq")),
        P(),
        P("dp", None),
        P("dp", None),
        P(),
        P(),
        P("dp", None),
    )
    out_specs = (P(("dp", "seq"), None), P())
    return jax.shard_map(
        on_device, mesh=mesh, in_specs=in_specs, out_specs=out_specs, check_vma=False
    )
```
